32 devices in a mesh: dp: 8 (over y, x, core), head: 4 (over z).
Axes of the slice: x: 2, y: 2, z: 4, core: 2. Of those that a mesh axis runs over, the one named last changes fastest.
Arguments:
- hidden_in: bfloat16 [2, 8192, 768], P(None, ('dp', 'head')), may hold values from -6 to 6
- teacher_in: bfloat16 [2, 8192, 768], P(None, ('dp', 'head')), may hold values from -6 to 6
- out_grad: bfloat16 [2, 8192, 768], P(None, ('dp', 'head')), may hold values from -6 to 6
- segment_ids: int32 [2, 16, 512], P(None, 'dp'), may hold values from 0 to 3, never falling along the last dimension, each value on 1 to 256 neighbouring positions
- qkv_latent: bfloat16 [3, 768, 768], P(None, None, 'head'), may hold values from -0.3125 to 0.3125
- out_latent: bfloat16 [768, 768], P('head'), may hold values from -0.875 to 0.875
- ffn_in_latent: bfloat16 [768, 3072], P(None, 'head'), may hold values from -0.21875 to 0.21875
- ffn_out_latent: bfloat16 [3072, 768], P('head'), may hold values from -0.109375 to 0.109375
- norm_gain: float32 [2, 768], replicated, may hold values from 0.5 to 1.5
- norm_bias: float32 [2, 768], replicated, may hold values from -2 to 2
- clips: float32 [4], replicated, may hold values from 0.75 to 2.5
- teacher_qkv: bfloat16 [3, 768, 768], P(None, None, 'head'), may hold values from -0.3125 to 0.3125
- teacher_out: bfloat16 [768, 768], P('head'), may hold values from -0.875 to 0.875
- teacher_ffn_in: bfloat16 [768, 3072], P(None, 'head'), may hold values from -0.21875 to 0.21875
- teacher_ffn_out: bfloat16 [3072, 768], P('head'), may hold values from -0.109375 to 0.109375
- teacher_gain: float32 [2, 768], replicated, may hold values from 0.5 to 1.5
- teacher_bias: float32 [2, 768], replicated, may hold values from -2 to 2
Outputs:
- hidden_out: bfloat16 [2, 8192, 768], P(None, ('dp', 'head'))
- hidden_in_grad: float32 [2, 8192, 768], P(None, ('dp', 'head'))
- qkv_grad: float32 [3, 768, 768], P(None, None, 'head')
- out_latent_grad: float32 [768, 768], P('head')
- ffn_in_grad: float32 [768, 3072], P(None, 'head')
- ffn_out_grad: float32 [3072, 768], P('head')
- gain_grad: float32 [2, 768], replicated
- bias_grad: float32 [2, 768], replicated
- clip_grad: float32 [4], replicated
The draws below stay inside these ranges and needn't reach their ends.
Inputs may be any that keep to these rules, and one draw needn't show every extreme that they name: `segment_ids`: within each packed row of 512 tokens the documents are numbered in order from 0, never falling; attention stays within a document.
All inputs are finite; a program needn't handle non-finite values.
Results may differ from the reference program's by a relative error of at most 0.014.
Values may be sent and summed in bfloat16 or wider, within the bound.
No kernel may reach another device: no remote copies, remote signals or barrier semaphores. Data moves between devices by JAX's collectives and lax.ppermute only.
A program may use at most 128 MiB of HBM per device.

```python
import math
import jax
import jax.numpy as jnp
import numpy as np
from jax import lax

D = 768
H = 12
HD = 64
FF = 3072
SEQ = 512
ROWS_MB = 2
MICRO = 2
TOK_MB = 8192
N_DP = 8


def shard_levels(key, shape, shards, smallest, high):
    factor_of = 1.0
    for position, parts in shards:
        draws = jax.random.uniform(jax.random.fold_in(jax.random.fold_in(key, 6), position), (parts,), jnp.float32, smallest / len(shards), high / len(shards))
        factor_of = factor_of * jnp.repeat(jnp.exp(draws), shape[position] // parts).reshape((-1,) + (1,) * (len(shape) - 1 - position))
    return factor_of


def length_profile(number_of, total, most, lean):
    weights = [(1 << 20) // math.isqrt(rank ** lean) + 1 for rank in range(2, number_of + 1)]
    rest, holding = total - most - (number_of - 1), [1] * (number_of - 1)
    while rest > 0:
        candidates = [i for i in range(number_of - 1) if holding[i] < most]
        whole, budget = sum([weights[i] for i in candidates]), rest
        for i in candidates:
            addition = min(most - holding[i], max(1, budget * weights[i] // whole), rest)
            holding[i] = holding[i] + addition
            rest = rest - addition
    return np.array([most] + holding)


def uneven(rng, amount, total, bound, slope):
    if amount == 2:
        one = jax.random.randint(rng, (), max(1, total - bound), min(bound, total - 1) + 1)
        return jnp.stack([one, total - one])
    tallies = jnp.asarray(length_profile(amount, total, bound, slope), jnp.int32)
    twos = (amount - 1) // 2
    source_of, receiver = tallies[1:1 + 2 * twos:2], tallies[2:2 + 2 * twos:2]
    margin = jnp.minimum(source_of - 1, bound - receiver)
    moved = jax.random.randint(jax.random.fold_in(rng, 1), (twos,), 0, 1 << 20) % (margin + 1)
    tallies = tallies.at[1:1 + 2 * twos:2].set(source_of - moved).at[2:2 + 2 * twos:2].set(receiver + moved)
    return tallies[jax.random.permutation(jax.random.fold_in(rng, 2), amount)]


def scatter_about(key, dims, spread, most, shards=(), dtype=jnp.bfloat16):
    drawn = jax.random.normal(key, dims, jnp.float32) * spread
    if len(shards) > 0:
        drawn = shard_levels(key, dims, shards, -0.22, 0.18) * drawn
    return jnp.clip(drawn, min=-most, max=most).astype(dtype)


def setup_inputs(seed: int = 0) -> dict:
    streams_of = jax.random.split(jax.random.key(seed), 18)
    return {
        "hidden_in": scatter_about(streams_of[0], (MICRO, TOK_MB, D), 1.0, 6.0, ((1, 32),)),
        "teacher_in": scatter_about(streams_of[1], (MICRO, TOK_MB, D), 1.0, 6.0, ((1, 32),)),
        "out_grad": scatter_about(streams_of[2], (MICRO, TOK_MB, D), 1.0, 6.0, ((1, 32),)),
        "segment_ids": jax.vmap(lambda own: jnp.searchsorted(jnp.cumsum(uneven(own, 4, SEQ, SEQ // 2, 1)), jnp.arange(SEQ), side="right"))(jax.random.split(streams_of[3], MICRO * (N_DP * ROWS_MB))).reshape((MICRO, N_DP * ROWS_MB, SEQ)).astype(jnp.int32),
        "qkv_latent": scatter_about(streams_of[4], (3, D, D), (D // 2) ** -0.5, 0.3125, ((2, 4),)),
        "out_latent": scatter_about(streams_of[5], (D, D), (D // 16) ** -0.5, 0.875, ((0, 4),)),
        "ffn_in_latent": scatter_about(streams_of[6], (D, FF), D ** -0.5, 0.21875, ((1, 4),)),
        "ffn_out_latent": scatter_about(streams_of[7], (FF, D), FF ** -0.5, 0.109375, ((0, 4),)),
        "norm_gain": jnp.clip(1.0 + 0.1 * jax.random.normal(streams_of[8], (2, D), jnp.float32), 0.5, 1.5),
        "norm_bias": scatter_about(streams_of[9], (2, D), 0.3, 2.0, (), jnp.float32),
        "clips": jnp.clip(jax.random.uniform(streams_of[10], (4,), jnp.float32, 0.75, 2.5), 0.75, 2.5),
        "teacher_qkv": scatter_about(streams_of[11], (3, D, D), (D // 2) ** -0.5, 0.3125, ((2, 4),)),
        "teacher_out": scatter_about(streams_of[12], (D, D), (D // 16) ** -0.5, 0.875, ((0, 4),)),
        "teacher_ffn_in": scatter_about(streams_of[13], (D, FF), D ** -0.5, 0.21875, ((1, 4),)),
        "teacher_ffn_out": scatter_about(streams_of[14], (FF, D), FF ** -0.5, 0.109375, ((0, 4),)),
        "teacher_gain": jnp.clip(1.0 + 0.1 * jax.random.normal(streams_of[15], (2, D), jnp.float32), 0.5, 1.5),
        "teacher_bias": scatter_about(streams_of[16], (2, D), 0.3, 2.0, (), jnp.float32),
    }


@jax.custom_vjp
def low(v):
    return lax.optimization_barrier(v.astype(jnp.bfloat16)).astype(jnp.float32)

@jax.custom_vjp
def low_back(v):
    return v

def low_keep(v):
    return (low(v), None)

def low_pass(kept, grad):
    return (grad,)

def back_keep(v):
    return (v, None)

def back_low(kept, grad):
    return (low(grad),)
low.defvjp(low_keep, low_pass)
low_back.defvjp(back_keep, back_low)

def project(left_op, right_op):
    return jnp.dot(left_op, right_op, precision=lax.Precision.HIGHEST, preferred_element_type=jnp.float32)

def soft_clip(values, clip_level):
    return clip_level * jnp.tanh(values / clip_level)

def binarize(latent):
    level = jnp.sqrt(jnp.mean(latent * latent) + 1e-06)
    return level * jnp.tanh(2.0 * latent / level)

def layer_norm(values, gain_vec, shift_vec):
    centred = values - lax.optimization_barrier(jnp.mean(values, axis=-1, keepdims=True))
    variance = lax.optimization_barrier(jnp.mean(centred * centred, axis=-1, keepdims=True))
    return centred * lax.rsqrt(variance + 1e-06) * gain_vec + shift_vec

def masked_scores(queries, key_rows, segment_row):
    scores = jnp.einsum('qhd,khd->hqk', queries, key_rows, precision=lax.Precision.HIGHEST) * 0.125
    same_segment = segment_row[:, None] == segment_row[None, :]
    return (jnp.where(same_segment[None], scores, -1000000000.0), same_segment)

def teacher_rows(operands):
    queries, key_rows, value_rows, segment_row = operands
    scores, same_segment = masked_scores(queries, key_rows, segment_row)
    soft_weights = jax.nn.softmax(scores, axis=-1)
    return low(jnp.einsum('hqk,khd->qhd', low(soft_weights), value_rows, precision=lax.Precision.HIGHEST))

def student_rows(operands):
    queries, key_rows, value_rows, t_queries, t_keys, segment_row = operands
    scores, same_segment = masked_scores(queries, key_rows, segment_row)
    scores = low_back(scores)
    soft_weights = jax.nn.softmax(scores, axis=-1)
    context = jnp.einsum('hqk,khd->qhd', low(soft_weights), value_rows, precision=lax.Precision.HIGHEST)
    t_scores, unused_mask = masked_scores(t_queries, t_keys, segment_row)
    gap_vals = jnp.where(same_segment[None], scores - t_scores, 0.0)
    return (context, jnp.sum(gap_vals * gap_vals) * (0.5 / SEQ))

def reference(hidden_in, teacher_in, out_grad, segment_ids, qkv_latent, out_latent, ffn_in_latent, ffn_out_latent, norm_gain, norm_bias, clips, teacher_qkv, teacher_out, teacher_ffn_in, teacher_ffn_out, teacher_gain, teacher_bias):
    count = MICRO * TOK_MB
    row_count = count // SEQ
    segment_rows = segment_ids.reshape(row_count, SEQ)
    t_input = teacher_in.astype(jnp.float32).reshape(count, D)
    t_qkv_w = teacher_qkv.astype(jnp.float32)
    t_out_w = teacher_out.astype(jnp.float32)
    t_ffn_in_w = teacher_ffn_in.astype(jnp.float32)
    t_ffn_out_w = teacher_ffn_out.astype(jnp.float32)
    cotangent = out_grad.astype(jnp.float32).reshape(count, D)

    def objective(qkv_w, out_w, ffn_in_w, ffn_out_w, gain_vec, shift_vec, clip_vec, inputs):
        t_qkv = low(jnp.einsum('nd,jde->jne', t_input, t_qkv_w, precision=lax.Precision.HIGHEST))
        t_qkv = t_qkv.reshape(3, row_count, SEQ, H, HD)
        t_context = lax.map(teacher_rows, (t_qkv[0], t_qkv[1], t_qkv[2], segment_rows)).reshape(count, D)
        t_first = layer_norm(t_input + project(t_context, t_out_w), teacher_gain[0], teacher_bias[0])
        t_hidden = low(jax.nn.gelu(project(low(t_first), t_ffn_in_w), approximate=False))
        t_result = layer_norm(t_first + project(t_hidden, t_ffn_out_w), teacher_gain[1], teacher_bias[1])
        qkv_bin = low(jax.vmap(binarize)(qkv_w))
        out_bin = low(binarize(out_w))
        ffn_in_bin = low(binarize(ffn_in_w))
        ffn_out_bin = low(binarize(ffn_out_w))
        inputs_quant = low(soft_clip(inputs, clip_vec[0]))
        qkv_vals = low_back(low(jnp.einsum('nd,jde->jne', inputs_quant, qkv_bin, precision=lax.Precision.HIGHEST)))
        qkv_vals = qkv_vals.reshape(3, row_count, SEQ, H, HD)
        context, att_losses = lax.map(jax.checkpoint(student_rows), (qkv_vals[0], qkv_vals[1], qkv_vals[2], t_qkv[0], t_qkv[1], segment_rows))
        context = low_back(context.reshape(count, D))
        ctx_quant = low(soft_clip(context, clip_vec[1]))
        first_norm = layer_norm(inputs + low_back(project(ctx_quant, out_bin)), gain_vec[0], shift_vec[0])
        first_quant = low(soft_clip(first_norm, clip_vec[2]))
        hidden_pre = low_back(project(first_quant, ffn_in_bin))
        hidden_quant = low(soft_clip(jax.nn.gelu(hidden_pre, approximate=False), clip_vec[3]))
        result = layer_norm(first_norm + low_back(project(hidden_quant, ffn_out_bin)), gain_vec[1], shift_vec[1])
        gap_vals = result - t_result
        total = jnp.sum(cotangent * result) + 0.5 * jnp.sum(gap_vals * gap_vals) + jnp.sum(att_losses)
        return (total, result)
    inputs = hidden_in.astype(jnp.float32).reshape(count, D)
    total, backward, result = jax.vjp(objective, qkv_latent.astype(jnp.float32), out_latent.astype(jnp.float32), ffn_in_latent.astype(jnp.float32), ffn_out_latent.astype(jnp.float32), norm_gain, norm_bias, clips, inputs, has_aux=True)
    grads = backward(jnp.ones_like(total))
    return (result.astype(jnp.bfloat16).reshape(MICRO, TOK_MB, D), grads[7].reshape(MICRO, TOK_MB, D), grads[0], grads[1], grads[2], grads[3], grads[4], grads[5], grads[6])
```

```python
import functools

import jax
import jax.numpy as jnp
from jax import lax
from jax.experimental import pallas as pl
from jax.experimental.pallas import tpu as pltpu
from jax.sharding import PartitionSpec as P

D = 768
HD = 64
FF = 3072
SEQ = 512
MICRO = 2
GROUP = 8
PIECE = D // GROUP
HALF_PIECE = PIECE // 2
UNIT = 3 * HALF_PIECE
BIT_C, BIT_X, BIT_Y = 1, 2, 4
NEG = -1000000000.0
BF = jnp.bfloat16
F32 = jnp.float32
VMEM_LIMIT = 56 * 1024 * 1024

GATHERED = (
    ("first", (0, BIT_X)),
    ("first", (BIT_Y, BIT_Y | BIT_X)),
    ("first", (BIT_C, BIT_C | BIT_X)),
    ("first", (BIT_C | BIT_Y, BIT_C | BIT_Y | BIT_X)),
    ("second", (0, BIT_Y)),
    ("second", (BIT_X, BIT_X | BIT_Y)),
    ("second", (BIT_C, BIT_C | BIT_Y)),
    ("second", (BIT_C | BIT_X, BIT_C | BIT_X | BIT_Y)),
)


def nn(a, b):
    return lax.dot_general(a, b, (((1,), (0,)), ((), ())), preferred_element_type=F32)


def nt(a, b):
    return lax.dot_general(a, b, (((1,), (1,)), ((), ())), preferred_element_type=F32)


def tn(a, b):
    return lax.dot_general(a, b, (((0,), (0,)), ((), ())), preferred_element_type=F32)


def normalize(values):
    centred = values - jnp.mean(values, axis=-1, keepdims=True)
    inv_std = lax.rsqrt(jnp.mean(centred * centred, axis=-1, keepdims=True) + 1e-06)
    return centred * inv_std, inv_std


def norm_back(upstream, normed, inv_std, gain_vec):
    scaled = upstream * gain_vec
    centred_grad = (
        scaled
        - jnp.mean(scaled, axis=-1, keepdims=True)
        - normed * jnp.mean(scaled * normed, axis=-1, keepdims=True)
    )
    return centred_grad * inv_std


def colsum(values):
    return jnp.sum(values, axis=0, keepdims=True)


def start_weights(place, own, parts, full, sems):
    copies = []

    def go(src, dst):
        copy = pltpu.make_async_copy(src, dst, sems.at[len(copies)])
        copy.start()
        copies.append(copy)

    go(own, full.at[0])
    for (kind, flips), part in zip(GATHERED, parts):
        for unit, flip in enumerate(flips):
            row = pl.multiple_of((place ^ flip) * PIECE, PIECE)
            mid = pl.multiple_of(row + HALF_PIECE, HALF_PIECE)
            base = unit * UNIT
            if kind == "first":
                go(part.at[pl.ds(base, PIECE)], full.at[1, pl.ds(row, PIECE)])
                go(part.at[pl.ds(base + PIECE, HALF_PIECE)], full.at[2, pl.ds(row, HALF_PIECE)])
            else:
                go(part.at[pl.ds(base, HALF_PIECE)], full.at[2, pl.ds(mid, HALF_PIECE)])
                go(part.at[pl.ds(base + HALF_PIECE, PIECE)], full.at[3, pl.ds(row, PIECE)])
    return copies


N_COPIES = 1 + 4 * len(GATHERED)


def store_pieces(place, acc, keep_ref, send_ref, slot):
    for flip in range(GROUP):
        row = pl.multiple_of((place ^ flip) * PIECE, PIECE)
        target = send_ref if flip & 1 else keep_ref
        target[flip // 2, slot] = acc[pl.ds(row, PIECE), :].astype(BF)


def attend_forward(student, place_ref, clips_ref, *refs):
    xa, xb, seg_row, seg_col, gain, bias, own = refs[:7]
    parts = refs[7:15]
    if student:
        full, qkv_out, lse_out, ctx_out, pre_out, quant_out, quant_t_out, xq_out, xqt_out = refs[15:24]
        rows, mask_bias, attn, ctx_t, sems = refs[24:]
    else:
        qkv_out, first_out, first_low_out = refs[15:18]
        full, rows, mask_bias, attn, ctx_t, sems = refs[18:]
        xq_out = rows
    place = place_ref[0]
    copies = start_weights(place, own, parts, full, sems)
    half = xa.shape[0]
    slots = full.shape[0]
    heads = D // slots // HD
    width = heads * HD
    rows[:half, :] = xa[...]
    rows[half:, :] = xb[...]
    if student:
        level = clips_ref[0]
        xq = (level * jnp.tanh(rows[...].astype(F32) / level)).astype(BF)
        xq_out[...] = xq
        xqt_out[...] = xq.T
    mask_bias[...] = jnp.where(seg_col[...] == seg_row[...], 0.0, NEG)
    attn[...] = jnp.zeros_like(attn)
    for copy in copies:
        copy.wait()

    def slot_step(slot, carry):
        qkv = nn(xq_out[...], full[slot, :, : 3 * width]).astype(BF)
        qkv_out[slot] = qkv
        for head in range(heads):
            lo = head * HD
            queries = qkv[:, lo : lo + HD] * BF(0.125)
            key_rows = qkv[:, width + lo : width + lo + HD]
            value_rows = qkv[:, 2 * width + lo : 2 * width + lo + HD]
            scores = nt(key_rows, queries) + mask_bias[...]
            peak = jnp.max(scores, axis=0, keepdims=True)
            powers = jnp.exp(scores - peak)
            total = jnp.sum(powers, axis=0, keepdims=True)
            probs = (powers * (1.0 / total)).astype(BF)
            ctx_t[lo : lo + HD, :] = tn(value_rows, probs)
            if student:
                lse_out[slot, head : head + 1, :] = peak + jnp.log(total)
        context = ctx_t[...].T
        if student:
            ctx_out[slot] = context
            level = clips_ref[1]
            low = (level * jnp.tanh(context / level)).astype(BF)
        else:
            low = context.astype(BF)
        attn[...] += nt(low, full[slot, :, 3 * width :])
        return carry

    lax.fori_loop(0, slots, slot_step, 0)
    pre = rows[...].astype(F32) + attn[...]
    first = normalize(pre)[0] * gain[...] + bias[...]
    if student:
        pre_out[...] = pre
        level = clips_ref[2]
        quant = (level * jnp.tanh(first / level)).astype(BF)
        quant_out[...] = quant
        quant_t_out[...] = quant.T
    else:
        first_out[...] = first
        first_low_out[...] = first.astype(BF)


def hidden_forward(student, place_ref, clips_ref, *refs):
    quant, own = refs[:2]
    parts = refs[2:10]
    if student:
        full, act_out, act_t_out, slope_out, clip_out = refs[10:15]
        pre, sems = refs[15:]
    else:
        (act_out,) = refs[10:11]
        full, pre, sems = refs[11:]
    copies = start_weights(place_ref[0], own, parts, full, sems)
    for copy in copies:
        copy.wait()
    slots = full.shape[0]
    step = 64

    def slot_step(slot, carry):
        pre[...] = nn(quant[...], full[slot])

        def row_step(index, carry):
            at = pl.ds(pl.multiple_of(index * step, step), step)
            values = pre[at, :]
            cdf = 0.5 * (1.0 + lax.erf(values * 0.7071067811865476))
            act = values * cdf
            if student:
                level = clips_ref[3]
                inverse = 1.0 / level
                ratio = act * inverse
                tangent = jnp.tanh(ratio)
                act_out[slot, at, :] = (level * tangent).astype(BF)
                slope = 1.0 - tangent * tangent
                density = jnp.exp(-0.5 * values * values) * 0.3989422804014327
                slope_out[slot, at, :] = (slope * (cdf + values * density)).astype(BF)
                clip_out[slot, at, :] = (tangent - ratio * slope).astype(BF)
            else:
                act_out[slot, at, :] = act.astype(BF)
            return carry

        lax.fori_loop(0, SEQ // step, row_step, 0)
        if student:
            act_t_out[slot] = act_out[slot].T
        return carry

    lax.fori_loop(0, slots, slot_step, 0)


def output_forward(student, place_ref, *refs):
    act, gain, bias, own = refs[:4]
    parts = refs[4:12]
    if student:
        pre, gain_one, bias_one, t_result, grad_a, grad_b = refs[12:18]
        full, own_out, partner_out, grad_out, low_out, gain_out, bias_out = refs[18:25]
        acc, sems = refs[25:]
    else:
        (first_in,) = refs[12:13]
        (result_out,) = refs[13:14]
        full, acc, sems = refs[14:]
    copies = start_weights(place_ref[0], own, parts, full, sems)
    if student:
        acc[...] = normalize(pre[...])[0] * gain_one[...] + bias_one[...]
    else:
        acc[...] = first_in[...]
    for copy in copies:
        copy.wait()
    for slot in range(full.shape[0]):
        acc[...] += nn(act[slot], full[slot])
    normed, inv_std = normalize(acc[...])
    result = normed * gain[...] + bias[...]
    if not student:
        result_out[...] = result
        return
    half = grad_a.shape[0]
    own_out[...] = result[:half].astype(BF)
    partner_out[...] = result[half:].astype(BF)
    cotangent = jnp.concatenate([grad_a[...].astype(F32), grad_b[...].astype(F32)], axis=0)
    grad_result = cotangent + result - t_result[...]
    gain_out[...] = colsum(grad_result * normed)
    bias_out[...] = colsum(grad_result)
    grad_pre = norm_back(grad_result, normed, inv_std, gain[...])
    grad_out[...] = grad_pre
    low_out[...] = grad_pre.astype(BF)


def weight_grad(place_ref, left_t, right, keep_ref, send_ref, acc):
    def slot_step(slot, carry):
        left = left_t[slot] if len(left_t.shape) == 3 else left_t[...]
        rows = right[slot] if len(right.shape) == 3 else right[...]
        acc[...] = nn(left, rows)
        store_pieces(place_ref[0], acc, keep_ref, send_ref, slot)
        return carry

    lax.fori_loop(0, keep_ref.shape[1], slot_step, 0)


def hidden_back(grad_low, full, slope, clip, grad_out, clip_out):
    clip_out[...] = jnp.zeros_like(clip_out)

    def slot_step(slot, carry):
        grad = nt(grad_low[...], full[slot])
        grad_out[slot] = (grad * slope[slot].astype(F32)).astype(BF)
        clip_out[...] += colsum(grad * clip[slot].astype(F32))
        return carry

    lax.fori_loop(0, full.shape[0], slot_step, 0)


def first_back(
    clips_ref, grad_hidden, full, pre, gain, bias, grad_two,
    grad_out, low_out, low_t_out, gain_out, bias_out, clip_out, acc,
):
    acc[...] = jnp.zeros_like(acc)

    def slot_step(slot, carry):
        acc[...] += nt(grad_hidden[slot], full[slot])
        return carry

    lax.fori_loop(0, full.shape[0], slot_step, 0)
    normed, inv_std = normalize(pre[...])
    first = normed * gain[...] + bias[...]
    level = clips_ref[2]
    ratio = first / level
    tangent = jnp.tanh(ratio)
    slope = 1.0 - tangent * tangent
    grad_fq = acc[...]
    clip_out[...] = colsum(grad_fq * (tangent - ratio * slope))
    upstream = grad_fq * slope + grad_two[...]
    gain_out[...] = colsum(upstream * normed)
    bias_out[...] = colsum(upstream)
    grad_pre = norm_back(upstream, normed, inv_std, gain[...])
    grad_out[...] = grad_pre
    low = grad_pre.astype(BF)
    low_out[...] = low
    low_t_out[...] = low.T


def attend_back(first, last, place_ref, clips_ref, *refs):
    seg_row, seg_col, qkv, t_qkv, lse, ctx, low, low_t, xq_t, full = refs[:10]
    rest = list(refs[10:])
    grad_in = None if first else rest.pop(0)
    if last:
        grad_one, xa, xb = rest[:3]
        rest = rest[3:]
    keep_ref, send_ref, clip_one_out = rest[:3]
    rest = rest[3:]
    if last:
        own_out, partner_out, clip_zero_out = rest[:3]
        rest = rest[3:]
    else:
        grad_out = rest.pop(0)
    mask_bias, mask_scale, grad_qkv, acc = rest
    same = seg_col[...] == seg_row[...]
    mask_bias[...] = jnp.where(same, 0.0, NEG)
    mask_scale[...] = jnp.where(same, 1.0 / SEQ, 0.0)
    width = ctx.shape[-1]
    heads = width // HD
    level = clips_ref[1]
    context = ctx[0]
    ratio = context / level
    tangent = jnp.tanh(ratio)
    slope = 1.0 - tangent * tangent
    grad_cq = nn(low[...], full[0, :, 3 * width :])
    clip_one_out[...] = colsum(grad_cq * (tangent - ratio * slope))
    grad_ctx = (grad_cq * slope).astype(BF)
    acc[:, 3 * width :] = nn(low_t[...], (level * tangent).astype(BF))
    for head in range(heads):
        lo = head * HD
        queries = qkv[0, :, lo : lo + HD] * BF(0.125)
        key_rows = qkv[0, :, width + lo : width + lo + HD]
        value_rows = qkv[0, :, 2 * width + lo : 2 * width + lo + HD]
        t_queries = t_qkv[0, :, lo : lo + HD] * BF(0.125)
        t_keys = t_qkv[0, :, width + lo : width + lo + HD]
        upstream = grad_ctx[:, lo : lo + HD]
        scores = nt(key_rows, queries)
        probs = jnp.exp(scores + mask_bias[...] - lse[0, head : head + 1, :])
        grad_probs = nt(value_rows, upstream)
        grad_values = nn(probs.astype(BF), upstream)
        row_sum = jnp.sum(probs * grad_probs, axis=0, keepdims=True)
        gap = scores - nt(t_keys, t_queries)
        grad_scores = (probs * (grad_probs - row_sum) + gap * mask_scale[...]).astype(BF)
        grad_keys = nn(grad_scores, queries)
        grad_queries = tn(key_rows, grad_scores).T * 0.125
        grad_qkv[:, lo : lo + HD] = grad_queries.astype(BF)
        grad_qkv[:, width + lo : width + lo + HD] = grad_keys.astype(BF)
        grad_qkv[:, 2 * width + lo : 2 * width + lo + HD] = grad_values.astype(BF)
    acc[:, : 3 * width] = nn(xq_t[...], grad_qkv[...])
    store_pieces(place_ref[0], acc, keep_ref, send_ref, 0)
    grad_xq = nt(grad_qkv[...], full[0, :, : 3 * width])
    if not first:
        grad_xq = grad_xq + grad_in[...]
    if not last:
        grad_out[...] = grad_xq
        return
    half = xa.shape[0]
    level = clips_ref[0]
    total = jnp.zeros((1, D), F32)
    for start, x_ref, out in ((0, xa, own_out), (half, xb, partner_out)):
        ratio = x_ref[...].astype(F32) / level
        tangent = jnp.tanh(ratio)
        slope = 1.0 - tangent * tangent
        grad = grad_xq[start : start + half]
        total = total + colsum(grad * (tangent - ratio * slope))
        out[...] = (grad * slope + grad_one[start : start + half, :]).astype(out.dtype)
    clip_zero_out[...] = total


def finish(place_ref, own_piece, p1, p2, p3, p4, p5, latent, scale, out):
    place = place_ref[0]

    def put(flip, first_half, source, unit):
        row = (place ^ flip) * PIECE + (0 if first_half else HALF_PIECE)
        at = pl.ds(pl.multiple_of(row, HALF_PIECE), HALF_PIECE)
        values = source[unit * HALF_PIECE : (unit + 1) * HALF_PIECE, :].astype(F32)
        out[at, :] = values + scale[...] * latent[at, :].astype(F32)

    put(0, True, own_piece, 0)
    put(0, False, own_piece, 1)
    put(BIT_X, True, p1, 0)
    put(BIT_Y, False, p1, 1)
    put(BIT_Y, True, p2, 0)
    put(BIT_Y | BIT_X, True, p2, 1)
    put(BIT_X, False, p3, 0)
    put(BIT_X | BIT_Y, False, p3, 1)
    for unit, flip in enumerate((0, BIT_X, BIT_Y, BIT_Y | BIT_X)):
        put(BIT_C | flip, True, p4, unit)
    for unit, flip in enumerate((0, BIT_Y, BIT_X, BIT_X | BIT_Y)):
        put(BIT_C | flip, False, p5, unit)


VM = pl.BlockSpec(memory_space=pltpu.VMEM)
SM = pl.BlockSpec(memory_space=pltpu.SMEM)
ANY = pl.BlockSpec(memory_space=pl.ANY)
DMA_SEMS = pltpu.SemaphoreType.DMA((N_COPIES,))


def shape(dims, dtype):
    return jax.ShapeDtypeStruct(dims, dtype)


def call(name, body, args, specs, outs, scratch, flops, out_specs=None, grid=None):
    total = sum(a.size * a.dtype.itemsize for a in args) + sum(
        o.size * o.dtype.itemsize for o in outs
    )
    return pl.pallas_call(
        body,
        name=name,
        grid=grid or (),
        in_specs=specs,
        out_specs=out_specs or [VM] * len(outs),
        out_shape=outs,
        scratch_shapes=scratch,
        compiler_params=pltpu.CompilerParams(vmem_limit_bytes=VMEM_LIMIT),
        cost_estimate=pl.CostEstimate(flops=flops, bytes_accessed=total, transcendentals=0),
    )(*args)


def flip_pairs(size, bit):
    return [(i, i ^ bit) for i in range(size)]


def swap(array, axis, size, bit):
    return lax.ppermute(array, axis, flip_pairs(size, bit))


def ring(array, size, step):
    return lax.ppermute(array, "head", [(i, (i + step) % size) for i in range(size)])


def gather_pieces(piece, dp, n):
    z = [ring(piece, n, step) for step in range(1, n)]
    first = jnp.concatenate([z[0], z[1][:HALF_PIECE]])
    second = jnp.concatenate([z[1][HALF_PIECE:], z[2]])
    first = jnp.concatenate([first, swap(first, "dp", dp, BIT_X)])
    second = jnp.concatenate([second, swap(second, "dp", dp, BIT_Y)])
    first_far = swap(first, "dp", dp, BIT_Y)
    second_far = swap(second, "dp", dp, BIT_X)
    return (
        first,
        first_far,
        swap(first, "dp", dp, BIT_C),
        swap(first_far, "dp", dp, BIT_C),
        second,
        second_far,
        swap(second, "dp", dp, BIT_C),
        swap(second_far, "dp", dp, BIT_C),
    )


def reduce_pieces(keep, send, dp):
    got = swap(send, "dp", dp, BIT_C)
    total = keep.astype(F32) + got.astype(F32)
    top, low = total[:, :, :HALF_PIECE], total[:, :, HALF_PIECE:]
    top_got = swap(jnp.stack([top[1], top[3]]).astype(BF), "dp", dp, BIT_X).astype(F32)
    low_got = swap(jnp.stack([low[2], low[3]]).astype(BF), "dp", dp, BIT_Y).astype(F32)
    top_two = swap((top[2] + top_got[1]).astype(BF), "dp", dp, BIT_Y).astype(F32)
    low_two = swap((low[1] + low_got[1]).astype(BF), "dp", dp, BIT_X).astype(F32)
    mine = jnp.concatenate(
        [top[0] + top_got[0] + top_two, low[0] + low_got[0] + low_two], axis=1
    )
    bit = GROUP
    while bit < dp:
        mine = mine + swap(mine.astype(BF), "dp", dp, bit).astype(F32)
        bit *= 2
    return mine


def reduce_slots(pieces, n):
    total = pieces[0]
    for step in range(1, n):
        total = total + ring(pieces[step].astype(BF), n, -step).astype(F32)
    return total


def share_pieces(piece, dp):
    top, low = piece[:HALF_PIECE], piece[HALF_PIECE:]
    top_x = swap(top, "dp", dp, BIT_X)
    low_y = swap(low, "dp", dp, BIT_Y)
    pair = jnp.concatenate([top, top_x])
    pair_low = jnp.concatenate([low, low_y])
    near = jnp.concatenate([top_x, low_y])
    far = swap(pair, "dp", dp, BIT_Y)
    far_low = swap(pair_low, "dp", dp, BIT_X)
    other = swap(jnp.concatenate([pair, far]), "dp", dp, BIT_C)
    other_low = swap(jnp.concatenate([pair_low, far_low]), "dp", dp, BIT_C)
    return near, far, far_low, other, other_low


def sum_over(values, sizes):
    for axis, size in sizes:
        bit = 1
        while bit < size:
            values = values + swap(values, axis, size, bit)
            bit *= 2
    return values


def on_device(
    dp,
    n,
    hidden_in,
    teacher_in,
    out_grad,
    segment_ids,
    qkv_latent,
    out_latent,
    ffn_in_latent,
    ffn_out_latent,
    norm_gain,
    norm_bias,
    clips,
    teacher_qkv,
    teacher_out,
    teacher_ffn_in,
    teacher_ffn_out,
    teacher_gain,
    teacher_bias,
):
    h = lax.axis_index("head")
    place = lax.axis_index("dp") % GROUP
    parity = h % MICRO
    half = hidden_in.shape[1]
    width = qkv_latent.shape[-1]
    heads = width // HD
    place_arr = place.astype(jnp.int32).reshape(1)

    def pick(array, index):
        return lax.dynamic_index_in_dim(array, index, 0, keepdims=False)

    def exchange(array):
        return swap(array, "head", n, 1)

    def piece_of(array):
        return lax.dynamic_slice_in_dim(array, place * PIECE, PIECE, axis=0)

    x_own = pick(hidden_in, parity)
    x_far = exchange(pick(hidden_in, 1 - parity))
    t_own = pick(teacher_in, parity)
    t_far = exchange(pick(teacher_in, 1 - parity))
    g_own = pick(out_grad, parity)
    g_far = exchange(pick(out_grad, 1 - parity))
    seg = pick(pick(segment_ids, parity), h // MICRO)
    seg = jnp.where(parity == 0, seg, jnp.concatenate([seg[half:], seg[:half]]))
    seg_row, seg_col = seg.reshape(1, SEQ), seg.reshape(SEQ, 1)

    def attention_weights(qkv, out):
        return jnp.concatenate([qkv[0], qkv[1], qkv[2], out.T], axis=1)

    t_attn = attention_weights(teacher_qkv, teacher_out)
    t_attn_parts = gather_pieces(piece_of(t_attn), dp, n)

    latents = [attention_weights(qkv_latent, out_latent), ffn_in_latent, ffn_out_latent]
    columns = jnp.sum(jnp.square(latents[0].astype(F32)), axis=0).reshape(4, width).sum(axis=1)
    squares = jnp.concatenate(
        [
            columns,
            jnp.sum(jnp.square(ffn_in_latent.astype(F32))).reshape(1),
            jnp.sum(jnp.square(ffn_out_latent.astype(F32))).reshape(1),
        ]
    )
    totals = sum_over(jnp.pad(squares, (0, 122)).reshape(1, 128), [("head", n)])[0, :6]
    entries = jnp.array([D * D, D * D, D * D, D * D, D * FF, FF * D], F32)
    levels_six = jnp.sqrt(totals / entries + 1e-06)
    levels = [
        jnp.repeat(levels_six[:4], width, total_repeat_length=D).reshape(1, D),
        levels_six[4].reshape(1, 1),
        levels_six[5].reshape(1, 1),
    ]

    def binarize(latent, level):
        return (level * jnp.tanh(2.0 * latent.astype(F32) / level)).astype(BF)

    bins = [binarize(latent, level) for latent, level in zip(latents, levels)]
    s_parts = [None] * 3
    s_parts[0] = gather_pieces(piece_of(bins[0]), dp, n)
    t_in_parts = gather_pieces(piece_of(teacher_ffn_in), dp, n)
    s_parts[1] = gather_pieces(piece_of(bins[1]), dp, n)
    t_out_parts = gather_pieces(piece_of(teacher_ffn_out), dp, n)
    s_parts[2] = gather_pieces(piece_of(bins[2]), dp, n)

    row = lambda array, index: array[index].reshape(1, D)
    big = pltpu.VMEM((n, D, D), BF)
    mm = 2 * SEQ * D * D

    attn_scratch = [
        pltpu.VMEM((SEQ, D), BF),
        pltpu.VMEM((SEQ, SEQ), F32),
        pltpu.VMEM((SEQ, D), F32),
        pltpu.VMEM((width, SEQ), F32),
        DMA_SEMS,
    ]
    t_qkv, t_first, t_first_low = call(
        "teacher_attend",
        functools.partial(attend_forward, False),
        (place_arr, clips, t_own, t_far, seg_row, seg_col, row(teacher_gain, 0), row(teacher_bias, 0), t_attn)
        + t_attn_parts,
        [SM, SM] + [VM] * 6 + [ANY] * 9,
        [shape((n, SEQ, 3 * width), BF), shape((SEQ, D), F32), shape((SEQ, D), BF)],
        [big] + attn_scratch,
        8 * mm,
    )
    full_attn, qkv, lse, ctx, pre_one, quant, quant_t, xq, xq_t = call(
        "student_attend",
        functools.partial(attend_forward, True),
        (place_arr, clips, x_own, x_far, seg_row, seg_col, row(norm_gain, 0), row(norm_bias, 0), bins[0])
        + s_parts[0],
        [SM, SM] + [VM] * 6 + [ANY] * 9,
        [
            shape((n, D, D), BF),
            shape((n, SEQ, 3 * width), BF),
            shape((n, 8, SEQ), F32),
            shape((n, SEQ, width), F32),
            shape((SEQ, D), F32),
            shape((SEQ, D), BF),
            shape((D, SEQ), BF),
            shape((SEQ, D), BF),
            shape((D, SEQ), BF),
        ],
        attn_scratch,
        8 * mm,
    )
    (t_act,) = call(
        "teacher_hidden",
        functools.partial(hidden_forward, False),
        (place_arr, clips, t_first_low, teacher_ffn_in) + t_in_parts,
        [SM, SM, VM] + [ANY] * 9,
        [shape((n, SEQ, D), BF)],
        [big, pltpu.VMEM((SEQ, D), F32), DMA_SEMS],
        6 * mm,
    )
    full_in, act, act_t, slope, clip_term = call(
        "student_hidden",
        functools.partial(hidden_forward, True),
        (place_arr, clips, quant, bins[1]) + s_parts[1],
        [SM, SM, VM] + [ANY] * 9,
        [
            shape((n, D, D), BF),
            shape((n, SEQ, D), BF),
            shape((n, D, SEQ), BF),
            shape((n, SEQ, D), BF),
            shape((n, SEQ, D), BF),
        ],
        [pltpu.VMEM((SEQ, D), F32), DMA_SEMS],
        8 * mm,
    )
    (t_result,) = call(
        "teacher_output",
        functools.partial(output_forward, False),
        (place_arr, t_act, row(teacher_gain, 1), row(teacher_bias, 1), teacher_ffn_out) + t_out_parts + (t_first,),
        [SM] + [VM] * 3 + [ANY] * 9 + [VM],
        [shape((SEQ, D), F32)],
        [big, pltpu.VMEM((SEQ, D), F32), DMA_SEMS],
        4 * mm,
    )
    full_out, out_own, out_far, grad_two, low_two, gain_two, bias_two = call(
        "student_output",
        functools.partial(output_forward, True),
        (place_arr, act, row(norm_gain, 1), row(norm_bias, 1), bins[2])
        + s_parts[2]
        + (pre_one, row(norm_gain, 0), row(norm_bias, 0), t_result, g_own, g_far),
        [SM] + [VM] * 3 + [ANY] * 9 + [VM] * 6,
        [
            shape((n, D, D), BF),
            shape((half, D), BF),
            shape((half, D), BF),
            shape((SEQ, D), F32),
            shape((SEQ, D), BF),
            shape((1, D), F32),
            shape((1, D), F32),
        ],
        [pltpu.VMEM((SEQ, D), F32), DMA_SEMS],
        4 * mm,
    )

    def grad_call(name, left_t, right):
        return call(
            name,
            weight_grad,
            (place_arr, left_t, right),
            [SM, VM, VM],
            [shape((GROUP // 2, n, PIECE, D), BF)] * 2,
            [pltpu.VMEM((D, D), F32)],
            4 * mm,
        )

    grad_out_w = reduce_pieces(*grad_call("ffn_out_weight", act_t, low_two), dp)
    grad_hidden, clip_three = call(
        "hidden_back",
        hidden_back,
        (low_two, full_out, slope, clip_term),
        [VM] * 4,
        [shape((n, SEQ, D), BF), shape((1, D), F32)],
        [],
        5 * mm,
    )
    grad_in_w = reduce_pieces(*grad_call("ffn_in_weight", quant_t, grad_hidden), dp)
    grad_one, low_one, low_one_t, gain_one, bias_one, clip_two = call(
        "first_back",
        first_back,
        (clips, grad_hidden, full_in, pre_one, row(norm_gain, 0), row(norm_bias, 0), grad_two),
        [SM] + [VM] * 6,
        [
            shape((SEQ, D), F32),
            shape((SEQ, D), BF),
            shape((D, SEQ), BF),
            shape((1, D), F32),
            shape((1, D), F32),
            shape((1, D), F32),
        ],
        [pltpu.VMEM((SEQ, D), F32)],
        4 * mm,
    )
    clip_one = jnp.zeros((1, width), F32)
    grad_xq = None
    attn_slots = []
    for slot in range(n):
        first, last = slot == 0, slot == n - 1

        def at(*dims, slot=slot):
            return pl.BlockSpec((1,) + dims, lambda i: (slot, 0, 0))

        def whole(*dims):
            return pl.BlockSpec(dims, lambda i: (0,) * len(dims))

        args = [place_arr, clips, seg_row, seg_col, qkv, t_qkv, lse, ctx, low_one, low_one_t, xq_t, full_attn]
        specs = [
            SM,
            SM,
            whole(1, SEQ),
            whole(SEQ, 1),
            at(SEQ, 3 * width),
            at(SEQ, 3 * width),
            at(8, SEQ),
            at(SEQ, width),
            whole(SEQ, D),
            whole(D, SEQ),
            whole(D, SEQ),
            at(D, D),
        ]
        if not first:
            args.append(grad_xq)
            specs.append(whole(SEQ, D))
        outs = [shape((GROUP // 2, 1, PIECE, D), BF)] * 2 + [shape((1, width), F32)]
        if last:
            args += [grad_one, x_own, x_far]
            specs += [whole(SEQ, D), whole(half, D), whole(half, D)]
            outs += [shape((half, D), F32), shape((half, D), BF), shape((1, D), F32)]
        else:
            outs += [shape((SEQ, D), F32)]
        results = pl.pallas_call(
            functools.partial(attend_back, first, last),
            name="attend_back",
            grid=(1,),
            in_specs=specs,
            out_specs=[whole(*o.shape) for o in outs],
            out_shape=outs,
            scratch_shapes=[
                pltpu.VMEM((SEQ, SEQ), F32),
                pltpu.VMEM((SEQ, SEQ), F32),
                pltpu.VMEM((SEQ, 3 * width), BF),
                pltpu.VMEM((D, D), F32),
            ],
            compiler_params=pltpu.CompilerParams(vmem_limit_bytes=VMEM_LIMIT),
            cost_estimate=pl.CostEstimate(flops=5 * mm, bytes_accessed=12 << 20, transcendentals=0),
        )(*args)
        attn_slots.append(reduce_pieces(results[0], results[1], dp)[0])
        clip_one = clip_one + results[2]
        if not last:
            grad_xq = results[3]
    in_grad_own, in_grad_far, clip_zero = results[3:6]

    everywhere = [("dp", dp), ("head", n)]
    norms = sum_over(jnp.concatenate([gain_one, gain_two, bias_one, bias_two]), everywhere)
    pieces = [
        reduce_slots(attn_slots, n),
        reduce_slots([grad_in_w[slot] for slot in range(n)], n),
        reduce_slots([grad_out_w[slot] for slot in range(n)], n),
    ]
    direct, scale_terms = [], []
    for piece, latent, level in zip(pieces, latents, levels):
        unit = 2.0 * piece_of(latent).astype(F32) / level
        tangent = jnp.tanh(unit)
        slope_sq = 1.0 - tangent * tangent
        direct.append((piece * 2.0 * slope_sq).astype(BF))
        scale_terms.append(jnp.sum(piece * (tangent - unit * slope_sq), axis=0))
    scalars = jnp.concatenate(
        [
            scale_terms[0].reshape(4, width).sum(axis=1),
            jnp.stack(
                [
                    jnp.sum(scale_terms[1]),
                    jnp.sum(scale_terms[2]),
                ]
            ),
            jnp.stack([jnp.sum(clip_zero), jnp.sum(clip_one), jnp.sum(clip_two), jnp.sum(clip_three)]),
        ]
    )
    repeats = dp // GROUP
    weights = jnp.array([1.0 / repeats] * 6 + [1.0] * 4, F32)
    sums = sum_over(jnp.pad(scalars * weights, (0, 118)).reshape(1, 128), everywhere)[0]
    scales = sums[:6] / (entries * levels_six)
    scale_rows = [
        jnp.repeat(scales[:4], width, total_repeat_length=D).reshape(1, D),
        jnp.broadcast_to(scales[4].reshape(1, 1), (1, D)),
        jnp.broadcast_to(scales[5].reshape(1, 1), (1, D)),
    ]
    finals = []
    for piece, latent, scale_row in zip(direct, latents, scale_rows):
        finals.append(
            call(
                "finish",
                finish,
                (place_arr, piece) + share_pieces(piece, dp) + (latent, scale_row),
                [SM] + [VM] * 8,
                [shape((D, D), F32)],
                [],
                0,
            )[0]
        )
    attn_grad = finals[0]
    qkv_grad = jnp.stack([attn_grad[:, j * width : (j + 1) * width] for j in range(3)])

    def both(own, far):
        first_row = jnp.where(parity == 0, own, far)
        second_row = jnp.where(parity == 0, far, own)
        return jnp.stack([first_row, second_row])

    return (
        both(out_own, exchange(out_far)),
        both(in_grad_own, exchange(in_grad_far).astype(F32)),
        qkv_grad,
        attn_grad[:, 3 * width :].T,
        finals[1],
        finals[2],
        norms[:2],
        norms[2:],
        sums[6:10],
    )


def solution(mesh):
    placed = (
        P(None, ("dp", "head"), None),
        P(None, ("dp", "head"), None),
        P(None, ("dp", "head"), None),
        P(None, "dp", None),
        P(None, None, "head"),
        P("head", None),
        P(None, "head"),
        P("head", None),
        P(),
        P(),
        P(),
        P(None, None, "head"),
        P("head", None),
        P(None, "head"),
        P("head", None),
        P(),
        P(),
    )
    return jax.shard_map(
        functools.partial(on_device, mesh.shape["dp"], mesh.shape["head"]),
        mesh=mesh,
        in_specs=placed,
        out_specs=(
            P(None, ("dp", "head"), None),
            P(None, ("dp", "head"), None),
            P(None, None, "head"),
            P("head", None),
            P(None, "head"),
            P("head", None),
            P(),
            P(),
            P(),
        ),
        check_vma=False,
    )
```

```python
import functools

import jax
import jax.numpy as jnp
from jax import lax
from jax.experimental import pallas as pl
from jax.experimental.pallas import tpu as pltpu
from jax.sharding import PartitionSpec as P

D = 768
HD = 64
FF = 3072
SEQ = 512
MICRO = 2
GROUP = 8
PIECE = D // GROUP
BIT_C, BIT_X, BIT_Y = 1, 2, 4
NEG = -1000000000.0
BF = jnp.bfloat16
F32 = jnp.float32
VMEM_WIDE = 56 * 1024 * 1024
VMEM_SMALL = 16 * 1024 * 1024

def nn(a, b):
    return lax.dot_general(a, b, (((1,), (0,)), ((), ())), preferred_element_type=F32)


def nt(a, b):
    return lax.dot_general(a, b, (((1,), (1,)), ((), ())), preferred_element_type=F32)


def tn(a, b):
    return lax.dot_general(a, b, (((0,), (0,)), ((), ())), preferred_element_type=F32)


def normalize(values):
    centred = values - jnp.mean(values, axis=-1, keepdims=True)
    inv_std = lax.rsqrt(jnp.mean(centred * centred, axis=-1, keepdims=True) + 1e-06)
    return centred * inv_std, inv_std


def norm_back(upstream, normed, inv_std, gain_vec):
    scaled = upstream * gain_vec
    centred_grad = (
        scaled
        - jnp.mean(scaled, axis=-1, keepdims=True)
        - normed * jnp.mean(scaled * normed, axis=-1, keepdims=True)
    )
    return centred_grad * inv_std


def colsum(values):
    return jnp.sum(values, axis=0, keepdims=True)


def crosswise(core, slot):
    return (slot + core) % 3 + 1


def xor_of(core, slot):
    return (1 - core) * slot + core * ((slot + 1) % 3 + 1)


def start_weights(place, by_xor, own, parts, full, sems):
    core = place & BIT_C
    bit_one = BIT_X + core * (BIT_Y - BIT_X)
    bit_two = BIT_X + BIT_Y - bit_one
    both = BIT_X | BIT_Y
    copies = []

    def go(src, dst):
        copy = pltpu.make_async_copy(src, dst, sems.at[len(copies)])
        copy.start()
        copies.append(copy)

    row = 0
    for array in own:
        go(array, full.at[0, pl.ds(row, array.shape[0])])
        row += array.shape[0]
    flips = (
        (0, bit_one),
        (bit_two, both),
        (BIT_C, BIT_C | bit_two),
        (BIT_C | bit_one, BIT_C | both),
    )
    for source, part in enumerate(parts):
        for unit in range(2):
            row = pl.multiple_of((place ^ flips[source][unit]) * PIECE, PIECE)
            for slot in range(1, N_SLOTS):
                if by_xor:
                    to = xor_of(core if source < 2 else 1 - core, slot)
                else:
                    to = slot if source < 2 else crosswise(1 - core, slot)
                start = (unit * (N_SLOTS - 1) + slot - 1) * PIECE
                go(part.at[pl.ds(start, PIECE)], full.at[to, pl.ds(row, PIECE)])
    return copies[: len(own)], copies[len(own) :]


def over_slots(copies, slots, step):
    for copy in copies[0]:
        copy.wait()
    step(0, 0)
    for copy in copies[1]:
        copy.wait()
    lax.fori_loop(1, slots, step, 0)


N_SLOTS = 4
N_PARTS = 4
N_COPIES = 2 + N_PARTS * 2 * (N_SLOTS - 1)


def store_pieces(place, acc, keep_ref, send_ref, keep_slot, send_slot):
    core = place & BIT_C
    bit_one = BIT_X + core * (BIT_Y - BIT_X)
    bit_two = BIT_X + BIT_Y - bit_one
    both = BIT_X | BIT_Y
    for index, flip in enumerate((0, bit_two, bit_one, both)):
        row = pl.multiple_of((place ^ flip) * PIECE, PIECE)
        keep_ref[index, keep_slot] = acc[pl.ds(row, PIECE), :].astype(BF)
    for index, flip in enumerate((0, bit_one, bit_two, both)):
        row = pl.multiple_of((place ^ BIT_C ^ flip) * PIECE, PIECE)
        send_ref[index, send_slot] = acc[pl.ds(row, PIECE), :].astype(BF)


ATTN_QKV = 3 * D // 4


def cut(meta, t_qkv, t_out, t_in, t_ffn_in, t_ffn_out, x_in, g_in, *refs):
    attn_piece, in_piece, out_piece, t_send, x_send, g_send, sems = refs
    place = meta[0]
    rows = pl.ds(pl.multiple_of(place * PIECE, PIECE), PIECE)
    there = 1 - meta[1]
    copies = [
        pltpu.make_async_copy(t_in.at[there], t_send, sems.at[1]),
        pltpu.make_async_copy(t_ffn_in.at[rows], in_piece, sems.at[2]),
        pltpu.make_async_copy(t_ffn_out.at[rows], out_piece, sems.at[3]),
        pltpu.make_async_copy(x_in.at[there], x_send, sems.at[4]),
        pltpu.make_async_copy(g_in.at[there], g_send, sems.at[5]),
    ]
    in_qkv = place < ATTN_QKV // PIECE

    @pl.when(in_qkv)
    def _():
        copy = pltpu.make_async_copy(t_qkv.at[rows], attn_piece, sems.at[0])
        copy.start()
        copy.wait()

    @pl.when(jnp.logical_not(in_qkv))
    def _():
        at = pl.ds(pl.multiple_of(place * PIECE - ATTN_QKV, PIECE), PIECE)
        copy = pltpu.make_async_copy(t_out.at[at], attn_piece, sems.at[0])
        copy.start()
        copy.wait()

    for copy in copies:
        copy.start()
    for copy in copies:
        copy.wait()


def sum_squares(qkv, out, ffn_in, ffn_out, attn, squares):
    attn[:ATTN_QKV, :] = qkv[...]
    attn[ATTN_QKV:, :] = out[...]
    squares[...] = jnp.zeros_like(squares)
    block = D // 4
    step_rows = 64
    for index, (latent, start, count) in enumerate(
        [(attn, j * block, block) for j in range(4)] + [(ffn_in, 0, D), (ffn_out, 0, D)]
    ):

        def step(i, carry, latent=latent, start=start):
            at = pl.ds(pl.multiple_of(start + i * step_rows, step_rows), step_rows)
            values = latent[at, :].astype(F32)
            return carry + jnp.sum((values * values).reshape(step_rows // 8, 8, D), axis=0)

        total = lax.fori_loop(0, count // step_rows, step, jnp.zeros((8, D), F32))
        squares[index : index + 1, :] = colsum(total)


def binarize(meta, squares, attn, ffn_in, ffn_out, *outs):
    bins, pieces, levels = outs[:3], outs[3:6], outs[6]
    entries = jnp.where(
        lax.broadcasted_iota(jnp.int32, (8, 1), 0) < 4, float(D * D), float(D * FF)
    )
    totals = jnp.sum(squares[...], axis=1, keepdims=True)
    levels[...] = jnp.broadcast_to(jnp.sqrt(totals / entries + 1e-06), (8, D))
    step_rows = 64
    for index, latent in enumerate((attn, ffn_in, ffn_out)):

        def step(i, carry, index=index, latent=latent):
            at = pl.ds(pl.multiple_of(i * step_rows, step_rows), step_rows)
            line = i // (D // 4 // step_rows) if index == 0 else index + 3
            level = levels[pl.ds(line, 1), :]
            bins[index][at, :] = (level * jnp.tanh(latent[at, :].astype(F32) * (2.0 / level))).astype(BF)
            return carry

        lax.fori_loop(0, D // step_rows, step, 0)
        pieces[index][...] = bins[index][pl.ds(pl.multiple_of(meta[0] * PIECE, PIECE), PIECE), :]


def same_segment(meta, segments):
    own = segments[meta[1], pl.ds(meta[2], 1), :].astype(F32)
    half = SEQ // 2
    turned = jnp.concatenate([own[:, half:], own[:, :half]], axis=1)
    lanes = jnp.where(meta[1] == 0, own, turned)
    column = jnp.broadcast_to(lanes, (8, SEQ)).T[:, :1]
    return column == lanes


S_SCALE, S_GAIN, S_BIAS, S_CLIP, S_ROWS = 0, 6, 8, 10, 16


def settle(attn, repeats, meta, levels, sums, *refs):
    count = (len(refs) - 2) // 2
    direct, sums_out = refs[-2:]
    at = pl.ds(pl.multiple_of(meta[0] * PIECE, PIECE), PIECE)
    block = meta[0] // 2
    sums_out[...] = sums[...]
    for index in range(count):
        level = levels[pl.ds(block, 1), :] if attn else levels[4 + index : 5 + index, :]
        grad, latent = refs[index][...], refs[count + index]
        unit = latent[at, :].astype(F32) * (2.0 / level)
        tangent = jnp.tanh(unit)
        slope = 1.0 - tangent * tangent
        direct[index] = (grad * 2.0 * slope).astype(BF)
        term = colsum(grad * (tangent - unit * slope)) * (1.0 / repeats)
        if attn:
            for j in range(4):
                sums_out[j : j + 1, :] = jnp.where(block == j, term, 0.0)
        else:
            sums_out[4 + index : 5 + index, :] = term


ROWS = 64


def by_rows(count, body):
    def step(index, carry):
        body(pl.ds(pl.multiple_of(index * ROWS, ROWS), ROWS))
        return carry

    lax.fori_loop(0, count // ROWS, step, 0)


def attend_forward(student, meta, clips_ref, *refs):
    xa, xb, segments, gain, bias = refs[:5]
    owned = 1 if student else 2
    own, refs = refs[5 : 5 + owned], refs[5 + owned :]
    parts, refs = refs[:N_PARTS], refs[N_PARTS:]
    if student:
        full, qkv_out, lse_out, ctx_out, pre_out, quant_out, quant_t_out, rows = refs[:8]
        mask_bias, attn, ctx_t, sems = refs[8:]
    else:
        qkv_out, first_out, first_low_out = refs[:3]
        full, rows, mask_bias, attn, ctx_t, sems = refs[3:]
    copies = start_weights(meta[0], True, own, parts, full, sems)
    half = xb.shape[0]
    slots = full.shape[0]
    width = D // slots
    heads = width // HD

    def x_at(at, index):
        return xa[meta[1], at, :] if index == 0 else xb[at, :]

    for index in range(2):

        def quantize(at, index=index):
            to = pl.ds(pl.multiple_of(at.start + index * half, ROWS), ROWS)
            values = x_at(at, index)
            if student:
                level = clips_ref[0]
                values = (level * jnp.tanh(values.astype(F32) / level)).astype(BF)
            rows[to, :] = values

        by_rows(half, quantize)
    mask_bias[...] = jnp.where(same_segment(meta, segments), 0.0, NEG)
    attn[...] = jnp.zeros_like(attn)

    def slot_step(slot, carry):
        qkv = nt(rows[...], full[slot, : 3 * width, :]).astype(BF)
        qkv_out[slot] = qkv
        for head in range(heads):
            lo = head * HD
            queries = qkv[:, lo : lo + HD] * BF(0.125)
            key_rows = qkv[:, width + lo : width + lo + HD]
            value_rows = qkv[:, 2 * width + lo : 2 * width + lo + HD]
            for at in range(0, SEQ, Q_BLOCK):
                scores = nt(key_rows, queries[at : at + Q_BLOCK]) + mask_bias[:, at : at + Q_BLOCK]
                peak = jnp.max(scores, axis=0, keepdims=True)
                powers = jnp.exp(scores - peak)
                total = jnp.sum(powers, axis=0, keepdims=True)
                probs = (powers * (1.0 / total)).astype(BF)
                ctx_t[lo : lo + HD, at : at + Q_BLOCK] = tn(value_rows, probs)
                if student:
                    lse_out[slot, head : head + 1, at : at + Q_BLOCK] = peak + jnp.log(total)
        context = ctx_t[...].T
        if student:
            ctx_out[slot] = context
            level = clips_ref[1]
            low = (level * jnp.tanh(context / level)).astype(BF)
        else:
            low = context.astype(BF)
        attn[...] += nn(low, full[slot, 3 * width :, :])
        return carry

    over_slots(copies, slots, slot_step)
    for index in range(2):

        def last(at, index=index):
            to = pl.ds(pl.multiple_of(at.start + index * half, ROWS), ROWS)
            pre = x_at(at, index).astype(F32) + attn[to, :]
            first = normalize(pre)[0] * gain[0:1, :] + bias[0:1, :]
            if student:
                pre_out[to, :] = pre
                level = clips_ref[2]
                quant_out[to, :] = (level * jnp.tanh(first / level)).astype(BF)
            else:
                first_out[to, :] = first
                first_low_out[to, :] = first.astype(BF)

        by_rows(half, last)
    if student:
        quant_t_out[...] = quant_out[...].T


Q_BLOCK = 512


def hidden_forward(student, meta, clips_ref, *refs):
    quant, own = refs[0], (refs[1],)
    parts = refs[2:6]
    if student:
        full, act_out, act_t_out, slope_out, clip_out = refs[6:11]
        pre, sems = refs[11:]
    else:
        (act_out,) = refs[6:7]
        full, pre, sems = refs[7:]
    copies = start_weights(meta[0], False, own, parts, full, sems)
    slots = full.shape[0]
    step = 64

    def slot_step(slot, carry):
        pre[...] = nn(quant[...], full[slot])

        def row_step(index, carry):
            at = pl.ds(pl.multiple_of(index * step, step), step)
            values = pre[at, :]
            cdf = 0.5 * (1.0 + lax.erf(values * 0.7071067811865476))
            act = values * cdf
            if student:
                level = clips_ref[3]
                inverse = 1.0 / level
                ratio = act * inverse
                tangent = jnp.tanh(ratio)
                act_out[slot, at, :] = (level * tangent).astype(BF)
                slope = 1.0 - tangent * tangent
                density = jnp.exp(-0.5 * values * values) * 0.3989422804014327
                slope_out[slot, at, :] = (slope * (cdf + values * density)).astype(BF)
                clip_out[slot, at, :] = (tangent - ratio * slope).astype(BF)
            else:
                act_out[slot, at, :] = act.astype(BF)
            return carry

        lax.fori_loop(0, SEQ // step, row_step, 0)
        if student:
            act_t_out[slot] = act_out[slot].T
        return carry

    over_slots(copies, slots, slot_step)


def output_forward(student, meta, *refs):
    act, gain, bias = refs[:3]
    own = (refs[3],)
    parts = refs[4:8]
    if student:
        pre, t_result, grad_a, grad_b = refs[8:12]
        full, own_out, partner_out, grad_out, low_out, sums_out = refs[12:18]
        acc, sems = refs[18:]
    else:
        (first_in,) = refs[8:9]
        (result_out,) = refs[9:10]
        full, acc, sems = refs[10:]
    copies = start_weights(meta[0], False, own, parts, full, sems)
    if student:

        def first(at):
            acc[at, :] = normalize(pre[at, :])[0] * gain[0:1, :] + bias[0:1, :]

        by_rows(SEQ, first)
    else:
        acc[...] = first_in[...]

    def slot_step(slot, carry):
        acc[...] += nn(act[slot], full[slot])
        return carry

    over_slots(copies, full.shape[0], slot_step)
    if not student:

        def result(at):
            result_out[at, :] = normalize(acc[at, :])[0] * gain[1:2, :] + bias[1:2, :]

        by_rows(SEQ, result)
        return
    half = grad_b.shape[0]
    sums_out[...] = jnp.zeros_like(sums_out)
    for index in range(2):

        def last(at, index=index):
            to = pl.ds(pl.multiple_of(at.start + index * half, ROWS), ROWS)
            normed, inv_std = normalize(acc[to, :])
            result = normed * gain[1:2, :] + bias[1:2, :]
            if index == 0:
                own_out[at, :] = result.astype(BF)
                cotangent = grad_a[meta[1], at, :]
            else:
                partner_out[at, :] = result.astype(BF)
                cotangent = grad_b[at, :]
            grad_result = cotangent.astype(F32) + result - t_result[to, :]
            sums_out[S_GAIN + 1 : S_GAIN + 2, :] += colsum(grad_result * normed)
            sums_out[S_BIAS + 1 : S_BIAS + 2, :] += colsum(grad_result)
            grad_pre = norm_back(grad_result, normed, inv_std, gain[1:2, :])
            grad_out[to, :] = grad_pre
            low_out[to, :] = grad_pre.astype(BF)

        by_rows(half, last)


def weight_grad(meta, left_t, right, keep_ref, send_ref, acc):
    def slot_step(slot, carry):
        left = left_t[slot] if len(left_t.shape) == 3 else left_t[...]
        rows = right[slot] if len(right.shape) == 3 else right[...]
        acc[...] = nn(left, rows)
        there = jnp.where(slot == 0, 0, crosswise(meta[0] & BIT_C, slot))
        store_pieces(meta[0], acc, keep_ref, send_ref, slot, there)
        return carry

    lax.fori_loop(0, keep_ref.shape[1], slot_step, 0)


def hidden_back(grad_low, full, slope, clip, sums, grad_out, sums_out):
    sums_out[...] = sums[...]

    def slot_step(slot, carry):
        grad = nt(grad_low[...], full[slot])
        grad_out[slot] = (grad * slope[slot].astype(F32)).astype(BF)
        sums_out[S_CLIP + 3 : S_CLIP + 4, :] += colsum(grad * clip[slot].astype(F32))
        return carry

    lax.fori_loop(0, full.shape[0], slot_step, 0)


def first_back(
    clips_ref, grad_hidden, full, pre, gain, bias, grad_two, sums, grad_out, low_out, sums_out, acc
):
    acc[...] = jnp.zeros_like(acc)

    def slot_step(slot, carry):
        acc[...] += nt(grad_hidden[slot], full[slot])
        return carry

    lax.fori_loop(0, full.shape[0], slot_step, 0)
    sums_out[...] = sums[...]
    level = clips_ref[2]

    def last(at):
        normed, inv_std = normalize(pre[at, :])
        ratio = (normed * gain[0:1, :] + bias[0:1, :]) / level
        tangent = jnp.tanh(ratio)
        slope = 1.0 - tangent * tangent
        grad_fq = acc[at, :]
        sums_out[S_CLIP + 2 : S_CLIP + 3, :] += colsum(grad_fq * (tangent - ratio * slope))
        upstream = grad_fq * slope + grad_two[at, :]
        sums_out[S_GAIN : S_GAIN + 1, :] += colsum(upstream * normed)
        sums_out[S_BIAS : S_BIAS + 1, :] += colsum(upstream)
        grad_pre = norm_back(upstream, normed, inv_std, gain[0:1, :])
        grad_out[at, :] = grad_pre
        low_out[at, :] = grad_pre.astype(BF)

    by_rows(SEQ, last)


def attend_back(slot, first, last, meta, clips_ref, *refs):
    segments, qkv, t_qkv, lse, ctx, low, xq, full, sums = refs[:9]
    rest = list(refs[9:])
    grad_in = None if first else rest.pop(0)
    if last:
        grad_one, xa, xb = rest[:3]
        rest = rest[3:]
    keep_ref, send_ref, sums_out = rest[:3]
    rest = rest[3:]
    if last:
        own_out, partner_out = rest[:2]
        rest = rest[2:]
    else:
        grad_out = rest.pop(0)
    mask_bias, mask_scale, grad_qkv, acc = rest
    same = same_segment(meta, segments)
    mask_bias[...] = jnp.where(same, 0.0, NEG)
    mask_scale[...] = jnp.where(same, 1.0 / SEQ, 0.0)
    width = ctx.shape[-1]
    heads = width // HD
    level = clips_ref[1]
    context = ctx[slot]
    ratio = context / level
    tangent = jnp.tanh(ratio)
    slope = 1.0 - tangent * tangent
    grad_cq = nt(low[...], full[slot, 3 * width :, :])
    sums_out[...] = sums[...]
    at_slot = slice(slot * width, (slot + 1) * width)
    clip_cols = colsum(grad_cq * (tangent - ratio * slope))
    sums_out[S_CLIP + 1 : S_CLIP + 2, at_slot] = clip_cols
    grad_ctx = (grad_cq * slope).astype(BF)
    acc[3 * width :, :] = nn((level * tangent).astype(BF).T, low[...])
    for head in range(heads):
        lo = head * HD
        queries = qkv[slot, :, lo : lo + HD] * BF(0.125)
        key_rows = qkv[slot, :, width + lo : width + lo + HD]
        value_rows = qkv[slot, :, 2 * width + lo : 2 * width + lo + HD]
        t_queries = t_qkv[slot, :, lo : lo + HD] * BF(0.125)
        t_keys = t_qkv[slot, :, width + lo : width + lo + HD]
        grad_keys = grad_values = 0.0
        for at in range(0, SEQ, Q_BLOCK):
            to = slice(at, at + Q_BLOCK)
            upstream = grad_ctx[to, lo : lo + HD]
            scores = nt(key_rows, queries[to])
            probs = jnp.exp(scores + mask_bias[:, to] - lse[slot, head : head + 1, to])
            grad_probs = nt(value_rows, upstream)
            grad_values = grad_values + nn(probs.astype(BF), upstream)
            row_sum = jnp.sum(probs * grad_probs, axis=0, keepdims=True)
            gap = scores - nt(t_keys, t_queries[to])
            grad_scores = (probs * (grad_probs - row_sum) + gap * mask_scale[:, to]).astype(BF)
            grad_keys = grad_keys + nn(grad_scores, queries[to])
            grad_queries = tn(key_rows, grad_scores).T * 0.125
            grad_qkv[to, lo : lo + HD] = grad_queries.astype(BF)
        grad_qkv[:, width + lo : width + lo + HD] = grad_keys.astype(BF)
        grad_qkv[:, 2 * width + lo : 2 * width + lo + HD] = grad_values.astype(BF)
    acc[: 3 * width, :] = nn(grad_qkv[...].T, xq[...])
    store_pieces(meta[0], acc, keep_ref, send_ref, 0, 0)
    grad_xq = nn(grad_qkv[...], full[slot, : 3 * width, :])
    if not first:
        grad_xq = grad_xq + grad_in[...]
    if not last:
        grad_out[...] = grad_xq
        return
    acc[:SEQ, :] = grad_xq
    half = xb.shape[0]
    level = clips_ref[0]
    for index in range(2):

        def finish_rows(at, index=index):
            to = pl.ds(pl.multiple_of(at.start + index * half, ROWS), ROWS)
            values = xa[meta[1], at, :] if index == 0 else xb[at, :]
            ratio = values.astype(F32) / level
            tangent = jnp.tanh(ratio)
            slope = 1.0 - tangent * tangent
            grad = acc[to, :]
            sums_out[S_CLIP : S_CLIP + 1, :] += colsum(grad * (tangent - ratio * slope))
            total = grad * slope + grad_one[to, :]
            if index == 0:
                own_out[at, :] = total
            else:
                partner_out[at, :] = total.astype(BF)

        by_rows(half, finish_rows)


def finish(attn, meta, own, other, sums, levels, *refs):
    count = own.shape[1]
    latents, outs, scales = refs[:count], refs[count:-1], refs[-1]
    place = meta[0]
    core = place & BIT_C
    bit_one = BIT_X + core * (BIT_Y - BIT_X)
    bit_two = BIT_X + BIT_Y - bit_one
    both = BIT_X | BIT_Y
    first, lines, entries = (0, 4, D * D) if attn else (4, 2, D * FF)
    for j in range(first, first + lines):
        total = jnp.sum(sums[j : j + 1, :], axis=1, keepdims=True)
        scales[j : j + 1, :] = total / (levels[j : j + 1, :] * entries)
    if not attn:
        gain_out, bias_out, clip_out = outs[2:5]
        gain_out[...] = sums[S_GAIN : S_GAIN + 2, :]
        bias_out[...] = sums[S_BIAS : S_BIAS + 2, :]
        clip_out[...] = jnp.broadcast_to(
            jnp.sum(sums[S_CLIP : S_CLIP + 4, :], axis=1, keepdims=True), clip_out.shape
        )
    for source, flips in (
        (own, (0, bit_one, bit_two, both)),
        (other, (BIT_C, BIT_C | bit_two, BIT_C | bit_one, BIT_C | both)),
    ):
        for unit, flip in enumerate(flips):
            piece = place ^ flip
            at = pl.ds(pl.multiple_of(piece * PIECE, PIECE), PIECE)
            for index in range(count):
                scale = scales[pl.ds(piece // 2, 1), :] if attn else scales[4 + index : 5 + index, :]
                values = source[unit, index].astype(F32) + scale * latents[index][at, :].astype(F32)
                if not attn:
                    outs[index][at, :] = values
                    continue
                in_qkv = piece < ATTN_QKV // PIECE

                @pl.when(in_qkv)
                def _(at=at, values=values):
                    outs[0][at, :] = values

                @pl.when(jnp.logical_not(in_qkv))
                def _(piece=piece, values=values):
                    row = pl.multiple_of(piece * PIECE - ATTN_QKV, PIECE)
                    outs[1][pl.ds(row, PIECE), :] = values


VM = pl.BlockSpec(memory_space=pltpu.VMEM)
SM = pl.BlockSpec(memory_space=pltpu.SMEM)
HBM = pl.BlockSpec(memory_space=pltpu.HBM)
DMA_SEMS = pltpu.SemaphoreType.DMA((N_COPIES,))


def shape(dims, dtype):
    return jax.ShapeDtypeStruct(dims, dtype)


def call(name, body, args, specs, outs, scratch, flops, out_specs=None, limit=VMEM_WIDE):
    total = sum(a.size * a.dtype.itemsize for a in args) + sum(
        o.size * o.dtype.itemsize for o in outs
    )
    return pl.pallas_call(
        body,
        name=name,
        in_specs=specs,
        out_specs=out_specs or [VM] * len(outs),
        out_shape=outs,
        scratch_shapes=scratch,
        compiler_params=pltpu.CompilerParams(vmem_limit_bytes=limit),
        cost_estimate=pl.CostEstimate(flops=flops, bytes_accessed=total, transcendentals=0),
    )(*args)


def swap(array, axis, size, bit):
    return lax.ppermute(array, axis, [(i, i ^ bit) for i in range(size)])


def swap_by_core(array, dp, bit_zero, bit_one):
    pairs = [(i, i ^ (bit_one if i & BIT_C else bit_zero)) for i in range(dp)]
    return lax.ppermute(array, "dp", pairs)


def near(array, dp):
    return swap_by_core(array, dp, BIT_X, BIT_Y)


def far(array, dp):
    return swap_by_core(array, dp, BIT_Y, BIT_X)


def cross(array, dp):
    return swap(array, "dp", dp, BIT_C)


def line(array, dp, n, bit_zero, bit_one):
    pairs = []
    for i in range(dp):
        for j in range(n):
            pairs.append((i * n + j, i * n + (j ^ (bit_one if i & BIT_C else bit_zero))))
    return lax.ppermute(array, ("dp", "head"), pairs)


def line_one(array, dp, n):
    return line(array, dp, n, 1, 3)


def line_two(array, dp, n):
    return line(array, dp, n, 2, 1)


class Line:
    def __init__(self, piece, dp, n):
        self.piece, self.dp, self.n = piece[None], dp, n
        self.flying = None
        self.stage = 0

    def land(self):
        stage, got = self.stage, self.flying
        self.stage += 1
        if stage == 0:
            self.flying = (line_one(self.piece, self.dp, self.n),)
        elif stage == 1:
            self.one = got[0]
            self.both = jnp.concatenate([self.piece, got[0]])
            self.flying = (line_two(self.both, self.dp, self.n),)
        else:
            self.flying = None
            remote = [self.one[0], got[0][0], got[0][1]]
            count = self.piece.shape[1]
            self.remote = [
                jnp.concatenate([r[index] for r in remote], axis=0) for index in range(count)
            ]


class Plane:
    def __init__(self, remote, dp):
        self.remote, self.dp = remote, dp
        self.flying = None
        self.stage = 0

    def land(self):
        dp, stage, got = self.dp, self.stage, self.flying
        self.stage += 1
        if stage == 0:
            self.flying = (near(self.remote, dp),)
        elif stage == 1:
            self.pair = jnp.concatenate([self.remote, got[0]])
            self.flying = (far(self.pair, dp), cross(self.pair, dp))
        elif stage == 2:
            self.pair_far, self.crossed = got
            self.flying = (cross(self.pair_far, dp),)
        else:
            self.parts = (self.pair, self.pair_far, self.crossed, got[0])
            self.flying = None


class Reduce:
    def __init__(self, keeps, sends, dp, n, mode):
        self.keeps, self.sends, self.dp, self.n, self.mode = keeps, sends, dp, n, mode
        self.flying = None
        self.stage = 0
        self.extra = None

    def land(self):
        dp, n, stage = self.dp, self.n, self.stage
        self.stage += 1
        got = self.flying
        if stage == 0:
            self.flying = tuple(cross(send, dp) for send in self.sends)
        elif stage == 1:
            totals = [k.astype(F32) + g.astype(F32) for k, g in zip(self.keeps, got)]
            self.total = totals[0] if len(totals) == 1 else jnp.concatenate(totals, axis=1)
            self.flying = (near(self.total[2:].astype(BF), dp),)
        elif stage == 2:
            self.total = self.total[:2] + got[0].astype(F32)
            self.flying = (far(self.total[1].astype(BF), dp),)
        elif stage == 3:
            self.total = self.total[0] + got[0].astype(F32)
            if self.mode == "whole":
                self.flying = (line_two(self.total[2:].astype(BF), dp, n),)
            elif self.mode == "sent":
                self.flying = (swap(self.total.astype(BF), "head", n, 2),)
            else:
                self.flying = self.extra
        elif stage == 4:
            if self.mode == "sent":
                self.flying = None
                self.result = got[0]
                return
            held = self.total[:2] if self.mode == "whole" else self.total
            self.total = held + got[0].astype(F32)
            out = self.total[1].astype(BF)
            self.flying = (
                line_one(out, dp, n) if self.mode == "whole" else swap(out, "head", n, 1),
            )
        elif stage == 5:
            mine = self.total[0] + got[0].astype(F32)
            bit = GROUP
            while bit < dp:
                mine = mine + swap(mine.astype(BF), "dp", dp, bit).astype(F32)
                bit *= 2
            self.result = mine
            self.flying = None


class Share:
    def __init__(self, piece, dp):
        self.piece, self.dp = piece[None], dp
        self.flying = None
        self.stage = 0

    def land(self):
        dp, stage = self.dp, self.stage
        self.stage += 1
        got = self.flying
        if stage == 0:
            self.flying = (near(self.piece, dp),)
        elif stage == 1:
            self.pair = jnp.concatenate([self.piece, got[0]])
            self.flying = (far(self.pair, dp),)
        elif stage == 2:
            self.quad = jnp.concatenate([self.pair, got[0]])
            self.flying = (cross(self.quad, dp),)
        elif stage == 3:
            self.result = (self.quad, got[0])
            self.flying = None


class Sum:
    def __init__(self, values, steps):
        self.values = values
        self.steps = steps
        self.flying = None
        self.stage = 0

    def land(self):
        got, values = self.flying, self.values
        if got is not None:
            self.values = values + got[0] if len(got) == 1 else (values + got[0]) + (got[1] + got[2])
        if self.stage < len(self.steps):
            axis, size, bits = self.steps[self.stage]
            flips = bits if len(bits) == 1 else (bits[0], bits[1], bits[0] | bits[1])
            self.flying = tuple(swap(self.values, axis, size, flip) for flip in flips)
        else:
            self.flying = None
            self.result = self.values
        self.stage += 1


def steps_over(axis, size, bit=1):
    steps = []
    while bit < size:
        bits = (bit, 2 * bit) if 2 * bit < size else (bit,)
        steps.append((axis, size, bits))
        bit <<= len(bits)
    return steps


def beside(flights, outs):
    flights = [f for f in flights if f.flying is not None]
    tied, outs = lax.optimization_barrier((tuple(f.flying for f in flights), tuple(outs)))
    for flight, flying in zip(flights, tied):
        flight.flying = flying
    return outs


class Once:
    def __init__(self, flying):
        self.flying = (flying,)

    def land(self):
        self.result = self.flying[0]
        self.flying = None


def land(*flights):
    for flight in flights:
        flight.land()


def on_device(
    dp,
    n,
    hidden_in,
    teacher_in,
    out_grad,
    segment_ids,
    qkv_latent,
    out_latent,
    ffn_in_latent,
    ffn_out_latent,
    norm_gain,
    norm_bias,
    clips,
    teacher_qkv,
    teacher_out,
    teacher_ffn_in,
    teacher_ffn_out,
    teacher_gain,
    teacher_bias,
):
    h = lax.axis_index("head")
    place = lax.axis_index("dp") % GROUP
    parity = h % MICRO
    half = hidden_in.shape[1]
    width = qkv_latent.shape[-1]
    meta = jnp.stack([place, parity, h // MICRO]).astype(jnp.int32)

    def exchange(array):
        return Once(swap(array, "head", n, 1))

    def tie(*values):
        return lax.optimization_barrier(values)

    def lines(array):
        return jnp.swapaxes(array, 1, 2).reshape(3 * width, D)

    big = pltpu.VMEM((n, D, D), BF)
    tall = pltpu.VMEM((SEQ, D), F32)
    mm = 2 * SEQ * D * D
    square, band, sheet = shape((D, D), BF), shape((PIECE, D), BF), shape((half, D), BF)
    weights = [HBM] * (1 + N_PARTS)

    t_qkv_rows, qkv_rows = lines(teacher_qkv), lines(qkv_latent)
    t_piece_attn, t_piece_in, t_piece_out, t_send, x_send, g_send = call(
        "cut",
        cut,
        (meta, t_qkv_rows, teacher_out, teacher_in, teacher_ffn_in, teacher_ffn_out, hidden_in, out_grad),
        [SM] + [HBM] * 7,
        [band] * 3 + [sheet] * 3,
        [pltpu.SemaphoreType.DMA((6,))],
        mm // 8,
    )
    z0 = Line(t_piece_attn[None], dp, n)
    land(z0)
    x_send, z0.piece = tie(x_send, z0.piece)
    x_ex = exchange(x_send)
    attn_latent, squares = call(
        "sum_squares",
        sum_squares,
        (qkv_rows, out_latent, ffn_in_latent, ffn_out_latent),
        [VM] * 4,
        [square, shape((8, D), F32)],
        [],
        mm,
    )
    latents = [attn_latent, ffn_in_latent, ffn_out_latent]
    total = Sum(squares, steps_over("head", n))
    land(total)
    land(z0)
    land(total)
    t_piece_in, z0.both = tie(t_piece_in, z0.both)
    z1 = Line(t_piece_in[None], dp, n)
    land(z1)
    results = beside(
        (z0, x_ex),
        call(
            "binarize",
            binarize,
            (meta, total.result) + tuple(latents),
            [SM] + [VM] * 4,
            [square] * 3 + [band] * 3 + [shape((8, D), F32)],
            [],
            mm,
        ),
    )
    bins, s_pieces, levels = results[:3], results[3:6], results[6]
    land(z0, x_ex)
    t_send, z0.remote[0] = tie(t_send, z0.remote[0])
    t_ex = exchange(t_send)
    p0 = Plane(z0.remote[0], dp)
    land(p0)
    land(z1)
    piece, p0.remote = tie(s_pieces[0], p0.remote)
    z2 = Line(piece[None], dp, n)
    land(z2)
    land(p0)
    land(z1)
    p1 = Plane(z1.remote[0], dp)
    land(p1)
    land(z2)
    t_piece_out, z2.both = tie(t_piece_out, z2.both)
    z3 = Line(t_piece_out[None], dp, n)
    land(z3)
    t_ex.flying, p0.flying = tie(t_ex.flying, p0.flying)
    land(t_ex)
    land(p0)
    land(p1)
    land(z2)
    p2 = Plane(z2.remote[0], dp)
    land(p2)
    land(z3)
    pieces_in, pieces_out, p2.remote = tie(s_pieces[1], s_pieces[2], p2.remote)
    z45 = Line(jnp.stack([pieces_in, pieces_out]), dp, n)
    land(z45)
    land(p0)

    attn_scratch = [
        pltpu.VMEM((SEQ, SEQ), F32),
        tall,
        pltpu.VMEM((width, SEQ), F32),
        DMA_SEMS,
    ]
    t_qkv, t_first, t_first_low = beside(
        (p1, p2, z3, z45),
        call(
            "teacher_attend",
            functools.partial(attend_forward, False),
            (meta, clips, teacher_in, t_ex.result, segment_ids, teacher_gain, teacher_bias, t_qkv_rows, teacher_out)
            + p0.parts,
            [SM, SM] + [VM] * 5 + [HBM] + weights,
            [shape((n, SEQ, 3 * width), BF), shape((SEQ, D), F32), shape((SEQ, D), BF)],
            [big, pltpu.VMEM((SEQ, D), BF)] + attn_scratch,
            8 * mm,
        ),
    )
    land(p1, p2, z3, z45)
    p3 = Plane(z3.remote[0], dp)
    land(p3, p1)
    (t_act,) = beside(
        (p2, p3, z45),
        call(
            "teacher_hidden",
            functools.partial(hidden_forward, False),
            (meta, clips, t_first_low, teacher_ffn_in) + p1.parts,
            [SM, SM, VM] + weights,
            [shape((n, SEQ, D), BF)],
            [big, tall, DMA_SEMS],
            6 * mm,
        ),
    )
    land(p2, p3, z45)
    p4, p5 = Plane(z45.remote[0], dp), Plane(z45.remote[1], dp)
    land(p4, p2)
    g_send, t_act = tie(g_send, t_act)
    g_ex = exchange(g_send)
    full_attn, qkv, lse, ctx, pre_one, quant, quant_t, xq = beside(
        (p3, p4, g_ex),
        call(
            "student_attend",
            functools.partial(attend_forward, True),
            (meta, clips, hidden_in, x_ex.result, segment_ids, norm_gain, norm_bias, bins[0])
            + p2.parts,
            [SM, SM] + [VM] * 5 + weights,
            [
                shape((n, D, D), BF),
                shape((n, SEQ, 3 * width), BF),
                shape((n, 8, SEQ), F32),
                shape((n, SEQ, width), F32),
                shape((SEQ, D), F32),
                shape((SEQ, D), BF),
                shape((D, SEQ), BF),
                shape((SEQ, D), BF),
            ],
            attn_scratch,
            8 * mm,
        ),
    )
    land(p3, p4, g_ex)
    p5.remote, quant = tie(p5.remote, quant)
    land(p5, p3)
    (t_result,) = beside(
        (p4, p5),
        call(
            "teacher_output",
            functools.partial(output_forward, False),
            (meta, t_act, teacher_gain, teacher_bias, teacher_ffn_out) + p3.parts + (t_first,),
            [SM] + [VM] * 3 + weights + [VM],
            [shape((SEQ, D), F32)],
            [big, tall, DMA_SEMS],
            4 * mm,
        ),
    )
    land(p4, p5, p4)
    full_in, act, act_t, slope, clip_term = beside(
        (p5,),
        call(
            "student_hidden",
            functools.partial(hidden_forward, True),
            (meta, clips, quant, bins[1]) + p4.parts,
            [SM, SM, VM] + weights,
            [
                shape((n, D, D), BF),
                shape((n, SEQ, D), BF),
                shape((n, D, SEQ), BF),
                shape((n, SEQ, D), BF),
                shape((n, SEQ, D), BF),
            ],
            [tall, DMA_SEMS],
            8 * mm,
        ),
    )
    land(p5, p5)
    full_out, out_own, out_far, grad_two, low_two, sums = call(
        "student_output",
        functools.partial(output_forward, True),
        (meta, act, norm_gain, norm_bias, bins[2]) + p5.parts + (pre_one, t_result, out_grad, g_ex.result),
        [SM] + [VM] * 3 + weights + [VM] * 4,
        [
            shape((n, D, D), BF),
            shape((half, D), BF),
            shape((half, D), BF),
            shape((SEQ, D), F32),
            shape((SEQ, D), BF),
            shape((S_ROWS, D), F32),
        ],
        [tall, DMA_SEMS],
        4 * mm,
    )

    def grad_call(name, left_t, right):
        return call(
            name,
            weight_grad,
            (meta, left_t, right),
            [SM, VM, VM],
            [shape((GROUP // 2, n, PIECE, D), BF)] * 2,
            [pltpu.VMEM((D, D), F32)],
            4 * mm,
            limit=VMEM_SMALL,
        )

    sums_shape = shape((S_ROWS, D), F32)
    out_ex = exchange(out_far)
    keep, send = grad_call("ffn_out_weight", act_t, low_two)
    r_out = Reduce([keep], [send], dp, n, "whole")
    land(r_out)
    grad_hidden, sums = beside(
        (r_out,),
        call(
            "hidden_back",
            hidden_back,
            (low_two, full_out, slope, clip_term, sums),
            [VM] * 5,
            [shape((n, SEQ, D), BF), sums_shape],
            [],
            5 * mm,
            limit=VMEM_SMALL,
        ),
    )
    land(r_out)
    keep, send = grad_call("ffn_in_weight", quant_t, grad_hidden)
    r_in = Reduce([keep], [send], dp, n, "whole")
    land(r_in)
    grad_one, low_one, sums = beside(
        (r_in, r_out, out_ex),
        call(
            "first_back",
            first_back,
            (clips, grad_hidden, full_in, pre_one, norm_gain, norm_bias, grad_two, sums),
            [SM] + [VM] * 7,
            [shape((SEQ, D), F32), shape((SEQ, D), BF), sums_shape],
            [tall],
            4 * mm,
            limit=VMEM_SMALL,
        ),
    )

    def attend_back_slot(slot, grad_xq, sums):
        first, last = slot == 2, slot == 1
        args = [meta, clips, segment_ids, qkv, t_qkv, lse, ctx, low_one, xq, full_attn, sums]
        outs = [shape((GROUP // 2, 1, PIECE, D), BF)] * 2 + [sums_shape]
        if not first:
            args.append(grad_xq)
        if last:
            args += [grad_one, hidden_in, x_ex.result]
            outs += [shape((half, D), F32), shape((half, D), BF)]
        else:
            outs += [shape((SEQ, D), F32)]
        return call(
            "attend_back",
            functools.partial(attend_back, slot, first, last),
            args,
            [SM, SM] + [VM] * (len(args) - 2),
            outs,
            [
                pltpu.VMEM((SEQ, SEQ), F32),
                pltpu.VMEM((SEQ, SEQ), F32),
                pltpu.VMEM((SEQ, 3 * width), BF),
                pltpu.VMEM((D, D), F32),
            ],
            5 * mm,
            limit=VMEM_SMALL,
        )

    land(r_out, r_in, out_ex)
    keep_2, send_2, sums, grad_xq = beside((r_out,), attend_back_slot(2, None, sums))
    land(r_out)
    keep_3, send_3, sums, grad_xq = beside((r_out,), attend_back_slot(3, grad_xq, sums))
    r_sent = Reduce([keep_2, keep_3], [send_2, send_3], dp, n, "sent")
    land(r_sent, r_out)
    keep_0, send_0, sums, grad_xq = beside((r_in, r_sent), attend_back_slot(0, grad_xq, sums))
    land(r_in, r_sent)
    keep_1, send_1, sums, in_grad_own, in_grad_far = beside(
        (r_in, r_sent, r_out), attend_back_slot(1, grad_xq, sums)
    )
    def both(own, far):
        first_row = jnp.where(parity == 0, own, far)
        second_row = jnp.where(parity == 0, far, own)
        return jnp.stack([first_row, second_row])

    r_kept = Reduce([keep_0, keep_1], [send_0, send_1], dp, n, "kept")
    land(r_kept)
    land(r_in, r_out)
    land(r_sent)
    land(r_kept)
    land(r_in)
    land(r_sent)
    repeats = dp // GROUP

    def settled(name, attn, pieces, latent_list, sums):
        count = len(pieces)
        return call(
            name,
            functools.partial(settle, attn, repeats),
            (meta, levels, sums) + tuple(pieces) + tuple(latent_list),
            [SM] + [VM] * (2 + 2 * count),
            [shape((count, PIECE, D), BF), sums_shape],
            [],
            mm // 4,
            limit=VMEM_SMALL,
        )

    land(r_in)
    direct_ffn, sums = settled("settle_hidden", False, [r_in.result, r_out.result], latents[1:], sums)
    land(r_kept)
    s_ffn = Share(direct_ffn, dp)
    land(s_ffn)
    land(r_sent)
    r_kept.extra = (r_sent.result,)
    land(r_kept, r_kept)
    land(s_ffn)
    in_grad_far, s_ffn.pair = tie(in_grad_far, s_ffn.pair)
    in_ex = exchange(in_grad_far)
    out_all = both(out_own, out_ex.result)
    (out_all,) = beside((r_kept,), (out_all,))
    land(r_kept)
    direct_attn, sums = settled("settle_attention", True, [r_kept.result], latents[:1], sums)
    s_attn = Share(direct_attn, dp)
    total = Sum(sums, [("dp", dp, (BIT_C,))] + steps_over("dp", dp, BIT_X) + steps_over("head", n))
    land(s_attn, total)
    land(total, s_ffn)
    land(s_attn)
    land(total)
    in_ex.flying, total.values = tie(in_ex.flying, total.values)
    land(in_ex)
    in_grad_all = both(in_grad_own, in_ex.result.astype(F32))
    (in_grad_all,) = beside((s_attn, total), (in_grad_all,))
    land(s_attn)
    while total.flying is not None:
        land(total)
    land(s_attn, s_ffn)
    sums = total.result
    in_grad, out_grad_w, gain_grad, bias_grad, clip_sums = call(
        "finish_hidden",
        functools.partial(finish, False),
        (meta,) + s_ffn.result + (sums, levels, latents[1], latents[2]),
        [SM] + [VM] * 6,
        [shape((D, D), F32)] * 2 + [shape((2, D), F32)] * 2 + [shape((4, 128), F32)],
        [pltpu.VMEM((8, D), F32)],
        mm // 4,
        limit=VMEM_SMALL,
    )
    qkv_grad, attn_out_grad = call(
        "finish_attention",
        functools.partial(finish, True),
        (meta,) + s_attn.result + (sums, levels, latents[0]),
        [SM] + [VM] * 5,
        [shape((ATTN_QKV, D), F32), shape((width, D), F32)],
        [pltpu.VMEM((8, D), F32)],
        mm // 4,
        limit=VMEM_SMALL,
    )
    qkv_grad = jnp.swapaxes(qkv_grad.reshape(3, width, D), 1, 2)
    clip_grad = clip_sums[:, 0]

    return (
        out_all,
        in_grad_all,
        qkv_grad,
        attn_out_grad,
        in_grad,
        out_grad_w,
        gain_grad,
        bias_grad,
        clip_grad,
    )


def solution(mesh):
    placed = (
        P(None, ("dp", "head"), None),
        P(None, ("dp", "head"), None),
        P(None, ("dp", "head"), None),
        P(None, "dp", None),
        P(None, None, "head"),
        P("head", None),
        P(None, "head"),
        P("head", None),
        P(),
        P(),
        P(),
        P(None, None, "head"),
        P("head", None),
        P(None, "head"),
        P("head", None),
        P(),
        P(),
    )
    return jax.shard_map(
        functools.partial(on_device, mesh.shape["dp"], mesh.shape["head"]),
        mesh=mesh,
        in_specs=placed,
        out_specs=(
            P(None, ("dp", "head"), None),
            P(None, ("dp", "head"), None),
            P(None, None, "head"),
            P("head", None),
            P(None, "head"),
            P("head", None),
            P(),
            P(),
            P(),
        ),
        check_vma=False,
    )
```

```python
import functools

import jax
import jax.numpy as jnp
from jax import lax
from jax.experimental import pallas as pl
from jax.experimental.pallas import tpu as pltpu
from jax.sharding import PartitionSpec as P

D = 768
HD = 64
FF = 3072
SEQ = 512
MICRO = 2
GROUP = 8
PIECE = D // GROUP
BIT_C, BIT_X, BIT_Y = 1, 2, 4
NEG = -1000000000.0
BF = jnp.bfloat16
F32 = jnp.float32
VMEM_WIDE = 56 * 1024 * 1024
VMEM_SMALL = 20 * 1024 * 1024
VMEM_MIDDLE = 32 * 1024 * 1024

def nn(a, b):
    return lax.dot_general(a, b, (((1,), (0,)), ((), ())), preferred_element_type=F32)


def nt(a, b):
    return lax.dot_general(a, b, (((1,), (1,)), ((), ())), preferred_element_type=F32)


def tn(a, b):
    return lax.dot_general(a, b, (((0,), (0,)), ((), ())), preferred_element_type=F32)


def normalize(values):
    centred = values - jnp.mean(values, axis=-1, keepdims=True)
    inv_std = lax.rsqrt(jnp.mean(centred * centred, axis=-1, keepdims=True) + 1e-06)
    return centred * inv_std, inv_std


def norm_back(upstream, normed, inv_std, gain_vec):
    scaled = upstream * gain_vec
    centred_grad = (
        scaled
        - jnp.mean(scaled, axis=-1, keepdims=True)
        - normed * jnp.mean(scaled * normed, axis=-1, keepdims=True)
    )
    return centred_grad * inv_std


def colsum(values):
    return jnp.sum(values, axis=0, keepdims=True)


def crosswise(core, slot):
    return (slot + core) % 3 + 1


def xor_of(core, slot):
    return (1 - core) * slot + core * ((slot + 1) % 3 + 1)


class Weights:
    def __init__(self, place, by_xor, own, parts, full, sems, out=None):
        core = place & BIT_C
        bit_one = BIT_X + core * (BIT_Y - BIT_X)
        bit_two = BIT_X + BIT_Y - bit_one
        both = BIT_X | BIT_Y
        self.pairs = []
        row = 0
        for array in own:
            self.pairs.append((array, full.at[0, pl.ds(row, array.shape[0])]))
            row += array.shape[0]
        self.owned = len(own)
        flips = (
            (0, bit_one),
            (bit_two, both),
            (BIT_C, BIT_C | bit_two),
            (BIT_C | bit_one, BIT_C | both),
        )
        for source, part in enumerate(parts):
            for unit in range(2):
                row = pl.multiple_of((place ^ flips[source][unit]) * PIECE, PIECE)
                for slot in range(1, N_SLOTS):
                    if by_xor:
                        to = xor_of(core if source < 2 else 1 - core, slot)
                    else:
                        to = slot if source < 2 else crosswise(1 - core, slot)
                    start = (unit * (N_SLOTS - 1) + slot - 1) * PIECE
                    self.pairs.append(
                        (part.at[pl.ds(start, PIECE)], full.at[to, pl.ds(row, PIECE)])
                    )
        self.sems, self.full, self.out = sems, full, out

    def copies(self):
        return [
            pltpu.make_async_copy(source, target, self.sems.at[index])
            for index, (source, target) in enumerate(self.pairs)
        ]

    def start(self):
        for copy in self.copies():
            copy.start()

    def wait(self, slot):
        @pl.when(slot == 0)
        def _():
            for copy in self.copies()[: self.owned]:
                copy.wait()

        @pl.when(slot == 1)
        def _():
            for copy in self.copies()[self.owned :]:
                copy.wait()
            if self.out is not None:
                self.whole().start()

    def whole(self):
        return pltpu.make_async_copy(self.full, self.out, self.sems.at[N_COPIES])

    def end(self):
        if self.out is not None:
            self.whole().wait()


N_SLOTS = 4
N_PARTS = 4
N_COPIES = 2 + N_PARTS * 2 * (N_SLOTS - 1)


def store_pieces(place, acc, keep_ref, send_ref):
    core = place & BIT_C
    bit_one = BIT_X + core * (BIT_Y - BIT_X)
    bit_two = BIT_X + BIT_Y - bit_one
    both = BIT_X | BIT_Y
    for index, flip in enumerate((0, bit_two, bit_one, both)):
        row = pl.multiple_of((place ^ flip) * PIECE, PIECE)
        keep_ref[index, 0] = acc[pl.ds(row, PIECE), :].astype(BF)
    for index, flip in enumerate((0, bit_one, bit_two, both)):
        row = pl.multiple_of((place ^ BIT_C ^ flip) * PIECE, PIECE)
        send_ref[index, 0] = acc[pl.ds(row, PIECE), :].astype(BF)


ATTN_QKV = 3 * D // 4


def cut_first(meta, t_qkv, t_out, t_ffn_in, attn_piece, in_piece, sems):
    place = meta[0]
    rows = pl.ds(pl.multiple_of(place * PIECE, PIECE), PIECE)
    other = pltpu.make_async_copy(t_ffn_in.at[rows], in_piece, sems.at[1])
    other.start()
    in_qkv = place < ATTN_QKV // PIECE

    @pl.when(in_qkv)
    def _():
        copy = pltpu.make_async_copy(t_qkv.at[rows], attn_piece, sems.at[0])
        copy.start()
        copy.wait()

    @pl.when(jnp.logical_not(in_qkv))
    def _():
        at = pl.ds(pl.multiple_of(place * PIECE - ATTN_QKV, PIECE), PIECE)
        copy = pltpu.make_async_copy(t_out.at[at], attn_piece, sems.at[0])
        copy.start()
        copy.wait()

    other.wait()


def cut_rest(meta, t_in, t_ffn_out, x_in, g_in, t_send, out_piece, x_send, g_send, sems):
    rows = pl.ds(pl.multiple_of(meta[0] * PIECE, PIECE), PIECE)
    there = 1 - meta[1]
    pairs = (
        (t_in.at[there], t_send),
        (t_ffn_out.at[rows], out_piece),
        (x_in.at[there], x_send),
        (g_in.at[there], g_send),
    )
    copies = [
        pltpu.make_async_copy(source, target, sems.at[index])
        for index, (source, target) in enumerate(pairs)
    ]
    for copy in copies:
        copy.start()
    for copy in copies:
        copy.wait()


def sum_squares(qkv, out, ffn_in, ffn_out, attn, squares):
    attn[:ATTN_QKV, :] = qkv[...]
    attn[ATTN_QKV:, :] = out[...]
    squares[...] = jnp.zeros_like(squares)
    block = D // 4
    step_rows = 64
    for index, (latent, start, count) in enumerate(
        [(attn, j * block, block) for j in range(4)] + [(ffn_in, 0, D), (ffn_out, 0, D)]
    ):

        def step(i, carry, latent=latent, start=start):
            at = pl.ds(pl.multiple_of(start + i * step_rows, step_rows), step_rows)
            values = latent[at, :].astype(F32)
            return carry + jnp.sum((values * values).reshape(step_rows // 8, 8, D), axis=0)

        total = lax.fori_loop(0, count // step_rows, step, jnp.zeros((8, D), F32))
        squares[index : index + 1, :] = colsum(total)


def binarize(meta, squares, attn, ffn_in, ffn_out, *outs):
    bins, pieces, levels = outs[:3], outs[3:6], outs[6]
    entries = jnp.where(
        lax.broadcasted_iota(jnp.int32, (8, 1), 0) < 4, float(D * D), float(D * FF)
    )
    totals = jnp.sum(squares[...], axis=1, keepdims=True)
    levels[...] = jnp.broadcast_to(jnp.sqrt(totals / entries + 1e-06), (8, D))
    step_rows = 64
    for index, latent in enumerate((attn, ffn_in, ffn_out)):

        def step(i, carry, index=index, latent=latent):
            at = pl.ds(pl.multiple_of(i * step_rows, step_rows), step_rows)
            line = i // (D // 4 // step_rows) if index == 0 else index + 3
            level = levels[pl.ds(line, 1), :]
            bins[index][at, :] = (level * jnp.tanh(latent[at, :].astype(F32) * (2.0 / level))).astype(BF)
            return carry

        lax.fori_loop(0, D // step_rows, step, 0)
        pieces[index][...] = bins[index][pl.ds(pl.multiple_of(meta[0] * PIECE, PIECE), PIECE), :]


def same_segment(meta, segments):
    own = segments[meta[1], pl.ds(meta[2], 1), :].astype(F32)
    half = SEQ // 2
    turned = jnp.concatenate([own[:, half:], own[:, :half]], axis=1)
    lanes = jnp.where(meta[1] == 0, own, turned)
    column = jnp.broadcast_to(lanes, (8, SEQ)).T[:, :1]
    return column == lanes


S_SCALE, S_GAIN, S_BIAS, S_CLIP, S_ROWS = 0, 6, 8, 10, 16


def settle(repeats, meta, levels, sums, *refs):
    grads, latents, (direct_attn, direct_ffn, sums_out) = refs[:3], refs[3:6], refs[6:]
    at = pl.ds(pl.multiple_of(meta[0] * PIECE, PIECE), PIECE)
    block = meta[0] // 2
    sums_out[...] = sums[...]
    for index in range(3):
        level = levels[pl.ds(block, 1), :] if index == 0 else levels[3 + index : 4 + index, :]
        grad = grads[index][...]
        unit = latents[index][at, :].astype(F32) * (2.0 / level)
        tangent = jnp.tanh(unit)
        slope = 1.0 - tangent * tangent
        direct = (grad * 2.0 * slope).astype(BF)
        term = colsum(grad * (tangent - unit * slope)) * (1.0 / repeats)
        if index == 0:
            direct_attn[0] = direct
            for j in range(4):
                sums_out[j : j + 1, :] = jnp.where(block == j, term, 0.0)
        else:
            direct_ffn[index - 1] = direct
            sums_out[3 + index : 4 + index, :] = term


ROWS = 256
FEW_ROWS = 32


def by_rows(count, body, rows=ROWS):
    def step(index, carry):
        body(pl.ds(pl.multiple_of(index * rows, rows), rows))
        return carry

    lax.fori_loop(0, count // rows, step, 0)


class Late:
    def __init__(self, sources, targets, sems):
        self.copies = [
            pltpu.make_async_copy(source, target, sems.at[index])
            for index, (source, target) in enumerate(zip(sources, targets))
        ]

    def start(self):
        for copy in self.copies:
            copy.start()

    def wait(self):
        for copy in self.copies:
            copy.wait()


def attend_forward(student, meta, *refs):
    clips_ref, xa, xb, segments, gain, bias = refs[:6]
    owned = 1 if student else 2
    own, refs = refs[6 : 6 + owned], refs[6 + owned :]
    parts, refs = refs[:N_PARTS], refs[N_PARTS:]
    if student:
        full_out, qkv_out, lse_out, ctx_out, pre_out, quant_out, quant_t_out, rows = refs[:8]
        refs = refs[8:]
    else:
        qkv_out, first_out, first_low_out = refs[:3]
        rows, refs = refs[3], refs[4:]
    full, rows_t, mask_bias, attn, sems = refs
    slot, slots = pl.program_id(0), full.shape[0]
    half = xb.shape[0]
    width = D // slots
    heads = width // HD

    def x_at(at, index):
        return xa[meta[1], at, :] if index == 0 else xb[at, :]

    weights = Weights(meta[0], True, own, parts, full, sems, full_out if student else None)

    @pl.when(slot == 0)
    def _():
        weights.start()
        for index in range(2):

            def quantize(at, index=index):
                to = pl.ds(pl.multiple_of(at.start + index * half, ROWS), ROWS)
                values = x_at(at, index)
                if student:
                    level = clips_ref[0]
                    values = (level * jnp.tanh(values.astype(F32) / level)).astype(BF)
                rows[to, :] = values

            by_rows(half, quantize)
        rows_t[...] = rows[...].T
        mask_bias[...] = jnp.where(same_segment(meta, segments), 0.0, NEG)
        attn[...] = jnp.zeros_like(attn)

    weights.wait(slot)
    qkv_t = nn(full[slot, : 3 * width, :], rows_t[...]).astype(BF)
    qkv_out[0] = qkv_t
    lows = []
    for head in range(heads):
        lo = head * HD
        queries = qkv_t[lo : lo + HD] * BF(0.125)
        keys = qkv_t[width + lo : width + lo + HD]
        values = qkv_t[2 * width + lo : 2 * width + lo + HD]
        scores = tn(keys, queries) + mask_bias[...]
        peak = jnp.max(scores, axis=0, keepdims=True)
        powers = jnp.exp(scores - peak)
        total = jnp.sum(powers, axis=0, keepdims=True)
        probs = (powers * (1.0 / total)).astype(BF)
        context = nn(values, probs)
        if student:
            lse_out[0, head : head + 1, :] = peak + jnp.log(total)
            ctx_out[0, lo : lo + HD, :] = context
            level = clips_ref[1]
            context = level * jnp.tanh(context / level)
        lows.append(context.astype(BF))
    attn[...] += tn(jnp.concatenate(lows, axis=0), full[slot, 3 * width :, :])

    @pl.when(slot == slots - 1)
    def _():
        for index in range(2):

            def last(at, index=index):
                to = pl.ds(pl.multiple_of(at.start + index * half, ROWS), ROWS)
                pre = x_at(at, index).astype(F32) + attn[to, :]
                first = normalize(pre)[0] * gain[0:1, :] + bias[0:1, :]
                if student:
                    pre_out[to, :] = pre
                    level = clips_ref[2]
                    quant_out[to, :] = (level * jnp.tanh(first / level)).astype(BF)
                else:
                    first_out[to, :] = first
                    first_low_out[to, :] = first.astype(BF)

            by_rows(half, last)
        if student:
            quant_t_out[...] = quant_out[...].T
        weights.end()


def hidden_forward(student, meta, clips_ref, quant, own, *refs):
    parts, refs = refs[:N_PARTS], refs[N_PARTS:]
    if student:
        full_out, act_out, act_t_out, slope_out, clip_out = refs[:5]
        refs = refs[5:]
    else:
        (act_out,), refs = refs[:1], refs[1:]
    full, pre, sems = refs
    slot, slots = pl.program_id(0), full.shape[0]
    weights = Weights(meta[0], False, (own,), parts, full, sems, full_out if student else None)

    @pl.when(slot == 0)
    def _():
        weights.start()

    weights.wait(slot)
    pre[...] = nn(quant[...], full[slot])

    def rows(at):
        values = pre[at, :]
        cdf = 0.5 * (1.0 + lax.erf(values * 0.7071067811865476))
        act = values * cdf
        if student:
            level = clips_ref[3]
            ratio = act * (1.0 / level)
            tangent = jnp.tanh(ratio)
            act_out[0, at, :] = (level * tangent).astype(BF)
            slope = 1.0 - tangent * tangent
            density = jnp.exp(values * values * -0.5) * 0.3989422804014327
            slope_out[0, at, :] = (slope * (cdf + values * density)).astype(BF)
            clip_out[0, at, :] = (tangent - ratio * slope).astype(BF)
        else:
            act_out[0, at, :] = act.astype(BF)

    by_rows(SEQ, rows, FEW_ROWS)
    if student:
        act_t_out[0] = act_out[0].T

    @pl.when(slot == slots - 1)
    def _():
        weights.end()


def output_forward(student, meta, act, gain, bias, own, *refs):
    parts, refs = refs[:N_PARTS], refs[N_PARTS:]
    if student:
        pre, t_result, grad_a, grad_b = refs[:4]
        full_out, own_out, partner_out, grad_out, low_out, sums_out = refs[4:10]
        refs = refs[10:]
    else:
        (first_in, result_out), refs = refs[:2], refs[2:]
    full, acc, sems, late_sems = refs[:4]
    held = refs[4:]
    slot, slots = pl.program_id(0), full.shape[0]
    weights = Weights(meta[0], False, (own,), parts, full, sems, full_out if student else None)

    if student:
        late = Late((pre, t_result, grad_a.at[meta[1]], grad_b), held, late_sems)
    else:
        late = Late((first_in,), held, late_sems)

    @pl.when(slot == 0)
    def _():
        weights.start()
        late.start()
        acc[...] = jnp.zeros_like(acc)

    weights.wait(slot)
    acc[...] += nn(act[0], full[slot])

    @pl.when(slot == slots - 1)
    def _():
        late.wait()
        if not student:

            def result_rows(at):
                total = held[0][at, :] + acc[at, :]
                result_out[at, :] = normalize(total)[0] * gain[1:2, :] + bias[1:2, :]

            by_rows(SEQ, result_rows)
            return
        half = held[3].shape[0]
        sums_out[...] = jnp.zeros_like(sums_out)
        for index in range(2):

            def last(at, index=index):
                to = pl.ds(pl.multiple_of(at.start + index * half, ROWS), ROWS)
                first = normalize(held[0][to, :])[0] * gain[0:1, :] + bias[0:1, :]
                normed, inv_std = normalize(first + acc[to, :])
                result = normed * gain[1:2, :] + bias[1:2, :]
                (own_out if index == 0 else partner_out)[at, :] = result.astype(BF)
                cotangent = held[2 + index][at, :].astype(F32)
                grad_result = cotangent + result - held[1][to, :]
                sums_out[S_GAIN + 1 : S_GAIN + 2, :] += colsum(grad_result * normed)
                sums_out[S_BIAS + 1 : S_BIAS + 2, :] += colsum(grad_result)
                grad_pre = norm_back(grad_result, normed, inv_std, gain[1:2, :])
                grad_out[to, :] = grad_pre
                low_out[to, :] = grad_pre.astype(BF)

            by_rows(half, last)
        weights.end()


def weight_grad(meta, left_t, right, keep_ref, send_ref, acc):
    left = left_t[0] if len(left_t.shape) == 3 else left_t[...]
    rows = right[0] if len(right.shape) == 3 else right[...]
    acc[...] = nn(left, rows)
    store_pieces(meta[0], acc, keep_ref, send_ref)


def hidden_back(meta, grad_low, full, slope, clip, sums, grad_out, sums_out):
    @pl.when(pl.program_id(0) == 0)
    def _():
        sums_out[...] = sums[...]

    grad = nt(grad_low[...], full[0])
    grad_out[0] = (grad * slope[0].astype(F32)).astype(BF)
    sums_out[S_CLIP + 3 : S_CLIP + 4, :] += colsum(grad * clip[0].astype(F32))


def first_back(
    meta, clips_ref, grad_hidden, full, pre_in, gain, bias, grad_two_in, sums, grad_out, low_out, sums_out,
    acc, pre, grad_two, sems,
):
    slot = pl.program_id(0)
    late = Late((pre_in, grad_two_in), (pre, grad_two), sems)

    @pl.when(slot == 0)
    def _():
        late.start()
        sums_out[...] = sums[...]
        acc[...] = jnp.zeros_like(acc)

    acc[...] += nt(grad_hidden[0], full[0])
    level = clips_ref[2]

    @pl.when(slot == N_SLOTS - 1)
    def _():
        late.wait()

        def last(at):
            normed, inv_std = normalize(pre[at, :])
            ratio = (normed * gain[0:1, :] + bias[0:1, :]) / level
            tangent = jnp.tanh(ratio)
            slope = 1.0 - tangent * tangent
            grad_fq = acc[at, :]
            sums_out[S_CLIP + 2 : S_CLIP + 3, :] += colsum(grad_fq * (tangent - ratio * slope))
            upstream = grad_fq * slope + grad_two[at, :]
            sums_out[S_GAIN : S_GAIN + 1, :] += colsum(upstream * normed)
            sums_out[S_BIAS : S_BIAS + 1, :] += colsum(upstream)
            grad_pre = norm_back(upstream, normed, inv_std, gain[0:1, :])
            grad_out[at, :] = grad_pre
            low_out[at, :] = grad_pre.astype(BF)

        by_rows(SEQ, last)


def attend_back(steps, first, last, meta, clips_ref, *refs):
    segments, qkv, t_qkv, lse, ctx, low, xq, full, sums = refs[:9]
    rest = list(refs[9:])
    grad_in = None if first else rest.pop(0)
    if last:
        grad_one, xa, xb = rest[:3]
        rest = rest[3:]
    keep_ref, send_ref, sums_out = rest[:3]
    rest = rest[3:]
    if last:
        own_out, partner_out = rest[:2]
        rest = rest[2:]
    else:
        grad_out = rest.pop(0)
    mask_bias, mask_scale, grad_qkv, acc, grad_acc = rest
    step = pl.program_id(0)

    @pl.when(step == 0)
    def _():
        same = same_segment(meta, segments)
        mask_bias[...] = jnp.where(same, 0.0, NEG)
        mask_scale[...] = jnp.where(same, 1.0 / SEQ, 0.0)
        sums_out[...] = sums[...]
        grad_acc[...] = jnp.zeros_like(grad_acc) if first else grad_in[...]

    width = ctx.shape[1]
    heads = width // HD
    level = clips_ref[1]
    ratio = ctx[0] / level
    tangent = jnp.tanh(ratio)
    slope = 1.0 - tangent * tangent
    grad_cq = nt(low[...], full[0, 3 * width :, :]).T
    clip_sum = jnp.sum(grad_cq * (tangent - ratio * slope), axis=0, keepdims=True)
    sums_out[S_CLIP + 1 : S_CLIP + 2, :SEQ] += clip_sum
    grad_ctx_t = (grad_cq * slope).astype(BF)
    grad_ctx = grad_ctx_t.T
    acc[3 * width :, :] = nn((level * tangent).astype(BF), low[...])
    for head in range(heads):
        lo = head * HD
        queries = qkv[0, lo : lo + HD, :] * BF(0.125)
        keys = qkv[0, width + lo : width + lo + HD, :]
        values = qkv[0, 2 * width + lo : 2 * width + lo + HD, :]
        t_queries = t_qkv[0, lo : lo + HD, :] * BF(0.125)
        t_keys = t_qkv[0, width + lo : width + lo + HD, :]
        scores = tn(keys, queries)
        probs = jnp.exp(scores + mask_bias[...] - lse[0, head : head + 1, :])
        grad_probs = tn(values, grad_ctx_t[lo : lo + HD, :])
        grad_values = nn(probs.astype(BF), grad_ctx[:, lo : lo + HD])
        row_sum = jnp.sum(probs * grad_probs, axis=0, keepdims=True)
        gap = scores - tn(t_keys, t_queries)
        grad_scores = (probs * (grad_probs - row_sum) + gap * mask_scale[...]).astype(BF)
        grad_keys = nn(grad_scores, queries.T)
        grad_qkv[lo : lo + HD, :] = (nn(keys, grad_scores) * 0.125).astype(BF)
        grad_qkv[width + lo : width + lo + HD, :] = grad_keys.T.astype(BF)
        grad_qkv[2 * width + lo : 2 * width + lo + HD, :] = grad_values.T.astype(BF)
    acc[: 3 * width, :] = nn(grad_qkv[...], xq[...])
    store_pieces(meta[0], acc, keep_ref, send_ref)
    grad_acc[...] += tn(grad_qkv[...], full[0, : 3 * width, :])

    @pl.when(step == steps - 1)
    def _():
        if not last:
            grad_out[...] = grad_acc[...]
            return
        half = xb.shape[0]
        level = clips_ref[0]
        for index in range(2):

            def finish_rows(at, index=index):
                to = pl.ds(pl.multiple_of(at.start + index * half, ROWS), ROWS)
                values = xa[meta[1], at, :] if index == 0 else xb[at, :]
                ratio = values.astype(F32) / level
                tangent = jnp.tanh(ratio)
                slope = 1.0 - tangent * tangent
                grad = grad_acc[to, :]
                sums_out[S_CLIP : S_CLIP + 1, :] += colsum(grad * (tangent - ratio * slope))
                total = grad * slope + grad_one[to, :]
                if index == 0:
                    own_out[at, :] = total
                else:
                    partner_out[at, :] = total.astype(BF)

            by_rows(half, finish_rows)


def finish(
    meta, attn_own, attn_other, own, other, sums, levels, attn_latent, in_latent, out_latent,
    qkv_out, attn_out, in_out, out_out, gain_out, bias_out, clip_out, scales, blocks, sems,
):
    place = meta[0]
    core = place & BIT_C
    bit_one = BIT_X + core * (BIT_Y - BIT_X)
    bit_two = BIT_X + BIT_Y - bit_one
    both = BIT_X | BIT_Y
    for j in range(6):
        total = jnp.sum(sums[j : j + 1, :], axis=1, keepdims=True)
        entries = D * D if j < 4 else D * FF
        scales[j : j + 1, :] = total / (levels[j : j + 1, :] * entries)
    gain_out[...] = sums[S_GAIN : S_GAIN + 2, :]
    bias_out[...] = sums[S_BIAS : S_BIAS + 2, :]
    clip_out[...] = jnp.broadcast_to(
        jnp.sum(sums[S_CLIP : S_CLIP + 4, :], axis=1, keepdims=True), clip_out.shape
    )
    flips = (0, bit_one, bit_two, both)
    flips += (BIT_C, BIT_C | bit_two, BIT_C | bit_one, BIT_C | both)

    def attn_copies(index):
        piece = place ^ flips[index]
        row = pl.multiple_of(piece * PIECE, PIECE)
        late = pl.multiple_of(jnp.maximum(piece * PIECE - ATTN_QKV, 0), PIECE)
        early = pl.multiple_of(jnp.minimum(row, ATTN_QKV - PIECE), PIECE)
        block = blocks.at[2, pl.ds(row, PIECE)]
        return (
            piece < ATTN_QKV // PIECE,
            pltpu.make_async_copy(block, qkv_out.at[pl.ds(early, PIECE)], sems.at[2, index]),
            pltpu.make_async_copy(block, attn_out.at[pl.ds(late, PIECE)], sems.at[2, index]),
        )

    copies = []
    for index, flip in enumerate(flips):
        piece = place ^ flip
        at = pl.ds(pl.multiple_of(piece * PIECE, PIECE), PIECE)
        unit = index % 4
        for kind, (latent, out) in enumerate(((in_latent, in_out), (out_latent, out_out))):
            source = own if index < 4 else other
            blocks[kind, at, :] = (
                source[unit, kind].astype(F32)
                + scales[4 + kind : 5 + kind, :] * latent[at, :].astype(F32)
            )
            copy = pltpu.make_async_copy(blocks.at[kind, at], out.at[at], sems.at[kind, index])
            copy.start()
            copies.append(copy)
        source = attn_own if index < 4 else attn_other
        blocks[2, at, :] = (
            source[unit, 0].astype(F32)
            + scales[pl.ds(piece // 2, 1), :] * attn_latent[at, :].astype(F32)
        )
        in_qkv, to_qkv, to_out = attn_copies(index)

        @pl.when(in_qkv)
        def _(copy=to_qkv):
            copy.start()

        @pl.when(jnp.logical_not(in_qkv))
        def _(copy=to_out):
            copy.start()

    for copy in copies:
        copy.wait()
    for index in range(8):
        in_qkv, to_qkv, to_out = attn_copies(index)

        @pl.when(in_qkv)
        def _(copy=to_qkv):
            copy.wait()

        @pl.when(jnp.logical_not(in_qkv))
        def _(copy=to_out):
            copy.wait()


VM = pl.BlockSpec(memory_space=pltpu.VMEM)
SM = pl.BlockSpec(memory_space=pltpu.SMEM)
HBM = pl.BlockSpec(memory_space=pltpu.HBM)
ANY = pl.BlockSpec(memory_space=pl.ANY)
DMA_SEMS = pltpu.SemaphoreType.DMA((N_COPIES + 1,))


def shape(dims, dtype):
    return jax.ShapeDtypeStruct(dims, dtype)


def cost(args, outs, flops):
    total = sum(a.size * a.dtype.itemsize for a in args) + sum(
        o.size * o.dtype.itemsize for o in outs
    )
    return pl.CostEstimate(flops=flops, bytes_accessed=total, transcendentals=0)


def call(name, body, args, specs, outs, scratch, flops, limit=VMEM_WIDE, out_specs=None):
    return pl.pallas_call(
        body,
        name=name,
        in_specs=specs,
        out_specs=out_specs or [VM] * len(outs),
        out_shape=outs,
        scratch_shapes=scratch,
        compiler_params=pltpu.CompilerParams(vmem_limit_bytes=limit),
        cost_estimate=cost(args, outs, flops),
    )(*args)


def every(array):
    dims = array.shape
    return pl.BlockSpec(dims, lambda i, meta: (0,) * len(dims))


def slot_of(array, first=0, rows=None):
    dims = array.shape
    block = (1, rows or dims[1]) + dims[2:]
    return pl.BlockSpec(block, lambda i, meta: ((first + i) % N_SLOTS,) + (0,) * (len(dims) - 1))


def call_by_slots(name, body, meta, args, specs, outs, out_specs, scratch, flops, steps=N_SLOTS, limit=VMEM_WIDE):
    return pl.pallas_call(
        body,
        name=name,
        grid_spec=pltpu.PrefetchScalarGridSpec(
            num_scalar_prefetch=1,
            grid=(steps,),
            in_specs=specs,
            out_specs=out_specs,
            scratch_shapes=scratch,
        ),
        out_shape=outs,
        compiler_params=pltpu.CompilerParams(vmem_limit_bytes=limit),
        cost_estimate=cost(args, outs, flops),
    )(meta, *args)


def swap(array, axis, size, bit):
    return lax.ppermute(array, axis, [(i, i ^ bit) for i in range(size)])


def swap_by_core(array, dp, bit_zero, bit_one):
    pairs = [(i, i ^ (bit_one if i & BIT_C else bit_zero)) for i in range(dp)]
    return lax.ppermute(array, "dp", pairs)


def near(array, dp):
    return swap_by_core(array, dp, BIT_X, BIT_Y)


def far(array, dp):
    return swap_by_core(array, dp, BIT_Y, BIT_X)


def cross(array, dp):
    return swap(array, "dp", dp, BIT_C)


def line(array, dp, n, bit_zero, bit_one):
    pairs = []
    for i in range(dp):
        for j in range(n):
            pairs.append((i * n + j, i * n + (j ^ (bit_one if i & BIT_C else bit_zero))))
    return lax.ppermute(array, ("dp", "head"), pairs)


def line_one(array, dp, n):
    return line(array, dp, n, 1, 3)


def line_two(array, dp, n):
    return line(array, dp, n, 2, 1)


class Line:
    def __init__(self, piece, dp, n):
        self.piece, self.dp, self.n = piece[None], dp, n
        self.flying = None
        self.stage = 0

    def land(self):
        stage, got = self.stage, self.flying
        self.stage += 1
        if stage == 0:
            self.flying = (line_one(self.piece, self.dp, self.n),)
        elif stage == 1:
            self.one = got[0]
            self.both = jnp.concatenate([self.piece, got[0]])
            self.flying = (line_two(self.both, self.dp, self.n),)
        else:
            self.flying = None
            remote = [self.one[0], got[0][0], got[0][1]]
            count = self.piece.shape[1]
            self.remote = [
                jnp.concatenate([r[index] for r in remote], axis=0) for index in range(count)
            ]


class Plane:
    def __init__(self, remote, dp):
        self.remote, self.dp = remote, dp
        self.flying = None
        self.stage = 0

    def land(self):
        dp, stage, got = self.dp, self.stage, self.flying
        self.stage += 1
        if stage == 0:
            self.flying = (near(self.remote, dp),)
        elif stage == 1:
            self.pair = jnp.concatenate([self.remote, got[0]])
            self.flying = (far(self.pair, dp),)
            self.crossed = cross(self.pair, dp)
        elif stage == 2:
            self.pair_far = got[0]
            self.flying = (cross(self.pair_far, dp),)
        else:
            self.parts = (self.pair, self.pair_far, self.crossed, got[0])
            self.flying = None


class Reduce:
    def __init__(self, keep, send, dp, n, mode, sent=None):
        self.keep, self.send, self.dp, self.n, self.mode = keep, send, dp, n, mode
        self.sent = sent
        self.flying = None
        self.stage = 0

    def land(self):
        dp, n, stage = self.dp, self.n, self.stage
        self.stage += 1
        got = self.flying
        if stage == 0:
            self.mark = self.send
            self.flying = (cross(self.send, dp),)
        elif stage == 1:
            self.total = self.keep.astype(F32) + got[0].astype(F32)
            self.mark = self.total[2:].astype(BF)
            self.flying = (near(self.mark, dp),)
        elif stage == 2:
            self.total = self.total[:2] + got[0].astype(F32)
            self.mark = self.total[1].astype(BF)
            self.flying = (far(self.mark, dp),)
        elif stage == 3:
            self.total = self.total[0] + got[0].astype(F32)
            if self.mode == "whole":
                self.mark = self.total[2:].astype(BF)
                self.flying = (line_two(self.mark, dp, n),)
            elif self.mode == "sent":
                self.mark = self.total.astype(BF)
                self.flying = (swap(self.mark, "head", n, 1),)
            else:
                self.mark = (self.total[0] + self.sent.result[1].astype(F32)).astype(BF)
                self.flying = (swap(self.mark, "head", n, 3),)
        elif stage == 4:
            if self.mode == "sent":
                self.flying, self.result = None, got[0]
            elif self.mode == "kept":
                self.finish(self.total[1] + self.sent.result[0].astype(F32) + got[0].astype(F32))
            else:
                self.total = self.total[:2] + got[0].astype(F32)
                self.mark = self.total[1].astype(BF)
                self.flying = (line_one(self.mark, dp, n),)
        elif stage == 5:
            self.finish(self.total[0] + got[0].astype(F32))

    def finish(self, mine):
        bit = GROUP
        while bit < self.dp:
            mine = mine + swap(mine.astype(BF), "dp", self.dp, bit).astype(F32)
            bit *= 2
        self.result, self.flying = mine, None


class Share:
    def __init__(self, piece, dp):
        self.piece, self.dp = piece[None], dp
        self.flying = None
        self.stage = 0

    def land(self):
        dp, stage = self.dp, self.stage
        self.stage += 1
        got = self.flying
        if stage == 0:
            self.flying = (near(self.piece, dp),)
        elif stage == 1:
            self.pair = jnp.concatenate([self.piece, got[0]])
            self.flying = (far(self.pair, dp),)
        elif stage == 2:
            self.quad = jnp.concatenate([self.pair, got[0]])
            self.flying = (cross(self.quad, dp),)
        elif stage == 3:
            self.result = (self.quad, got[0])
            self.flying = None


class Sum:
    def __init__(self, values, steps):
        self.values = values
        self.steps = steps
        self.flying = None
        self.stage = 0

    def land(self):
        got, values = self.flying, self.values
        if got is not None:
            self.values = values + got[0] if len(got) == 1 else (values + got[0]) + (got[1] + got[2])
        if self.stage < len(self.steps):
            axis, size, bits = self.steps[self.stage]
            flips = bits if len(bits) == 1 else (bits[0], bits[1], bits[0] | bits[1])
            self.flying = tuple(swap(self.values, axis, size, flip) for flip in flips)
        else:
            self.flying = None
            self.result = self.values
        self.stage += 1


def steps_over(axis, size, bit=1):
    steps = []
    while bit < size:
        bits = (bit, 2 * bit) if 2 * bit < size else (bit,)
        steps.append((axis, size, bits))
        bit <<= len(bits)
    return steps


def beside(flights, outs):
    flights = [f for f in flights if f.flying is not None]
    tied, outs = lax.optimization_barrier((tuple(f.flying for f in flights), tuple(outs)))
    for flight, flying in zip(flights, tied):
        flight.flying = flying
    return outs


class Once:
    def __init__(self, flying):
        self.flying = (flying,)

    def land(self):
        self.result = self.flying[0]
        self.flying = None


def then(first, *later):
    for flight in later:
        flight.flying, first.mark = lax.optimization_barrier((flight.flying, first.mark))


def land(*flights):
    for flight in flights:
        flight.land()


def on_device(
    dp,
    n,
    hidden_in,
    teacher_in,
    out_grad,
    segment_ids,
    qkv_latent,
    out_latent,
    ffn_in_latent,
    ffn_out_latent,
    norm_gain,
    norm_bias,
    clips,
    teacher_qkv,
    teacher_out,
    teacher_ffn_in,
    teacher_ffn_out,
    teacher_gain,
    teacher_bias,
):
    h = lax.axis_index("head")
    place = lax.axis_index("dp") % GROUP
    parity = h % MICRO
    half = hidden_in.shape[1]
    width = qkv_latent.shape[-1]
    meta = jnp.stack([place, parity, h // MICRO]).astype(jnp.int32)

    def exchange(array):
        return Once(swap(array, "head", n, 1))

    def tie(*values):
        return lax.optimization_barrier(values)

    def lines(array):
        return jnp.swapaxes(array, 1, 2).reshape(3 * width, D)

    big = pltpu.VMEM((n, D, D), BF)
    tall = pltpu.VMEM((SEQ, D), F32)
    mm = 2 * SEQ * D * D
    square, band, sheet = shape((D, D), BF), shape((PIECE, D), BF), shape((half, D), BF)
    weights = [ANY] * (1 + N_PARTS)

    t_qkv_rows, qkv_rows = lines(teacher_qkv), lines(qkv_latent)
    t_piece_attn, t_piece_in = call(
        "cut_first",
        cut_first,
        (meta, t_qkv_rows, teacher_out, teacher_ffn_in),
        [SM] + [HBM] * 3,
        [band] * 2,
        [pltpu.SemaphoreType.DMA((2,))],
        mm // 8,
    )
    z0, z1 = Line(t_piece_attn[None], dp, n), Line(t_piece_in[None], dp, n)
    land(z0, z1)
    t_send, t_piece_out, x_send, g_send = call(
        "cut_rest",
        cut_rest,
        (meta, teacher_in, teacher_ffn_out, hidden_in, out_grad),
        [SM] + [HBM] * 4,
        [sheet, band, sheet, sheet],
        [pltpu.SemaphoreType.DMA((4,))],
        mm // 8,
    )
    land(z0)
    t_send, z0.both = tie(t_send, z0.both)
    t_ex = exchange(t_send)
    attn_latent, squares = call(
        "sum_squares",
        sum_squares,
        (qkv_rows, out_latent, ffn_in_latent, ffn_out_latent),
        [VM] * 4,
        [square, shape((8, D), F32)],
        [],
        mm,
    )
    latents = [attn_latent, ffn_in_latent, ffn_out_latent]
    total = Sum(squares, steps_over("head", n))
    land(total)
    total.values, z1.flying = tie(total.values, z1.flying)
    land(z1)
    land(total)
    results = beside(
        (z0,),
        call(
            "binarize",
            binarize,
            (meta, total.result) + tuple(latents),
            [SM] + [VM] * 4,
            [square] * 3 + [band] * 3 + [shape((8, D), F32)],
            [],
            mm,
        ),
    )
    bins, s_pieces, levels = results[:3], results[3:6], results[6]
    land(z0)
    p0 = Plane(z0.remote[0], dp)
    land(p0)
    piece, p0.remote = tie(s_pieces[0], p0.remote)
    z2 = Line(piece[None], dp, n)
    land(z2)
    land(z1)
    p1 = Plane(z1.remote[0], dp)
    land(p0)
    p1.remote, p0.pair = tie(p1.remote, p0.pair)
    land(p1)
    land(z2)
    t_piece_out, z2.both = tie(t_piece_out, z2.both)
    z3 = Line(t_piece_out[None], dp, n)
    land(z3)
    land(t_ex)
    land(p0)
    p1.flying, p0.pair_far = tie(p1.flying, p0.pair_far)
    land(p1)
    z2.flying, p1.pair = tie(z2.flying, p1.pair)
    land(z2)
    p2 = Plane(z2.remote[0], dp)
    land(p2)
    land(z3)
    pieces_in, pieces_out, p2.remote = tie(s_pieces[1], s_pieces[2], p2.remote)
    z45 = Line(jnp.stack([pieces_in, pieces_out]), dp, n)
    land(z45)
    x_send, p1.pair = tie(x_send, p1.pair)
    x_ex = exchange(x_send)
    land(p0)

    def slots_shape(rows, columns, dtype=BF):
        return shape((n, rows, columns), dtype)

    def run(name, body, args, specs, outs, out_specs, scratch, flops, limit=VMEM_WIDE):
        specs = [spec if spec is not None else every(arg) for spec, arg in zip(specs, args)]
        out_specs = [spec if spec is not None else every(out) for spec, out in zip(out_specs, outs)]
        return call_by_slots(name, body, meta, args, specs, outs, out_specs, scratch, flops, limit=limit)

    attn_scratch = [big, pltpu.VMEM((D, SEQ), BF), pltpu.VMEM((SEQ, SEQ), F32), tall, DMA_SEMS]
    qkv_shape = slots_shape(3 * width, SEQ)
    tall_shape, low_shape = shape((SEQ, D), F32), shape((SEQ, D), BF)
    t_qkv, t_first, t_first_low = beside(
        (p1, p2, z3, z45, x_ex),
        run(
            "teacher_attend",
            functools.partial(attend_forward, False),
            (clips, teacher_in, t_ex.result, segment_ids, teacher_gain, teacher_bias, t_qkv_rows, teacher_out)
            + p0.parts,
            [SM] + [None] * 5 + [HBM] + weights,
            [qkv_shape, tall_shape, low_shape],
            [slot_of(qkv_shape)] + [None] * 2,
            [pltpu.VMEM((SEQ, D), BF)] + attn_scratch,
            8 * mm,
        ),
    )
    land(p1, p2, z3, z45, x_ex)
    p3 = Plane(z3.remote[0], dp)
    land(p3, p1)
    act_shape = slots_shape(SEQ, D)
    (t_act,) = beside(
        (p2, p3, z45),
        run(
            "teacher_hidden",
            functools.partial(hidden_forward, False),
            (clips, t_first_low, teacher_ffn_in) + p1.parts,
            [SM, None] + weights,
            [act_shape],
            [slot_of(act_shape)],
            [big, tall, DMA_SEMS],
            6 * mm,
        ),
    )
    land(p2, p3, z45)
    p4, p5 = Plane(z45.remote[0], dp), Plane(z45.remote[1], dp)
    land(p4, p2)
    big_shape, quant_t_shape = shape((n, D, D), BF), shape((D, SEQ), BF)
    lse_shape, ctx_shape = slots_shape(8, SEQ, F32), slots_shape(width, SEQ, F32)
    full_attn, qkv, lse, ctx, pre_one, quant, quant_t, xq = beside(
        (p3, p4),
        run(
            "student_attend",
            functools.partial(attend_forward, True),
            (clips, hidden_in, x_ex.result, segment_ids, norm_gain, norm_bias, bins[0]) + p2.parts,
            [SM] + [None] * 5 + weights,
            [big_shape, qkv_shape, lse_shape, ctx_shape, tall_shape, low_shape, quant_t_shape, low_shape],
            [HBM] + [slot_of(a) for a in (qkv_shape, lse_shape, ctx_shape)] + [None] * 4,
            attn_scratch,
            8 * mm,
        ),
    )
    land(p3, p4)
    p5.remote, quant = tie(p5.remote, quant)
    land(p5, p3)
    (t_result,) = beside(
        (p4, p5),
        run(
            "teacher_output",
            functools.partial(output_forward, False),
            (t_act, teacher_gain, teacher_bias, teacher_ffn_out) + p3.parts + (t_first,),
            [slot_of(t_act), None, None] + weights + [ANY],
            [tall_shape],
            [None],
            [big, tall, DMA_SEMS, pltpu.SemaphoreType.DMA((1,)), tall],
            4 * mm,
        ),
    )
    land(p4, p5, p4)
    g_send, t_result = tie(g_send, t_result)
    g_ex = exchange(g_send)
    act_t_shape = slots_shape(D, SEQ)
    full_in, act, act_t, slope, clip_term = beside(
        (p5, g_ex),
        run(
            "student_hidden",
            functools.partial(hidden_forward, True),
            (clips, quant, bins[1]) + p4.parts,
            [SM, None] + weights,
            [big_shape, act_shape, act_t_shape, act_shape, act_shape],
            [HBM] + [slot_of(a) for a in (act_shape, act_t_shape, act_shape, act_shape)],
            [big, tall, DMA_SEMS],
            8 * mm,
        ),
    )
    land(p5, p5, g_ex)
    sums_shape = shape((S_ROWS, D), F32)
    full_out, out_own, out_far, grad_two, low_two, sums = run(
        "student_output",
        functools.partial(output_forward, True),
        (act, norm_gain, norm_bias, bins[2]) + p5.parts + (pre_one, t_result, out_grad, g_ex.result),
        [slot_of(act), None, None] + weights + [ANY] * 4,
        [big_shape, sheet, sheet, tall_shape, low_shape, sums_shape],
        [HBM] + [None] * 5,
        [big, tall, DMA_SEMS, pltpu.SemaphoreType.DMA((4,)), tall, tall] + [pltpu.VMEM((half, D), BF)] * 2,
        4 * mm,
    )

    def grad_call(name, left_t, right):
        pieces_shape = shape((GROUP // 2, n, PIECE, D), BF)
        block = (GROUP // 2, 1, PIECE, D)

        def there(i, meta):
            return (0, jnp.where(i == 0, 0, crosswise(meta[0] & BIT_C, i)), 0, 0)

        return run(
            name,
            weight_grad,
            (left_t, right),
            [slot_of(a) if len(a.shape) == 3 else None for a in (left_t, right)],
            [pieces_shape] * 2,
            [pl.BlockSpec(block, lambda i, meta: (0, i, 0, 0)), pl.BlockSpec(block, there)],
            [pltpu.VMEM((D, D), F32)],
            4 * mm,
            limit=VMEM_SMALL,
        )

    out_ex = exchange(out_far)
    keep, send = grad_call("ffn_out_weight", act_t, low_two)
    r_out = Reduce(keep, send, dp, n, "whole")
    land(r_out)
    grad_hidden, sums = beside(
        (r_out,),
        run(
            "hidden_back",
            hidden_back,
            (low_two, full_out, slope, clip_term, sums),
            [None] + [slot_of(a) for a in (full_out, slope, clip_term)] + [None],
            [act_shape, sums_shape],
            [slot_of(act_shape), None],
            [],
            5 * mm,
            limit=VMEM_SMALL,
        ),
    )
    land(r_out)
    grad_hidden, r_out.mark = tie(grad_hidden, r_out.mark)
    keep, send = grad_call("ffn_in_weight", quant_t, grad_hidden)
    r_in = Reduce(keep, send, dp, n, "whole")
    land(r_in)
    grad_hidden, r_in.mark = tie(grad_hidden, r_in.mark)
    grad_one, low_one, sums = beside(
        (r_in, r_out, out_ex),
        run(
            "first_back",
            first_back,
            (clips, grad_hidden, full_in, pre_one, norm_gain, norm_bias, grad_two, sums),
            [SM, slot_of(grad_hidden), slot_of(full_in), ANY, None, None, ANY, None],
            [tall_shape, low_shape, sums_shape],
            [None] * 3,
            [tall] * 3 + [pltpu.SemaphoreType.DMA((2,))],
            4 * mm,
            limit=VMEM_SMALL,
        ),
    )

    def attend_back_slots(first_slot, steps, grad_xq, sums):
        first, last = first_slot == 1, first_slot == 3
        args = (clips, segment_ids, qkv, t_qkv, lse, ctx, low_one, xq, full_attn, sums)
        one = [slot_of(a, first_slot) for a in (qkv, t_qkv, lse, ctx)]
        one[1] = slot_of(t_qkv, first_slot, 2 * width)
        specs = [SM, every(segment_ids)] + one
        specs += [every(low_one), every(xq), slot_of(full_attn, first_slot), every(sums)]
        pieces_shape = shape((GROUP // 2, steps, PIECE, D), BF)
        block = pl.BlockSpec((GROUP // 2, 1, PIECE, D), lambda i, meta: (0, i, 0, 0))
        outs = [pieces_shape] * 2 + [sums_shape]
        more = () if first else (grad_xq,)
        if last:
            more += (grad_one, hidden_in, x_ex.result)
            outs += [shape((half, D), F32), sheet]
        else:
            outs += [tall_shape]
        return call_by_slots(
            "attend_back",
            functools.partial(attend_back, steps, first, last),
            meta,
            args + more,
            specs + [every(a) for a in more],
            outs,
            [block, block] + [every(o) for o in outs[2:]],
            [
                pltpu.VMEM((SEQ, SEQ), F32),
                pltpu.VMEM((SEQ, SEQ), F32),
                pltpu.VMEM((3 * width, SEQ), BF),
                pltpu.VMEM((D, D), F32),
                tall,
            ],
            5 * steps * mm,
            steps=steps,
            limit=VMEM_MIDDLE,
        )

    land(r_out, r_in, out_ex)
    low_one, r_out.mark, r_in.mark = tie(low_one, r_out.mark, r_in.mark)
    keep, send, sums, grad_xq = beside((r_out,), attend_back_slots(1, 2, None, sums))
    r_sent = Reduce(keep, send, dp, n, "sent")
    land(r_sent)
    land(r_out)
    then(r_out, r_in)
    land(r_in)
    then(r_in, r_sent)
    land(r_sent)
    grad_xq, r_sent.mark, r_out.mark = tie(grad_xq, r_sent.mark, r_out.mark)
    keep, send, sums, in_grad_own, in_grad_far = beside(
        (r_sent, r_in, r_out), attend_back_slots(3, 2, grad_xq, sums)
    )
    def both(own, far):
        first_row = jnp.where(parity == 0, own, far)
        second_row = jnp.where(parity == 0, far, own)
        return jnp.stack([first_row, second_row])

    r_kept = Reduce(keep, send, dp, n, "kept", r_sent)
    land(r_kept)
    land(r_sent)
    then(r_sent, r_kept)
    land(r_kept)
    then(r_kept, r_in, r_out)
    land(r_in)
    then(r_in, r_out)
    land(r_out)
    then(r_out, r_sent)
    land(r_sent)
    repeats = dp // GROUP

    then(r_sent, r_kept)
    land(r_kept)
    then(r_kept, r_sent, r_in)
    land(r_in)
    land(r_sent)
    land(r_kept)
    out_all = both(out_own, out_ex.result)
    (out_all,) = beside((r_kept, r_in, r_out), (out_all,))
    land(r_in, r_out, r_kept)
    in_grad_far, kept = tie(in_grad_far, r_kept.result)
    r_kept.result = kept
    in_ex = exchange(in_grad_far)
    direct_attn, direct_ffn, sums = call(
        "settle",
        functools.partial(settle, repeats),
        (meta, levels, sums, r_kept.result, r_in.result, r_out.result) + tuple(latents),
        [SM] + [VM] * 8,
        [shape((1, PIECE, D), BF), shape((2, PIECE, D), BF), sums_shape],
        [],
        mm // 4,
        limit=VMEM_SMALL,
    )
    s_attn, s_ffn = Share(direct_attn, dp), Share(direct_ffn, dp)
    total = Sum(sums, [("dp", dp, (BIT_C,))] + steps_over("dp", dp, BIT_X) + steps_over("head", n))
    land(total, s_attn, s_ffn)
    land(total)
    s_attn.flying, total.values = tie(s_attn.flying, total.values)
    land(s_attn)
    s_ffn.flying, s_attn.pair = tie(s_ffn.flying, s_attn.pair)
    land(s_ffn)
    total.flying, s_ffn.pair = tie(total.flying, s_ffn.pair)
    land(total)
    in_ex.flying, total.values = tie(in_ex.flying, total.values)
    land(in_ex)
    in_grad_all = both(in_grad_own, in_ex.result.astype(F32))
    (in_grad_all,) = beside((s_attn, total, s_ffn), (in_grad_all,))
    land(s_attn)
    while total.flying is not None:
        land(total)
    land(s_ffn, s_attn, s_ffn)
    sums = total.result
    flat = shape((D, D), F32)
    qkv_grad, attn_out_grad, in_grad, out_grad_w, gain_grad, bias_grad, clip_sums = call(
        "finish",
        finish,
        (meta,) + s_attn.result + s_ffn.result + (sums, levels) + tuple(latents),
        [SM] + [VM] * 9,
        [shape((ATTN_QKV, D), F32), shape((width, D), F32), flat, flat]
        + [shape((2, D), F32)] * 2
        + [shape((4, 128), F32)],
        [pltpu.VMEM((8, D), F32), pltpu.VMEM((3, D, D), F32), pltpu.SemaphoreType.DMA((3, 8))],
        mm // 2,
        limit=VMEM_SMALL,
        out_specs=[HBM] * 4 + [VM] * 3,
    )
    qkv_grad = jnp.swapaxes(qkv_grad.reshape(3, width, D), 1, 2)
    clip_grad = clip_sums[:, 0]

    return (
        out_all,
        in_grad_all,
        qkv_grad,
        attn_out_grad,
        in_grad,
        out_grad_w,
        gain_grad,
        bias_grad,
        clip_grad,
    )


def solution(mesh):
    placed = (
        P(None, ("dp", "head"), None),
        P(None, ("dp", "head"), None),
        P(None, ("dp", "head"), None),
        P(None, "dp", None),
        P(None, None, "head"),
        P("head", None),
        P(None, "head"),
        P("head", None),
        P(),
        P(),
        P(),
        P(None, None, "head"),
        P("head", None),
        P(None, "head"),
        P("head", None),
        P(),
        P(),
    )
    return jax.shard_map(
        functools.partial(on_device, mesh.shape["dp"], mesh.shape["head"]),
        mesh=mesh,
        in_specs=placed,
        out_specs=(
            P(None, ("dp", "head"), None),
            P(None, ("dp", "head"), None),
            P(None, None, "head"),
            P("head", None),
            P(None, "head"),
            P("head", None),
            P(),
            P(),
            P(),
        ),
        check_vma=False,
    )
```

```python
import functools

import jax
import jax.numpy as jnp
from jax import lax
from jax.experimental import pallas as pl
from jax.experimental.pallas import tpu as pltpu
from jax.sharding import PartitionSpec as P

D = 768
HD = 64
FF = 3072
SEQ = 512
MICRO = 2
GROUP = 8
PIECE = D // GROUP
BIT_C, BIT_X, BIT_Y = 1, 2, 4
NEG = -1000000000.0
BF = jnp.bfloat16
F32 = jnp.float32
VMEM_WIDE = 56 * 1024 * 1024
VMEM_SMALL = 20 * 1024 * 1024
VMEM_MIDDLE = 32 * 1024 * 1024

def nn(a, b):
    return lax.dot_general(a, b, (((1,), (0,)), ((), ())), preferred_element_type=F32)


def nt(a, b):
    return lax.dot_general(a, b, (((1,), (1,)), ((), ())), preferred_element_type=F32)


def tn(a, b):
    return lax.dot_general(a, b, (((0,), (0,)), ((), ())), preferred_element_type=F32)


def normalize(values):
    centred = values - jnp.mean(values, axis=-1, keepdims=True)
    inv_std = lax.rsqrt(jnp.mean(centred * centred, axis=-1, keepdims=True) + 1e-06)
    return centred * inv_std, inv_std


def norm_back(upstream, normed, inv_std, gain_vec):
    scaled = upstream * gain_vec
    centred_grad = (
        scaled
        - jnp.mean(scaled, axis=-1, keepdims=True)
        - normed * jnp.mean(scaled * normed, axis=-1, keepdims=True)
    )
    return centred_grad * inv_std


def colsum(values):
    return jnp.sum(values, axis=0, keepdims=True)


def crosswise(core, slot):
    return (slot + core) % 3 + 1


def xor_of(core, slot):
    return (1 - core) * slot + core * ((slot + 1) % 3 + 1)


class Weights:
    def __init__(self, place, by_xor, own, parts, full, sems, out=None):
        core = place & BIT_C
        bit_one = BIT_X + core * (BIT_Y - BIT_X)
        bit_two = BIT_X + BIT_Y - bit_one
        both = BIT_X | BIT_Y
        self.pairs = []
        row = 0
        for array in own:
            self.pairs.append((array, full.at[0, pl.ds(row, array.shape[0])]))
            row += array.shape[0]
        self.owned = len(own)
        flips = (
            (0, bit_one),
            (bit_two, both),
            (BIT_C, BIT_C | bit_two),
            (BIT_C | bit_one, BIT_C | both),
        )
        for source, part in enumerate(parts):
            for unit in range(2):
                row = pl.multiple_of((place ^ flips[source][unit]) * PIECE, PIECE)
                for slot in range(1, N_SLOTS):
                    if by_xor:
                        to = xor_of(core if source < 2 else 1 - core, slot)
                    else:
                        to = slot if source < 2 else crosswise(1 - core, slot)
                    start = (unit * (N_SLOTS - 1) + slot - 1) * PIECE
                    self.pairs.append(
                        (part.at[pl.ds(start, PIECE)], full.at[to, pl.ds(row, PIECE)])
                    )
        self.sems, self.full, self.out = sems, full, out

    def copies(self):
        return [
            pltpu.make_async_copy(source, target, self.sems.at[index])
            for index, (source, target) in enumerate(self.pairs)
        ]

    def start(self):
        for copy in self.copies():
            copy.start()

    def wait(self, slot):
        @pl.when(slot == 0)
        def _():
            for copy in self.copies()[: self.owned]:
                copy.wait()

        @pl.when(slot == 1)
        def _():
            for copy in self.copies()[self.owned :]:
                copy.wait()
            if self.out is not None:
                self.whole().start()

    def whole(self):
        return pltpu.make_async_copy(self.full, self.out, self.sems.at[N_COPIES])

    def end(self):
        if self.out is not None:
            self.whole().wait()


N_SLOTS = 4
N_PARTS = 4
N_COPIES = 2 + N_PARTS * 2 * (N_SLOTS - 1)


def store_pieces(place, acc, keep_ref, send_ref):
    core = place & BIT_C
    bit_one = BIT_X + core * (BIT_Y - BIT_X)
    bit_two = BIT_X + BIT_Y - bit_one
    both = BIT_X | BIT_Y
    for index, flip in enumerate((0, bit_two, bit_one, both)):
        row = pl.multiple_of((place ^ flip) * PIECE, PIECE)
        keep_ref[index, 0] = acc[pl.ds(row, PIECE), :].astype(BF)
    for index, flip in enumerate((0, bit_one, bit_two, both)):
        row = pl.multiple_of((place ^ BIT_C ^ flip) * PIECE, PIECE)
        send_ref[index, 0] = acc[pl.ds(row, PIECE), :].astype(BF)


ATTN_QKV = 3 * D // 4


def cut_first(meta, t_qkv, t_out, t_ffn_in, attn_piece, in_piece, sems):
    place = meta[0]
    rows = pl.ds(pl.multiple_of(place * PIECE, PIECE), PIECE)
    other = pltpu.make_async_copy(t_ffn_in.at[rows], in_piece, sems.at[1])
    other.start()
    in_qkv = place < ATTN_QKV // PIECE

    @pl.when(in_qkv)
    def _():
        copy = pltpu.make_async_copy(t_qkv.at[rows], attn_piece, sems.at[0])
        copy.start()
        copy.wait()

    @pl.when(jnp.logical_not(in_qkv))
    def _():
        at = pl.ds(pl.multiple_of(place * PIECE - ATTN_QKV, PIECE), PIECE)
        copy = pltpu.make_async_copy(t_out.at[at], attn_piece, sems.at[0])
        copy.start()
        copy.wait()

    other.wait()


def cut_rest(meta, t_in, t_ffn_out, x_in, g_in, t_send, out_piece, x_send, g_send, sems):
    rows = pl.ds(pl.multiple_of(meta[0] * PIECE, PIECE), PIECE)
    there = 1 - meta[1]
    pairs = (
        (t_in.at[there], t_send),
        (t_ffn_out.at[rows], out_piece),
        (x_in.at[there], x_send),
        (g_in.at[there], g_send),
    )
    copies = [
        pltpu.make_async_copy(source, target, sems.at[index])
        for index, (source, target) in enumerate(pairs)
    ]
    for copy in copies:
        copy.start()
    for copy in copies:
        copy.wait()


def sum_squares(qkv, out, ffn_in, ffn_out, attn, squares):
    attn[:ATTN_QKV, :] = qkv[...]
    attn[ATTN_QKV:, :] = out[...]
    squares[...] = jnp.zeros_like(squares)
    block = D // 4
    step_rows = 64
    for index, (latent, start, count) in enumerate(
        [(attn, j * block, block) for j in range(4)] + [(ffn_in, 0, D), (ffn_out, 0, D)]
    ):

        def step(i, carry, latent=latent, start=start):
            at = pl.ds(pl.multiple_of(start + i * step_rows, step_rows), step_rows)
            values = latent[at, :].astype(F32)
            return carry + jnp.sum((values * values).reshape(step_rows // 8, 8, D), axis=0)

        total = lax.fori_loop(0, count // step_rows, step, jnp.zeros((8, D), F32))
        squares[index : index + 1, :] = colsum(total)


def binarize(meta, squares, attn, ffn_in, ffn_out, *outs):
    bins, pieces, levels = outs[:3], outs[3:6], outs[6]
    entries = jnp.where(
        lax.broadcasted_iota(jnp.int32, (8, 1), 0) < 4, float(D * D), float(D * FF)
    )
    totals = jnp.sum(squares[...], axis=1, keepdims=True)
    levels[...] = jnp.broadcast_to(jnp.sqrt(totals / entries + 1e-06), (8, D))
    step_rows = 64
    for index, latent in enumerate((attn, ffn_in, ffn_out)):

        def step(i, carry, index=index, latent=latent):
            at = pl.ds(pl.multiple_of(i * step_rows, step_rows), step_rows)
            line = i // (D // 4 // step_rows) if index == 0 else index + 3
            level = levels[pl.ds(line, 1), :]
            bins[index][at, :] = (level * jnp.tanh(latent[at, :].astype(F32) * (2.0 / level))).astype(BF)
            return carry

        lax.fori_loop(0, D // step_rows, step, 0)
        pieces[index][...] = bins[index][pl.ds(pl.multiple_of(meta[0] * PIECE, PIECE), PIECE), :]


def same_segment(meta, segments):
    own = segments[meta[1], pl.ds(meta[2], 1), :].astype(F32)
    half = SEQ // 2
    turned = jnp.concatenate([own[:, half:], own[:, :half]], axis=1)
    lanes = jnp.where(meta[1] == 0, own, turned)
    column = jnp.broadcast_to(lanes, (8, SEQ)).T[:, :1]
    return column == lanes


S_SCALE, S_GAIN, S_BIAS, S_CLIP, S_ROWS = 0, 6, 8, 10, 16


def settle(repeats, meta, levels, sums, *refs):
    grads, latents, (direct_attn, direct_ffn, sums_out) = refs[:3], refs[3:6], refs[6:]
    at = pl.ds(pl.multiple_of(meta[0] * PIECE, PIECE), PIECE)
    block = meta[0] // 2
    sums_out[...] = sums[...]
    for index in range(3):
        level = levels[pl.ds(block, 1), :] if index == 0 else levels[3 + index : 4 + index, :]
        grad = grads[index][...]
        unit = latents[index][at, :].astype(F32) * (2.0 / level)
        tangent = jnp.tanh(unit)
        slope = 1.0 - tangent * tangent
        direct = (grad * 2.0 * slope).astype(BF)
        term = colsum(grad * (tangent - unit * slope)) * (1.0 / repeats)
        if index == 0:
            direct_attn[0] = direct
            for j in range(4):
                sums_out[j : j + 1, :] = jnp.where(block == j, term, 0.0)
        else:
            direct_ffn[index - 1] = direct
            sums_out[3 + index : 4 + index, :] = term


ROWS = 256
HIDDEN_BLOCK = 256


def by_rows(count, body, rows=ROWS):
    def step(index, carry):
        body(pl.ds(pl.multiple_of(index * rows, rows), rows))
        return carry

    lax.fori_loop(0, count // rows, step, 0)


class Late:
    def __init__(self, sources, targets, sems):
        self.copies = [
            pltpu.make_async_copy(source, target, sems.at[index])
            for index, (source, target) in enumerate(zip(sources, targets))
        ]

    def start(self):
        for copy in self.copies:
            copy.start()

    def wait(self):
        for copy in self.copies:
            copy.wait()


def attend_forward(student, meta, *refs):
    clips_ref, xa, xb, segments, gain, bias = refs[:6]
    owned = 1 if student else 2
    own, refs = refs[6 : 6 + owned], refs[6 + owned :]
    parts, refs = refs[:N_PARTS], refs[N_PARTS:]
    if student:
        full_out, qkv_out, lse_out, ctx_out, pre_out, quant_out, quant_t_out, rows = refs[:8]
        refs = refs[8:]
    else:
        qkv_out, first_out, first_low_out = refs[:3]
        rows, refs = refs[3], refs[4:]
    full, rows_t, mask_bias, attn, sems = refs
    slot, slots = pl.program_id(0), full.shape[0]
    half = xb.shape[0]
    width = D // slots
    heads = width // HD

    def x_at(at, index):
        return xa[meta[1], at, :] if index == 0 else xb[at, :]

    weights = Weights(meta[0], True, own, parts, full, sems, full_out if student else None)

    @pl.when(slot == 0)
    def _():
        weights.start()
        for index in range(2):

            def quantize(at, index=index):
                to = pl.ds(pl.multiple_of(at.start + index * half, ROWS), ROWS)
                values = x_at(at, index)
                if student:
                    level = clips_ref[0]
                    values = (level * jnp.tanh(values.astype(F32) / level)).astype(BF)
                rows[to, :] = values

            by_rows(half, quantize)
        rows_t[...] = rows[...].T
        mask_bias[...] = jnp.where(same_segment(meta, segments), 0.0, NEG)
        attn[...] = jnp.zeros_like(attn)

    weights.wait(slot)
    qkv_t = nn(full[slot, : 3 * width, :], rows_t[...]).astype(BF)
    qkv_out[0] = qkv_t
    lows = []
    for head in range(heads):
        lo = head * HD
        queries = qkv_t[lo : lo + HD] * BF(0.125)
        keys = qkv_t[width + lo : width + lo + HD]
        values = qkv_t[2 * width + lo : 2 * width + lo + HD]
        scores = tn(keys, queries) + mask_bias[...]
        peak = jnp.max(scores, axis=0, keepdims=True)
        powers = jnp.exp(scores - peak)
        total = jnp.sum(powers, axis=0, keepdims=True)
        probs = (powers * (1.0 / total)).astype(BF)
        context = nn(values, probs)
        if student:
            lse_out[0, head : head + 1, :] = peak + jnp.log(total)
            ctx_out[0, lo : lo + HD, :] = context
            level = clips_ref[1]
            context = level * jnp.tanh(context / level)
        lows.append(context.astype(BF))
    attn[...] += tn(jnp.concatenate(lows, axis=0), full[slot, 3 * width :, :])

    @pl.when(slot == slots - 1)
    def _():
        for index in range(2):

            def last(at, index=index):
                to = pl.ds(pl.multiple_of(at.start + index * half, ROWS), ROWS)
                pre = x_at(at, index).astype(F32) + attn[to, :]
                first = normalize(pre)[0] * gain[0:1, :] + bias[0:1, :]
                if student:
                    pre_out[to, :] = pre
                    level = clips_ref[2]
                    quant_out[to, :] = (level * jnp.tanh(first / level)).astype(BF)
                else:
                    first_out[to, :] = first
                    first_low_out[to, :] = first.astype(BF)

            by_rows(half, last)
        if student:
            quant_t_out[...] = quant_out[...].T
        weights.end()


def hidden_forward(student, meta, clips_ref, quant, own, *refs):
    parts, refs = refs[:N_PARTS], refs[N_PARTS:]
    if student:
        full_out, act_out, act_t_out, slope_out, clip_out = refs[:5]
        refs = refs[5:]
    else:
        (act_out,), refs = refs[:1], refs[1:]
    full, sems = refs
    slot, slots = pl.program_id(0), full.shape[0]
    weights = Weights(meta[0], False, (own,), parts, full, sems, full_out if student else None)

    @pl.when(slot == 0)
    def _():
        weights.start()

    weights.wait(slot)
    for start in range(0, D, HIDDEN_BLOCK):
        columns = slice(start, start + HIDDEN_BLOCK)
        values = nn(quant[...], full[slot, :, columns])
        cdf = 0.5 * (1.0 + lax.erf(values * 0.7071067811865476))
        act = values * cdf
        if not student:
            act_out[0, :, columns] = act.astype(BF)
            continue
        level = clips_ref[3]
        ratio = act * (1.0 / level)
        tangent = jnp.tanh(ratio)
        quantized = (level * tangent).astype(BF)
        act_out[0, :, columns] = quantized
        act_t_out[0, columns, :] = quantized.T
        slope = 1.0 - tangent * tangent
        density = jnp.exp(values * values * -0.5) * 0.3989422804014327
        slope_out[0, :, columns] = (slope * (cdf + values * density)).astype(BF)
        clip_out[0, :, columns] = (tangent - ratio * slope).astype(BF)

    @pl.when(slot == slots - 1)
    def _():
        weights.end()


def output_forward(student, meta, act, gain, bias, own, *refs):
    parts, refs = refs[:N_PARTS], refs[N_PARTS:]
    if student:
        pre, t_result, grad_a, grad_b = refs[:4]
        full_out, own_out, partner_out, grad_out, low_out, sums_out = refs[4:10]
        refs = refs[10:]
    else:
        (first_in, result_out), refs = refs[:2], refs[2:]
    full, acc, sems, late_sems = refs[:4]
    held = refs[4:]
    slot, slots = pl.program_id(0), full.shape[0]
    weights = Weights(meta[0], False, (own,), parts, full, sems, full_out if student else None)

    if student:
        late = Late((pre, t_result, grad_a.at[meta[1]], grad_b), held, late_sems)
    else:
        late = Late((first_in,), held, late_sems)

    @pl.when(slot == 0)
    def _():
        weights.start()
        late.start()
        acc[...] = jnp.zeros_like(acc)

    weights.wait(slot)
    acc[...] += nn(act[0], full[slot])

    @pl.when(slot == slots - 1)
    def _():
        late.wait()
        if not student:

            def result_rows(at):
                total = held[0][at, :] + acc[at, :]
                result_out[at, :] = normalize(total)[0] * gain[1:2, :] + bias[1:2, :]

            by_rows(SEQ, result_rows)
            return
        half = held[3].shape[0]
        sums_out[...] = jnp.zeros_like(sums_out)
        for index in range(2):

            def last(at, index=index):
                to = pl.ds(pl.multiple_of(at.start + index * half, ROWS), ROWS)
                first = normalize(held[0][to, :])[0] * gain[0:1, :] + bias[0:1, :]
                normed, inv_std = normalize(first + acc[to, :])
                result = normed * gain[1:2, :] + bias[1:2, :]
                (own_out if index == 0 else partner_out)[at, :] = result.astype(BF)
                cotangent = held[2 + index][at, :].astype(F32)
                grad_result = cotangent + result - held[1][to, :]
                sums_out[S_GAIN + 1 : S_GAIN + 2, :] += colsum(grad_result * normed)
                sums_out[S_BIAS + 1 : S_BIAS + 2, :] += colsum(grad_result)
                grad_pre = norm_back(grad_result, normed, inv_std, gain[1:2, :])
                grad_out[to, :] = grad_pre
                low_out[to, :] = grad_pre.astype(BF)

            by_rows(half, last)
        weights.end()


def weight_grad(meta, left_t, right, keep_ref, send_ref, acc):
    left = left_t[0] if len(left_t.shape) == 3 else left_t[...]
    rows = right[0] if len(right.shape) == 3 else right[...]
    acc[...] = nn(left, rows)
    store_pieces(meta[0], acc, keep_ref, send_ref)


def hidden_back(meta, grad_low, full, slope, clip, sums, grad_out, sums_out):
    @pl.when(pl.program_id(0) == 0)
    def _():
        sums_out[...] = sums[...]

    grad = nt(grad_low[...], full[0])
    grad_out[0] = (grad * slope[0].astype(F32)).astype(BF)
    sums_out[S_CLIP + 3 : S_CLIP + 4, :] += colsum(grad * clip[0].astype(F32))


def first_back(
    meta, clips_ref, grad_hidden, full, pre_in, gain, bias, grad_two_in, sums, grad_out, low_out, sums_out,
    acc, pre, grad_two, sems,
):
    slot = pl.program_id(0)
    late = Late((pre_in, grad_two_in), (pre, grad_two), sems)

    @pl.when(slot == 0)
    def _():
        late.start()
        sums_out[...] = sums[...]
        acc[...] = jnp.zeros_like(acc)

    acc[...] += nt(grad_hidden[0], full[0])
    level = clips_ref[2]

    @pl.when(slot == N_SLOTS - 1)
    def _():
        late.wait()

        def last(at):
            normed, inv_std = normalize(pre[at, :])
            ratio = (normed * gain[0:1, :] + bias[0:1, :]) / level
            tangent = jnp.tanh(ratio)
            slope = 1.0 - tangent * tangent
            grad_fq = acc[at, :]
            sums_out[S_CLIP + 2 : S_CLIP + 3, :] += colsum(grad_fq * (tangent - ratio * slope))
            upstream = grad_fq * slope + grad_two[at, :]
            sums_out[S_GAIN : S_GAIN + 1, :] += colsum(upstream * normed)
            sums_out[S_BIAS : S_BIAS + 1, :] += colsum(upstream)
            grad_pre = norm_back(upstream, normed, inv_std, gain[0:1, :])
            grad_out[at, :] = grad_pre
            low_out[at, :] = grad_pre.astype(BF)

        by_rows(SEQ, last)


def attend_back(steps, first, last, meta, clips_ref, *refs):
    segments, qkv, t_qkv, lse, ctx, low, xq, full, sums = refs[:9]
    rest = list(refs[9:])
    grad_in = None if first else rest.pop(0)
    if last:
        grad_one, xa, xb = rest[:3]
        rest = rest[3:]
    keep_ref, send_ref, sums_out = rest[:3]
    rest = rest[3:]
    if last:
        own_out, partner_out = rest[:2]
        rest = rest[2:]
    else:
        grad_out = rest.pop(0)
    mask_bias, mask_scale, grad_qkv, acc, grad_acc = rest
    step = pl.program_id(0)

    @pl.when(step == 0)
    def _():
        same = same_segment(meta, segments)
        mask_bias[...] = jnp.where(same, 0.0, NEG)
        mask_scale[...] = jnp.where(same, 1.0 / SEQ, 0.0)
        sums_out[...] = sums[...]
        grad_acc[...] = jnp.zeros_like(grad_acc) if first else grad_in[...]

    width = ctx.shape[1]
    heads = width // HD
    level = clips_ref[1]
    ratio = ctx[0] / level
    tangent = jnp.tanh(ratio)
    slope = 1.0 - tangent * tangent
    grad_cq = nt(low[...], full[0, 3 * width :, :]).T
    clip_sum = jnp.sum(grad_cq * (tangent - ratio * slope), axis=0, keepdims=True)
    sums_out[S_CLIP + 1 : S_CLIP + 2, :SEQ] += clip_sum
    grad_ctx_t = (grad_cq * slope).astype(BF)
    grad_ctx = grad_ctx_t.T
    acc[3 * width :, :] = nn((level * tangent).astype(BF), low[...])
    for head in range(heads):
        lo = head * HD
        queries = qkv[0, lo : lo + HD, :] * BF(0.125)
        keys = qkv[0, width + lo : width + lo + HD, :]
        values = qkv[0, 2 * width + lo : 2 * width + lo + HD, :]
        t_queries = t_qkv[0, lo : lo + HD, :] * BF(0.125)
        t_keys = t_qkv[0, width + lo : width + lo + HD, :]
        scores = tn(keys, queries)
        probs = jnp.exp(scores + mask_bias[...] - lse[0, head : head + 1, :])
        grad_probs = tn(values, grad_ctx_t[lo : lo + HD, :])
        grad_values = nn(probs.astype(BF), grad_ctx[:, lo : lo + HD])
        row_sum = jnp.sum(probs * grad_probs, axis=0, keepdims=True)
        gap = scores - tn(t_keys, t_queries)
        grad_scores = (probs * (grad_probs - row_sum) + gap * mask_scale[...]).astype(BF)
        grad_keys = nn(grad_scores, queries.T)
        grad_qkv[lo : lo + HD, :] = (nn(keys, grad_scores) * 0.125).astype(BF)
        grad_qkv[width + lo : width + lo + HD, :] = grad_keys.T.astype(BF)
        grad_qkv[2 * width + lo : 2 * width + lo + HD, :] = grad_values.T.astype(BF)
    acc[: 3 * width, :] = nn(grad_qkv[...], xq[...])
    store_pieces(meta[0], acc, keep_ref, send_ref)
    grad_acc[...] += tn(grad_qkv[...], full[0, : 3 * width, :])

    @pl.when(step == steps - 1)
    def _():
        if not last:
            grad_out[...] = grad_acc[...]
            return
        half = xb.shape[0]
        level = clips_ref[0]
        for index in range(2):

            def finish_rows(at, index=index):
                to = pl.ds(pl.multiple_of(at.start + index * half, ROWS), ROWS)
                values = xa[meta[1], at, :] if index == 0 else xb[at, :]
                ratio = values.astype(F32) / level
                tangent = jnp.tanh(ratio)
                slope = 1.0 - tangent * tangent
                grad = grad_acc[to, :]
                sums_out[S_CLIP : S_CLIP + 1, :] += colsum(grad * (tangent - ratio * slope))
                total = grad * slope + grad_one[to, :]
                if index == 0:
                    own_out[at, :] = total
                else:
                    partner_out[at, :] = total.astype(BF)

            by_rows(half, finish_rows)


def finish(
    meta, attn_own, attn_other, own, other, sums, levels, attn_latent, in_latent, out_latent,
    qkv_out, attn_out, in_out, out_out, gain_out, bias_out, clip_out, scales, blocks, sems,
):
    place = meta[0]
    core = place & BIT_C
    bit_one = BIT_X + core * (BIT_Y - BIT_X)
    bit_two = BIT_X + BIT_Y - bit_one
    both = BIT_X | BIT_Y
    for j in range(6):
        total = jnp.sum(sums[j : j + 1, :], axis=1, keepdims=True)
        entries = D * D if j < 4 else D * FF
        scales[j : j + 1, :] = total / (levels[j : j + 1, :] * entries)
    gain_out[...] = sums[S_GAIN : S_GAIN + 2, :]
    bias_out[...] = sums[S_BIAS : S_BIAS + 2, :]
    clip_out[...] = jnp.broadcast_to(
        jnp.sum(sums[S_CLIP : S_CLIP + 4, :], axis=1, keepdims=True), clip_out.shape
    )
    flips = (0, bit_one, bit_two, both)
    flips += (BIT_C, BIT_C | bit_two, BIT_C | bit_one, BIT_C | both)

    def attn_copies(index):
        piece = place ^ flips[index]
        row = pl.multiple_of(piece * PIECE, PIECE)
        late = pl.multiple_of(jnp.maximum(piece * PIECE - ATTN_QKV, 0), PIECE)
        early = pl.multiple_of(jnp.minimum(row, ATTN_QKV - PIECE), PIECE)
        block = blocks.at[2, pl.ds(row, PIECE)]
        return (
            piece < ATTN_QKV // PIECE,
            pltpu.make_async_copy(block, qkv_out.at[pl.ds(early, PIECE)], sems.at[2, index]),
            pltpu.make_async_copy(block, attn_out.at[pl.ds(late, PIECE)], sems.at[2, index]),
        )

    copies = []
    for index, flip in enumerate(flips):
        piece = place ^ flip
        at = pl.ds(pl.multiple_of(piece * PIECE, PIECE), PIECE)
        unit = index % 4
        for kind, (latent, out) in enumerate(((in_latent, in_out), (out_latent, out_out))):
            source = own if index < 4 else other
            blocks[kind, at, :] = (
                source[unit, kind].astype(F32)
                + scales[4 + kind : 5 + kind, :] * latent[at, :].astype(F32)
            )
            copy = pltpu.make_async_copy(blocks.at[kind, at], out.at[at], sems.at[kind, index])
            copy.start()
            copies.append(copy)
        source = attn_own if index < 4 else attn_other
        blocks[2, at, :] = (
            source[unit, 0].astype(F32)
            + scales[pl.ds(piece // 2, 1), :] * attn_latent[at, :].astype(F32)
        )
        in_qkv, to_qkv, to_out = attn_copies(index)

        @pl.when(in_qkv)
        def _(copy=to_qkv):
            copy.start()

        @pl.when(jnp.logical_not(in_qkv))
        def _(copy=to_out):
            copy.start()

    for copy in copies:
        copy.wait()
    for index in range(8):
        in_qkv, to_qkv, to_out = attn_copies(index)

        @pl.when(in_qkv)
        def _(copy=to_qkv):
            copy.wait()

        @pl.when(jnp.logical_not(in_qkv))
        def _(copy=to_out):
            copy.wait()


VM = pl.BlockSpec(memory_space=pltpu.VMEM)
SM = pl.BlockSpec(memory_space=pltpu.SMEM)
HBM = pl.BlockSpec(memory_space=pltpu.HBM)
ANY = pl.BlockSpec(memory_space=pl.ANY)
DMA_SEMS = pltpu.SemaphoreType.DMA((N_COPIES + 1,))


def shape(dims, dtype):
    return jax.ShapeDtypeStruct(dims, dtype)


def cost(args, outs, flops):
    total = sum(a.size * a.dtype.itemsize for a in args) + sum(
        o.size * o.dtype.itemsize for o in outs
    )
    return pl.CostEstimate(flops=flops, bytes_accessed=total, transcendentals=0)


def call(name, body, args, specs, outs, scratch, flops, limit=VMEM_WIDE, out_specs=None):
    return pl.pallas_call(
        body,
        name=name,
        in_specs=specs,
        out_specs=out_specs or [VM] * len(outs),
        out_shape=outs,
        scratch_shapes=scratch,
        compiler_params=pltpu.CompilerParams(vmem_limit_bytes=limit),
        cost_estimate=cost(args, outs, flops),
    )(*args)


def every(array):
    dims = array.shape
    return pl.BlockSpec(dims, lambda i, meta: (0,) * len(dims))


def slot_of(array, first=0, rows=None):
    dims = array.shape
    block = (1, rows or dims[1]) + dims[2:]
    return pl.BlockSpec(block, lambda i, meta: ((first + i) % N_SLOTS,) + (0,) * (len(dims) - 1))


def call_by_slots(name, body, meta, args, specs, outs, out_specs, scratch, flops, steps=N_SLOTS, limit=VMEM_WIDE):
    return pl.pallas_call(
        body,
        name=name,
        grid_spec=pltpu.PrefetchScalarGridSpec(
            num_scalar_prefetch=1,
            grid=(steps,),
            in_specs=specs,
            out_specs=out_specs,
            scratch_shapes=scratch,
        ),
        out_shape=outs,
        compiler_params=pltpu.CompilerParams(vmem_limit_bytes=limit),
        cost_estimate=cost(args, outs, flops),
    )(meta, *args)


def swap(array, axis, size, bit):
    return lax.ppermute(array, axis, [(i, i ^ bit) for i in range(size)])


def swap_by_core(array, dp, bit_zero, bit_one):
    pairs = [(i, i ^ (bit_one if i & BIT_C else bit_zero)) for i in range(dp)]
    return lax.ppermute(array, "dp", pairs)


def near(array, dp):
    return swap_by_core(array, dp, BIT_X, BIT_Y)


def far(array, dp):
    return swap_by_core(array, dp, BIT_Y, BIT_X)


def cross(array, dp):
    return swap(array, "dp", dp, BIT_C)


def line(array, dp, n, bit_zero, bit_one):
    pairs = []
    for i in range(dp):
        for j in range(n):
            pairs.append((i * n + j, i * n + (j ^ (bit_one if i & BIT_C else bit_zero))))
    return lax.ppermute(array, ("dp", "head"), pairs)


def line_one(array, dp, n):
    return line(array, dp, n, 1, 3)


def line_two(array, dp, n):
    return line(array, dp, n, 2, 1)


class Line:
    def __init__(self, piece, dp, n):
        self.piece, self.dp, self.n = piece[None], dp, n
        self.flying = None
        self.stage = 0

    def land(self):
        stage, got = self.stage, self.flying
        self.stage += 1
        if stage == 0:
            self.flying = (line_one(self.piece, self.dp, self.n),)
        elif stage == 1:
            self.one = got[0]
            self.both = jnp.concatenate([self.piece, got[0]])
            self.flying = (line_two(self.both, self.dp, self.n),)
        else:
            self.flying = None
            remote = [self.one[0], got[0][0], got[0][1]]
            count = self.piece.shape[1]
            self.remote = [
                jnp.concatenate([r[index] for r in remote], axis=0) for index in range(count)
            ]


class Plane:
    def __init__(self, remote, dp):
        self.remote, self.dp = remote, dp
        self.flying = None
        self.stage = 0

    def land(self):
        dp, stage, got = self.dp, self.stage, self.flying
        self.stage += 1
        if stage == 0:
            self.flying = (near(self.remote, dp),)
        elif stage == 1:
            self.pair = jnp.concatenate([self.remote, got[0]])
            self.flying = (far(self.pair, dp),)
            self.crossed = cross(self.pair, dp)
        elif stage == 2:
            self.pair_far = got[0]
            self.flying = (cross(self.pair_far, dp),)
        else:
            self.parts = (self.pair, self.pair_far, self.crossed, got[0])
            self.flying = None


class Reduce:
    def __init__(self, keep, send, dp, n, mode, sent=None):
        self.keep, self.send, self.dp, self.n, self.mode = keep, send, dp, n, mode
        self.sent = sent
        self.flying = None
        self.stage = 0

    def land(self):
        dp, n, stage = self.dp, self.n, self.stage
        self.stage += 1
        got = self.flying
        if stage == 0:
            self.mark = self.send
            self.flying = (cross(self.send, dp),)
        elif stage == 1:
            self.total = self.keep.astype(F32) + got[0].astype(F32)
            self.mark = self.total[2:].astype(BF)
            self.flying = (near(self.mark, dp),)
        elif stage == 2:
            self.total = self.total[:2] + got[0].astype(F32)
            self.mark = self.total[1].astype(BF)
            self.flying = (far(self.mark, dp),)
        elif stage == 3:
            self.total = self.total[0] + got[0].astype(F32)
            if self.mode == "whole":
                self.mark = self.total[2:].astype(BF)
                self.flying = (line_two(self.mark, dp, n),)
            elif self.mode == "sent":
                self.mark = self.total.astype(BF)
                self.flying = (swap(self.mark, "head", n, 1),)
            else:
                self.mark = (self.total[0] + self.sent.result[1].astype(F32)).astype(BF)
                self.flying = (swap(self.mark, "head", n, 3),)
        elif stage == 4:
            if self.mode == "sent":
                self.flying, self.result = None, got[0]
            elif self.mode == "kept":
                self.finish(self.total[1] + self.sent.result[0].astype(F32) + got[0].astype(F32))
            else:
                self.total = self.total[:2] + got[0].astype(F32)
                self.mark = self.total[1].astype(BF)
                self.flying = (line_one(self.mark, dp, n),)
        elif stage == 5:
            self.finish(self.total[0] + got[0].astype(F32))

    def finish(self, mine):
        bit = GROUP
        while bit < self.dp:
            mine = mine + swap(mine.astype(BF), "dp", self.dp, bit).astype(F32)
            bit *= 2
        self.result, self.flying = mine, None


class Share:
    def __init__(self, piece, dp):
        self.piece, self.dp = piece[None], dp
        self.flying = None
        self.stage = 0

    def land(self):
        dp, stage = self.dp, self.stage
        self.stage += 1
        got = self.flying
        if stage == 0:
            self.flying = (near(self.piece, dp),)
        elif stage == 1:
            self.pair = jnp.concatenate([self.piece, got[0]])
            self.flying = (far(self.pair, dp),)
        elif stage == 2:
            self.quad = jnp.concatenate([self.pair, got[0]])
            self.flying = (cross(self.quad, dp),)
        elif stage == 3:
            self.result = (self.quad, got[0])
            self.flying = None


class Sum:
    def __init__(self, values, steps):
        self.values = values
        self.steps = steps
        self.flying = None
        self.stage = 0

    def land(self):
        got, values = self.flying, self.values
        if got is not None:
            self.values = values + got[0] if len(got) == 1 else (values + got[0]) + (got[1] + got[2])
        if self.stage < len(self.steps):
            axis, size, bits = self.steps[self.stage]
            flips = bits if len(bits) == 1 else (bits[0], bits[1], bits[0] | bits[1])
            self.flying = tuple(swap(self.values, axis, size, flip) for flip in flips)
        else:
            self.flying = None
            self.result = self.values
        self.stage += 1


def steps_over(axis, size, bit=1):
    steps = []
    while bit < size:
        bits = (bit, 2 * bit) if 2 * bit < size else (bit,)
        steps.append((axis, size, bits))
        bit <<= len(bits)
    return steps


def beside(flights, outs):
    flights = [f for f in flights if f.flying is not None]
    tied, outs = lax.optimization_barrier((tuple(f.flying for f in flights), tuple(outs)))
    for flight, flying in zip(flights, tied):
        flight.flying = flying
    return outs


class Once:
    def __init__(self, flying):
        self.flying = (flying,)

    def land(self):
        self.result = self.flying[0]
        self.flying = None


def then(first, *later):
    for flight in later:
        flight.flying, first.mark = lax.optimization_barrier((flight.flying, first.mark))


def land(*flights):
    for flight in flights:
        flight.land()


def on_device(
    dp,
    n,
    hidden_in,
    teacher_in,
    out_grad,
    segment_ids,
    qkv_latent,
    out_latent,
    ffn_in_latent,
    ffn_out_latent,
    norm_gain,
    norm_bias,
    clips,
    teacher_qkv,
    teacher_out,
    teacher_ffn_in,
    teacher_ffn_out,
    teacher_gain,
    teacher_bias,
):
    h = lax.axis_index("head")
    place = lax.axis_index("dp") % GROUP
    parity = h % MICRO
    half = hidden_in.shape[1]
    width = qkv_latent.shape[-1]
    meta = jnp.stack([place, parity, h // MICRO]).astype(jnp.int32)

    def exchange(array):
        return Once(swap(array, "head", n, 1))

    def tie(*values):
        return lax.optimization_barrier(values)

    def lines(array):
        return jnp.swapaxes(array, 1, 2).reshape(3 * width, D)

    big = pltpu.VMEM((n, D, D), BF)
    tall = pltpu.VMEM((SEQ, D), F32)
    mm = 2 * SEQ * D * D
    square, band, sheet = shape((D, D), BF), shape((PIECE, D), BF), shape((half, D), BF)
    weights = [ANY] * (1 + N_PARTS)

    t_qkv_rows, qkv_rows = lines(teacher_qkv), lines(qkv_latent)
    t_piece_attn, t_piece_in = call(
        "cut_first",
        cut_first,
        (meta, t_qkv_rows, teacher_out, teacher_ffn_in),
        [SM] + [HBM] * 3,
        [band] * 2,
        [pltpu.SemaphoreType.DMA((2,))],
        mm // 8,
    )
    z0, z1 = Line(t_piece_attn[None], dp, n), Line(t_piece_in[None], dp, n)
    land(z0, z1)
    t_send, t_piece_out, x_send, g_send = call(
        "cut_rest",
        cut_rest,
        (meta, teacher_in, teacher_ffn_out, hidden_in, out_grad),
        [SM] + [HBM] * 4,
        [sheet, band, sheet, sheet],
        [pltpu.SemaphoreType.DMA((4,))],
        mm // 8,
    )
    land(z0)
    t_send, z0.both = tie(t_send, z0.both)
    t_ex = exchange(t_send)
    attn_latent, squares = call(
        "sum_squares",
        sum_squares,
        (qkv_rows, out_latent, ffn_in_latent, ffn_out_latent),
        [VM] * 4,
        [square, shape((8, D), F32)],
        [],
        mm,
    )
    latents = [attn_latent, ffn_in_latent, ffn_out_latent]
    total = Sum(squares, steps_over("head", n))
    land(total)
    total.values, z1.flying = tie(total.values, z1.flying)
    land(z1)
    land(total)
    results = beside(
        (z0,),
        call(
            "binarize",
            binarize,
            (meta, total.result) + tuple(latents),
            [SM] + [VM] * 4,
            [square] * 3 + [band] * 3 + [shape((8, D), F32)],
            [],
            mm,
        ),
    )
    bins, s_pieces, levels = results[:3], results[3:6], results[6]
    land(z0)
    p0 = Plane(z0.remote[0], dp)
    land(p0)
    piece, p0.remote = tie(s_pieces[0], p0.remote)
    z2 = Line(piece[None], dp, n)
    land(z2)
    land(z1)
    p1 = Plane(z1.remote[0], dp)
    land(p0)
    p1.remote, p0.pair = tie(p1.remote, p0.pair)
    land(p1)
    land(z2)
    t_piece_out, z2.both = tie(t_piece_out, z2.both)
    z3 = Line(t_piece_out[None], dp, n)
    land(z3)
    land(t_ex)
    land(p0)
    p1.flying, p0.pair_far = tie(p1.flying, p0.pair_far)
    land(p1)
    z2.flying, p1.pair = tie(z2.flying, p1.pair)
    land(z2)
    p2 = Plane(z2.remote[0], dp)
    land(p2)
    land(z3)
    pieces_in, pieces_out, p2.remote = tie(s_pieces[1], s_pieces[2], p2.remote)
    z45 = Line(jnp.stack([pieces_in, pieces_out]), dp, n)
    land(z45)
    x_send, p1.pair = tie(x_send, p1.pair)
    x_ex = exchange(x_send)
    land(p0)

    def slots_shape(rows, columns, dtype=BF):
        return shape((n, rows, columns), dtype)

    def run(name, body, args, specs, outs, out_specs, scratch, flops, limit=VMEM_WIDE):
        specs = [spec if spec is not None else every(arg) for spec, arg in zip(specs, args)]
        out_specs = [spec if spec is not None else every(out) for spec, out in zip(out_specs, outs)]
        return call_by_slots(name, body, meta, args, specs, outs, out_specs, scratch, flops, limit=limit)

    attn_scratch = [big, pltpu.VMEM((D, SEQ), BF), pltpu.VMEM((SEQ, SEQ), F32), tall, DMA_SEMS]
    qkv_shape = slots_shape(3 * width, SEQ)
    tall_shape, low_shape = shape((SEQ, D), F32), shape((SEQ, D), BF)
    t_qkv, t_first, t_first_low = beside(
        (p1, p2, z3, z45, x_ex),
        run(
            "teacher_attend",
            functools.partial(attend_forward, False),
            (clips, teacher_in, t_ex.result, segment_ids, teacher_gain, teacher_bias, t_qkv_rows, teacher_out)
            + p0.parts,
            [SM] + [None] * 5 + [HBM] + weights,
            [qkv_shape, tall_shape, low_shape],
            [slot_of(qkv_shape)] + [None] * 2,
            [pltpu.VMEM((SEQ, D), BF)] + attn_scratch,
            8 * mm,
        ),
    )
    land(p1, p2, z3, z45, x_ex)
    p3 = Plane(z3.remote[0], dp)
    land(p3, p1)
    act_shape = slots_shape(SEQ, D)
    (t_act,) = beside(
        (p2, p3, z45),
        run(
            "teacher_hidden",
            functools.partial(hidden_forward, False),
            (clips, t_first_low, teacher_ffn_in) + p1.parts,
            [SM, None] + weights,
            [act_shape],
            [slot_of(act_shape)],
            [big, DMA_SEMS],
            6 * mm,
        ),
    )
    land(p2, p3, z45)
    p4, p5 = Plane(z45.remote[0], dp), Plane(z45.remote[1], dp)
    land(p4, p2)
    big_shape, quant_t_shape = shape((n, D, D), BF), shape((D, SEQ), BF)
    lse_shape, ctx_shape = slots_shape(8, SEQ, F32), slots_shape(width, SEQ, F32)
    full_attn, qkv, lse, ctx, pre_one, quant, quant_t, xq = beside(
        (p3, p4),
        run(
            "student_attend",
            functools.partial(attend_forward, True),
            (clips, hidden_in, x_ex.result, segment_ids, norm_gain, norm_bias, bins[0]) + p2.parts,
            [SM] + [None] * 5 + weights,
            [big_shape, qkv_shape, lse_shape, ctx_shape, tall_shape, low_shape, quant_t_shape, low_shape],
            [HBM] + [slot_of(a) for a in (qkv_shape, lse_shape, ctx_shape)] + [None] * 4,
            attn_scratch,
            8 * mm,
        ),
    )
    land(p3, p4)
    p5.remote, quant = tie(p5.remote, quant)
    land(p5, p3)
    (t_result,) = beside(
        (p4, p5),
        run(
            "teacher_output",
            functools.partial(output_forward, False),
            (t_act, teacher_gain, teacher_bias, teacher_ffn_out) + p3.parts + (t_first,),
            [slot_of(t_act), None, None] + weights + [ANY],
            [tall_shape],
            [None],
            [big, tall, DMA_SEMS, pltpu.SemaphoreType.DMA((1,)), tall],
            4 * mm,
        ),
    )
    land(p4, p5, p4)
    g_send, t_result = tie(g_send, t_result)
    g_ex = exchange(g_send)
    act_t_shape = slots_shape(D, SEQ)
    full_in, act, act_t, slope, clip_term = beside(
        (p5, g_ex),
        run(
            "student_hidden",
            functools.partial(hidden_forward, True),
            (clips, quant, bins[1]) + p4.parts,
            [SM, None] + weights,
            [big_shape, act_shape, act_t_shape, act_shape, act_shape],
            [HBM] + [slot_of(a) for a in (act_shape, act_t_shape, act_shape, act_shape)],
            [big, DMA_SEMS],
            8 * mm,
        ),
    )
    land(p5, p5, g_ex)
    sums_shape = shape((S_ROWS, D), F32)
    full_out, out_own, out_far, grad_two, low_two, sums = run(
        "student_output",
        functools.partial(output_forward, True),
        (act, norm_gain, norm_bias, bins[2]) + p5.parts + (pre_one, t_result, out_grad, g_ex.result),
        [slot_of(act), None, None] + weights + [ANY] * 4,
        [big_shape, sheet, sheet, tall_shape, low_shape, sums_shape],
        [HBM] + [None] * 5,
        [big, tall, DMA_SEMS, pltpu.SemaphoreType.DMA((4,)), tall, tall] + [pltpu.VMEM((half, D), BF)] * 2,
        4 * mm,
    )

    def grad_call(name, left_t, right):
        pieces_shape = shape((GROUP // 2, n, PIECE, D), BF)
        block = (GROUP // 2, 1, PIECE, D)

        def there(i, meta):
            return (0, jnp.where(i == 0, 0, crosswise(meta[0] & BIT_C, i)), 0, 0)

        return run(
            name,
            weight_grad,
            (left_t, right),
            [slot_of(a) if len(a.shape) == 3 else None for a in (left_t, right)],
            [pieces_shape] * 2,
            [pl.BlockSpec(block, lambda i, meta: (0, i, 0, 0)), pl.BlockSpec(block, there)],
            [pltpu.VMEM((D, D), F32)],
            4 * mm,
            limit=VMEM_SMALL,
        )

    out_ex = exchange(out_far)
    keep, send = grad_call("ffn_out_weight", act_t, low_two)
    r_out = Reduce(keep, send, dp, n, "whole")
    land(r_out)
    grad_hidden, sums = beside(
        (r_out,),
        run(
            "hidden_back",
            hidden_back,
            (low_two, full_out, slope, clip_term, sums),
            [None] + [slot_of(a) for a in (full_out, slope, clip_term)] + [None],
            [act_shape, sums_shape],
            [slot_of(act_shape), None],
            [],
            5 * mm,
            limit=VMEM_SMALL,
        ),
    )
    land(r_out)
    grad_hidden, r_out.mark = tie(grad_hidden, r_out.mark)
    keep, send = grad_call("ffn_in_weight", quant_t, grad_hidden)
    r_in = Reduce(keep, send, dp, n, "whole")
    land(r_in)
    grad_hidden, r_in.mark = tie(grad_hidden, r_in.mark)
    grad_one, low_one, sums = beside(
        (r_in, r_out, out_ex),
        run(
            "first_back",
            first_back,
            (clips, grad_hidden, full_in, pre_one, norm_gain, norm_bias, grad_two, sums),
            [SM, slot_of(grad_hidden), slot_of(full_in), ANY, None, None, ANY, None],
            [tall_shape, low_shape, sums_shape],
            [None] * 3,
            [tall] * 3 + [pltpu.SemaphoreType.DMA((2,))],
            4 * mm,
            limit=VMEM_SMALL,
        ),
    )

    def attend_back_slots(first_slot, steps, grad_xq, sums):
        first, last = first_slot == 1, first_slot == 3
        args = (clips, segment_ids, qkv, t_qkv, lse, ctx, low_one, xq, full_attn, sums)
        one = [slot_of(a, first_slot) for a in (qkv, t_qkv, lse, ctx)]
        one[1] = slot_of(t_qkv, first_slot, 2 * width)
        specs = [SM, every(segment_ids)] + one
        specs += [every(low_one), every(xq), slot_of(full_attn, first_slot), every(sums)]
        pieces_shape = shape((GROUP // 2, steps, PIECE, D), BF)
        block = pl.BlockSpec((GROUP // 2, 1, PIECE, D), lambda i, meta: (0, i, 0, 0))
        outs = [pieces_shape] * 2 + [sums_shape]
        more = () if first else (grad_xq,)
        if last:
            more += (grad_one, hidden_in, x_ex.result)
            outs += [shape((half, D), F32), sheet]
        else:
            outs += [tall_shape]
        return call_by_slots(
            "attend_back",
            functools.partial(attend_back, steps, first, last),
            meta,
            args + more,
            specs + [every(a) for a in more],
            outs,
            [block, block] + [every(o) for o in outs[2:]],
            [
                pltpu.VMEM((SEQ, SEQ), F32),
                pltpu.VMEM((SEQ, SEQ), F32),
                pltpu.VMEM((3 * width, SEQ), BF),
                pltpu.VMEM((D, D), F32),
                tall,
            ],
            5 * steps * mm,
            steps=steps,
            limit=VMEM_MIDDLE,
        )

    land(r_out, r_in, out_ex)
    low_one, r_out.mark, r_in.mark = tie(low_one, r_out.mark, r_in.mark)
    keep, send, sums, grad_xq = beside((r_out,), attend_back_slots(1, 2, None, sums))
    r_sent = Reduce(keep, send, dp, n, "sent")
    land(r_sent)
    land(r_out)
    then(r_out, r_in)
    land(r_in)
    then(r_in, r_sent)
    land(r_sent)
    grad_xq, r_sent.mark, r_out.mark = tie(grad_xq, r_sent.mark, r_out.mark)
    keep, send, sums, in_grad_own, in_grad_far = beside(
        (r_sent, r_in, r_out), attend_back_slots(3, 2, grad_xq, sums)
    )
    def both(own, far):
        first_row = jnp.where(parity == 0, own, far)
        second_row = jnp.where(parity == 0, far, own)
        return jnp.stack([first_row, second_row])

    r_kept = Reduce(keep, send, dp, n, "kept", r_sent)
    land(r_kept)
    land(r_sent)
    then(r_sent, r_kept)
    land(r_kept)
    then(r_kept, r_in, r_out)
    land(r_in)
    then(r_in, r_out)
    land(r_out)
    then(r_out, r_sent)
    land(r_sent)
    repeats = dp // GROUP

    then(r_sent, r_kept)
    land(r_kept)
    then(r_kept, r_sent, r_in)
    land(r_in)
    land(r_sent)
    land(r_kept)
    out_all = both(out_own, out_ex.result)
    (out_all,) = beside((r_kept, r_in, r_out), (out_all,))
    land(r_in, r_out, r_kept)
    in_grad_far, kept = tie(in_grad_far, r_kept.result)
    r_kept.result = kept
    in_ex = exchange(in_grad_far)
    direct_attn, direct_ffn, sums = call(
        "settle",
        functools.partial(settle, repeats),
        (meta, levels, sums, r_kept.result, r_in.result, r_out.result) + tuple(latents),
        [SM] + [VM] * 8,
        [shape((1, PIECE, D), BF), shape((2, PIECE, D), BF), sums_shape],
        [],
        mm // 4,
        limit=VMEM_SMALL,
    )
    s_attn, s_ffn = Share(direct_attn, dp), Share(direct_ffn, dp)
    total = Sum(sums, [("dp", dp, (BIT_C,))] + steps_over("dp", dp, BIT_X) + steps_over("head", n))
    land(total, s_attn, s_ffn)
    land(total)
    s_attn.flying, total.values = tie(s_attn.flying, total.values)
    land(s_attn)
    s_ffn.flying, s_attn.pair = tie(s_ffn.flying, s_attn.pair)
    land(s_ffn)
    total.flying, s_ffn.pair = tie(total.flying, s_ffn.pair)
    land(total)
    in_ex.flying, total.values = tie(in_ex.flying, total.values)
    land(in_ex)
    in_grad_all = both(in_grad_own, in_ex.result.astype(F32))
    (in_grad_all,) = beside((s_attn, total, s_ffn), (in_grad_all,))
    land(s_attn)
    while total.flying is not None:
        land(total)
    land(s_ffn, s_attn, s_ffn)
    sums = total.result
    flat = shape((D, D), F32)
    qkv_grad, attn_out_grad, in_grad, out_grad_w, gain_grad, bias_grad, clip_sums = call(
        "finish",
        finish,
        (meta,) + s_attn.result + s_ffn.result + (sums, levels) + tuple(latents),
        [SM] + [VM] * 9,
        [shape((ATTN_QKV, D), F32), shape((width, D), F32), flat, flat]
        + [shape((2, D), F32)] * 2
        + [shape((4, 128), F32)],
        [pltpu.VMEM((8, D), F32), pltpu.VMEM((3, D, D), F32), pltpu.SemaphoreType.DMA((3, 8))],
        mm // 2,
        limit=VMEM_SMALL,
        out_specs=[HBM] * 4 + [VM] * 3,
    )
    qkv_grad = jnp.swapaxes(qkv_grad.reshape(3, width, D), 1, 2)
    clip_grad = clip_sums[:, 0]

    return (
        out_all,
        in_grad_all,
        qkv_grad,
        attn_out_grad,
        in_grad,
        out_grad_w,
        gain_grad,
        bias_grad,
        clip_grad,
    )


def solution(mesh):
    placed = (
        P(None, ("dp", "head"), None),
        P(None, ("dp", "head"), None),
        P(None, ("dp", "head"), None),
        P(None, "dp", None),
        P(None, None, "head"),
        P("head", None),
        P(None, "head"),
        P("head", None),
        P(),
        P(),
        P(),
        P(None, None, "head"),
        P("head", None),
        P(None, "head"),
        P("head", None),
        P(),
        P(),
    )
    return jax.shard_map(
        functools.partial(on_device, mesh.shape["dp"], mesh.shape["head"]),
        mesh=mesh,
        in_specs=placed,
        out_specs=(
            P(None, ("dp", "head"), None),
            P(None, ("dp", "head"), None),
            P(None, None, "head"),
            P("head", None),
            P(None, "head"),
            P("head", None),
            P(),
            P(),
            P(),
        ),
        check_vma=False,
    )
```

```python
import functools

import jax
import jax.numpy as jnp
from jax import lax
from jax.experimental import pallas as pl
from jax.experimental.pallas import tpu as pltpu
from jax.sharding import PartitionSpec as P

D = 768
HD = 64
FF = 3072
SEQ = 512
MICRO = 2
GROUP = 8
PIECE = D // GROUP
BIT_C, BIT_X, BIT_Y = 1, 2, 4
NEG = -1000000000.0
BF = jnp.bfloat16
F32 = jnp.float32
VMEM_WIDE = 56 * 1024 * 1024
VMEM_SMALL = 20 * 1024 * 1024
VMEM_MIDDLE = 32 * 1024 * 1024

def nn(a, b):
    return lax.dot_general(a, b, (((1,), (0,)), ((), ())), preferred_element_type=F32)


def nt(a, b):
    return lax.dot_general(a, b, (((1,), (1,)), ((), ())), preferred_element_type=F32)


def tn(a, b):
    return lax.dot_general(a, b, (((0,), (0,)), ((), ())), preferred_element_type=F32)


def normalize(values):
    centred = values - jnp.mean(values, axis=-1, keepdims=True)
    inv_std = lax.rsqrt(jnp.mean(centred * centred, axis=-1, keepdims=True) + 1e-06)
    return centred * inv_std, inv_std


def norm_back(upstream, normed, inv_std, gain_vec):
    scaled = upstream * gain_vec
    centred_grad = (
        scaled
        - jnp.mean(scaled, axis=-1, keepdims=True)
        - normed * jnp.mean(scaled * normed, axis=-1, keepdims=True)
    )
    return centred_grad * inv_std


def colsum(values):
    return jnp.sum(values, axis=0, keepdims=True)


def crosswise(core, slot):
    return (slot + core) % 3 + 1


def xor_of(core, slot):
    return (1 - core) * slot + core * ((slot + 1) % 3 + 1)


class Weights:
    def __init__(self, place, by_xor, own, parts, full, sems, out=None):
        core = place & BIT_C
        bit_one = BIT_X + core * (BIT_Y - BIT_X)
        bit_two = BIT_X + BIT_Y - bit_one
        both = BIT_X | BIT_Y
        self.pairs = []
        row = 0
        for array in own:
            self.pairs.append((array, full.at[0, pl.ds(row, array.shape[0])]))
            row += array.shape[0]
        self.owned = len(own)
        flips = (
            (0, bit_one),
            (bit_two, both),
            (BIT_C, BIT_C | bit_two),
            (BIT_C | bit_one, BIT_C | both),
        )
        for source, part in enumerate(parts):
            for unit in range(2):
                row = pl.multiple_of((place ^ flips[source][unit]) * PIECE, PIECE)
                for slot in range(1, N_SLOTS):
                    if by_xor:
                        to = xor_of(core if source < 2 else 1 - core, slot)
                    else:
                        to = slot if source < 2 else crosswise(1 - core, slot)
                    start = (unit * (N_SLOTS - 1) + slot - 1) * PIECE
                    self.pairs.append(
                        (part.at[pl.ds(start, PIECE)], full.at[to, pl.ds(row, PIECE)])
                    )
        self.sems, self.full, self.out = sems, full, out

    def copies(self):
        return [
            pltpu.make_async_copy(source, target, self.sems.at[index])
            for index, (source, target) in enumerate(self.pairs)
        ]

    def start(self):
        for copy in self.copies():
            copy.start()

    def wait(self, slot):
        @pl.when(slot == 0)
        def _():
            for copy in self.copies()[: self.owned]:
                copy.wait()

        @pl.when(slot == 1)
        def _():
            for copy in self.copies()[self.owned :]:
                copy.wait()
            if self.out is not None:
                self.whole().start()

    def whole(self):
        return pltpu.make_async_copy(self.full, self.out, self.sems.at[N_COPIES])

    def end(self):
        if self.out is not None:
            self.whole().wait()


N_SLOTS = 4
N_PARTS = 4
N_COPIES = 2 + N_PARTS * 2 * (N_SLOTS - 1)


def store_pieces(place, acc, keep_ref, send_ref):
    core = place & BIT_C
    bit_one = BIT_X + core * (BIT_Y - BIT_X)
    bit_two = BIT_X + BIT_Y - bit_one
    both = BIT_X | BIT_Y
    for index, flip in enumerate((0, bit_two, bit_one, both)):
        row = pl.multiple_of((place ^ flip) * PIECE, PIECE)
        keep_ref[index, 0] = acc[pl.ds(row, PIECE), :].astype(BF)
    for index, flip in enumerate((0, bit_one, bit_two, both)):
        row = pl.multiple_of((place ^ BIT_C ^ flip) * PIECE, PIECE)
        send_ref[index, 0] = acc[pl.ds(row, PIECE), :].astype(BF)


ATTN_QKV = 3 * D // 4


def cut_first(meta, t_qkv, t_out, t_ffn_in, attn_piece, in_piece, sems):
    place = meta[0]
    rows = pl.ds(pl.multiple_of(place * PIECE, PIECE), PIECE)
    other = pltpu.make_async_copy(t_ffn_in.at[rows], in_piece, sems.at[1])
    other.start()
    in_qkv = place < ATTN_QKV // PIECE

    @pl.when(in_qkv)
    def _():
        copy = pltpu.make_async_copy(t_qkv.at[rows], attn_piece, sems.at[0])
        copy.start()
        copy.wait()

    @pl.when(jnp.logical_not(in_qkv))
    def _():
        at = pl.ds(pl.multiple_of(place * PIECE - ATTN_QKV, PIECE), PIECE)
        copy = pltpu.make_async_copy(t_out.at[at], attn_piece, sems.at[0])
        copy.start()
        copy.wait()

    other.wait()


def cut_rest(meta, t_in, t_ffn_out, x_in, g_in, t_send, out_piece, x_send, g_send, sems):
    rows = pl.ds(pl.multiple_of(meta[0] * PIECE, PIECE), PIECE)
    there = 1 - meta[1]
    pairs = (
        (t_in.at[there], t_send),
        (t_ffn_out.at[rows], out_piece),
        (x_in.at[there], x_send),
        (g_in.at[there], g_send),
    )
    copies = [
        pltpu.make_async_copy(source, target, sems.at[index])
        for index, (source, target) in enumerate(pairs)
    ]
    for copy in copies:
        copy.start()
    for copy in copies:
        copy.wait()


def sum_squares(qkv, out, ffn_in, ffn_out, attn, squares):
    attn[:ATTN_QKV, :] = qkv[...]
    attn[ATTN_QKV:, :] = out[...]
    squares[...] = jnp.zeros_like(squares)
    block = D // 4
    step_rows = 64
    for index, (latent, start, count) in enumerate(
        [(attn, j * block, block) for j in range(4)] + [(ffn_in, 0, D), (ffn_out, 0, D)]
    ):

        def step(i, carry, latent=latent, start=start):
            at = pl.ds(pl.multiple_of(start + i * step_rows, step_rows), step_rows)
            values = latent[at, :].astype(F32)
            return carry + jnp.sum((values * values).reshape(step_rows // 8, 8, D), axis=0)

        total = lax.fori_loop(0, count // step_rows, step, jnp.zeros((8, D), F32))
        squares[index : index + 1, :] = colsum(total)


def binarize(meta, squares, attn, ffn_in, ffn_out, *outs):
    bins, pieces, levels = outs[:3], outs[3:6], outs[6]
    entries = jnp.where(
        lax.broadcasted_iota(jnp.int32, (8, 1), 0) < 4, float(D * D), float(D * FF)
    )
    totals = jnp.sum(squares[...], axis=1, keepdims=True)
    levels[...] = jnp.broadcast_to(jnp.sqrt(totals / entries + 1e-06), (8, D))
    step_rows = 64
    for index, latent in enumerate((attn, ffn_in, ffn_out)):

        def step(i, carry, index=index, latent=latent):
            at = pl.ds(pl.multiple_of(i * step_rows, step_rows), step_rows)
            line = i // (D // 4 // step_rows) if index == 0 else index + 3
            level = levels[pl.ds(line, 1), :]
            bins[index][at, :] = (level * jnp.tanh(latent[at, :].astype(F32) * (2.0 / level))).astype(BF)
            return carry

        lax.fori_loop(0, D // step_rows, step, 0)
        pieces[index][...] = bins[index][pl.ds(pl.multiple_of(meta[0] * PIECE, PIECE), PIECE), :]


def same_segment(meta, segments):
    own = segments[meta[1], pl.ds(meta[2], 1), :].astype(F32)
    half = SEQ // 2
    turned = jnp.concatenate([own[:, half:], own[:, :half]], axis=1)
    lanes = jnp.where(meta[1] == 0, own, turned)
    column = jnp.broadcast_to(lanes, (8, SEQ)).T[:, :1]
    return column == lanes


S_SCALE, S_GAIN, S_BIAS, S_CLIP, S_ROWS = 0, 6, 8, 10, 16


def settle(repeats, meta, levels, sums, *refs):
    grads, latents, (direct_attn, direct_ffn, sums_out) = refs[:3], refs[3:6], refs[6:]
    at = pl.ds(pl.multiple_of(meta[0] * PIECE, PIECE), PIECE)
    block = meta[0] // 2
    sums_out[...] = sums[...]
    for index in range(3):
        level = levels[pl.ds(block, 1), :] if index == 0 else levels[3 + index : 4 + index, :]
        grad = grads[index][...]
        unit = latents[index][at, :].astype(F32) * (2.0 / level)
        tangent = jnp.tanh(unit)
        slope = 1.0 - tangent * tangent
        direct = (grad * 2.0 * slope).astype(BF)
        term = colsum(grad * (tangent - unit * slope)) * (1.0 / repeats)
        if index == 0:
            direct_attn[0] = direct
            for j in range(4):
                sums_out[j : j + 1, :] = jnp.where(block == j, term, 0.0)
        else:
            direct_ffn[index - 1] = direct
            sums_out[3 + index : 4 + index, :] = term


ROWS = 256
HIDDEN_BLOCK = 256


def by_rows(count, body, rows=ROWS):
    def step(index, carry):
        body(pl.ds(pl.multiple_of(index * rows, rows), rows))
        return carry

    lax.fori_loop(0, count // rows, step, 0)


class Late:
    def __init__(self, sources, targets, sems):
        self.copies = [
            pltpu.make_async_copy(source, target, sems.at[index])
            for index, (source, target) in enumerate(zip(sources, targets))
        ]

    def start(self):
        for copy in self.copies:
            copy.start()

    def wait(self):
        for copy in self.copies:
            copy.wait()


def attend_forward(student, meta, *refs):
    clips_ref, xa, xb, segments, gain, bias = refs[:6]
    owned = 1 if student else 2
    own, refs = refs[6 : 6 + owned], refs[6 + owned :]
    parts, refs = refs[:N_PARTS], refs[N_PARTS:]
    if student:
        full_out, qkv_out, lse_out, ctx_out, pre_out, quant_out, quant_t_out, rows = refs[:8]
        refs = refs[8:]
    else:
        qkv_out, first_out, first_low_out = refs[:3]
        rows, refs = refs[3], refs[4:]
    full, rows_t, mask_bias, attn, sems = refs
    slot, slots = pl.program_id(0), full.shape[0]
    half = xb.shape[0]
    width = D // slots
    heads = width // HD

    def x_at(at, index):
        return xa[meta[1], at, :] if index == 0 else xb[at, :]

    weights = Weights(meta[0], True, own, parts, full, sems, full_out if student else None)

    @pl.when(slot == 0)
    def _():
        weights.start()
        for index in range(2):

            def quantize(at, index=index):
                to = pl.ds(pl.multiple_of(at.start + index * half, ROWS), ROWS)
                values = x_at(at, index)
                if student:
                    level = clips_ref[0]
                    values = (level * jnp.tanh(values.astype(F32) / level)).astype(BF)
                rows[to, :] = values

            by_rows(half, quantize)
        rows_t[...] = rows[...].T
        mask_bias[...] = jnp.where(same_segment(meta, segments), 0.0, NEG)
        attn[...] = jnp.zeros_like(attn)

    weights.wait(slot)
    qkv_t = nn(full[slot, : 3 * width, :], rows_t[...]).astype(BF)
    qkv_out[0] = qkv_t
    lows = []
    for head in range(heads):
        lo = head * HD
        queries = qkv_t[lo : lo + HD] * BF(0.125)
        keys = qkv_t[width + lo : width + lo + HD]
        values = qkv_t[2 * width + lo : 2 * width + lo + HD]
        scores = tn(keys, queries) + mask_bias[...]
        peak = jnp.max(scores, axis=0, keepdims=True)
        powers = jnp.exp(scores - peak)
        total = jnp.sum(powers, axis=0, keepdims=True)
        context = nn(values, powers.astype(BF)) * (1.0 / total)
        if student:
            lse_out[0, head : head + 1, :] = peak + jnp.log(total)
            ctx_out[0, lo : lo + HD, :] = context
            level = clips_ref[1]
            context = level * jnp.tanh(context / level)
        lows.append(context.astype(BF))
    attn[...] += tn(jnp.concatenate(lows, axis=0), full[slot, 3 * width :, :])

    @pl.when(slot == slots - 1)
    def _():
        for index in range(2):

            def last(at, index=index):
                to = pl.ds(pl.multiple_of(at.start + index * half, ROWS), ROWS)
                pre = x_at(at, index).astype(F32) + attn[to, :]
                first = normalize(pre)[0] * gain[0:1, :] + bias[0:1, :]
                if student:
                    pre_out[to, :] = pre
                    level = clips_ref[2]
                    quant_out[to, :] = (level * jnp.tanh(first / level)).astype(BF)
                else:
                    first_out[to, :] = first
                    first_low_out[to, :] = first.astype(BF)

            by_rows(half, last)
        if student:
            quant_t_out[...] = quant_out[...].T
        weights.end()


def hidden_forward(student, meta, clips_ref, quant, own, *refs):
    parts, refs = refs[:N_PARTS], refs[N_PARTS:]
    if student:
        full_out, act_out, act_t_out, slope_out, clip_out = refs[:5]
        refs = refs[5:]
    else:
        (act_out,), refs = refs[:1], refs[1:]
    full, sems = refs
    slot, slots = pl.program_id(0), full.shape[0]
    weights = Weights(meta[0], False, (own,), parts, full, sems, full_out if student else None)

    @pl.when(slot == 0)
    def _():
        weights.start()

    weights.wait(slot)
    for start in range(0, D, HIDDEN_BLOCK):
        columns = slice(start, start + HIDDEN_BLOCK)
        values = nn(quant[...], full[slot, :, columns])
        cdf = 0.5 * (1.0 + lax.erf(values * 0.7071067811865476))
        act = values * cdf
        if not student:
            act_out[0, :, columns] = act.astype(BF)
            continue
        level = clips_ref[3]
        ratio = act * (1.0 / level)
        tangent = jnp.tanh(ratio)
        quantized = (level * tangent).astype(BF)
        act_out[0, :, columns] = quantized
        act_t_out[0, columns, :] = quantized.T
        slope = 1.0 - tangent * tangent
        density = jnp.exp(values * values * -0.5) * 0.3989422804014327
        slope_out[0, :, columns] = (slope * (cdf + values * density)).astype(BF)
        clip_out[0, :, columns] = (tangent - ratio * slope).astype(BF)

    @pl.when(slot == slots - 1)
    def _():
        weights.end()


def output_forward(student, meta, act, gain, bias, own, *refs):
    parts, refs = refs[:N_PARTS], refs[N_PARTS:]
    if student:
        pre, t_result, grad_a, grad_b = refs[:4]
        full_out, own_out, partner_out, grad_out, low_out, sums_out = refs[4:10]
        refs = refs[10:]
    else:
        (first_in, result_out), refs = refs[:2], refs[2:]
    full, acc, sems, late_sems = refs[:4]
    held = refs[4:]
    slot, slots = pl.program_id(0), full.shape[0]
    weights = Weights(meta[0], False, (own,), parts, full, sems, full_out if student else None)

    if student:
        late = Late((pre, t_result, grad_a.at[meta[1]], grad_b), held, late_sems)
    else:
        late = Late((first_in,), held, late_sems)

    @pl.when(slot == 0)
    def _():
        weights.start()
        late.start()
        acc[...] = jnp.zeros_like(acc)

    weights.wait(slot)
    acc[...] += nn(act[0], full[slot])

    @pl.when(slot == slots - 1)
    def _():
        late.wait()
        if not student:

            def result_rows(at):
                total = held[0][at, :] + acc[at, :]
                result_out[at, :] = normalize(total)[0] * gain[1:2, :] + bias[1:2, :]

            by_rows(SEQ, result_rows)
            return
        half = held[3].shape[0]
        sums_out[...] = jnp.zeros_like(sums_out)
        for index in range(2):

            def last(at, index=index):
                to = pl.ds(pl.multiple_of(at.start + index * half, ROWS), ROWS)
                first = normalize(held[0][to, :])[0] * gain[0:1, :] + bias[0:1, :]
                normed, inv_std = normalize(first + acc[to, :])
                result = normed * gain[1:2, :] + bias[1:2, :]
                (own_out if index == 0 else partner_out)[at, :] = result.astype(BF)
                cotangent = held[2 + index][at, :].astype(F32)
                grad_result = cotangent + result - held[1][to, :]
                sums_out[S_GAIN + 1 : S_GAIN + 2, :] += colsum(grad_result * normed)
                sums_out[S_BIAS + 1 : S_BIAS + 2, :] += colsum(grad_result)
                grad_pre = norm_back(grad_result, normed, inv_std, gain[1:2, :])
                grad_out[to, :] = grad_pre
                low_out[to, :] = grad_pre.astype(BF)

            by_rows(half, last)
        weights.end()


def weight_grad(meta, left_t, right, keep_ref, send_ref, acc):
    left = left_t[0] if len(left_t.shape) == 3 else left_t[...]
    rows = right[0] if len(right.shape) == 3 else right[...]
    acc[...] = nn(left, rows)
    store_pieces(meta[0], acc, keep_ref, send_ref)


def hidden_back(meta, grad_low, full, slope, clip, sums, grad_out, sums_out):
    @pl.when(pl.program_id(0) == 0)
    def _():
        sums_out[...] = sums[...]

    grad = nt(grad_low[...], full[0])
    grad_out[0] = (grad * slope[0].astype(F32)).astype(BF)
    sums_out[S_CLIP + 3 : S_CLIP + 4, :] += colsum(grad * clip[0].astype(F32))


def first_back(
    meta, clips_ref, grad_hidden, full, pre_in, gain, bias, grad_two_in, sums, grad_out, low_out, sums_out,
    acc, pre, grad_two, sems,
):
    slot = pl.program_id(0)
    late = Late((pre_in, grad_two_in), (pre, grad_two), sems)

    @pl.when(slot == 0)
    def _():
        late.start()
        sums_out[...] = sums[...]
        acc[...] = jnp.zeros_like(acc)

    acc[...] += nt(grad_hidden[0], full[0])
    level = clips_ref[2]

    @pl.when(slot == N_SLOTS - 1)
    def _():
        late.wait()

        def last(at):
            normed, inv_std = normalize(pre[at, :])
            ratio = (normed * gain[0:1, :] + bias[0:1, :]) / level
            tangent = jnp.tanh(ratio)
            slope = 1.0 - tangent * tangent
            grad_fq = acc[at, :]
            sums_out[S_CLIP + 2 : S_CLIP + 3, :] += colsum(grad_fq * (tangent - ratio * slope))
            upstream = grad_fq * slope + grad_two[at, :]
            sums_out[S_GAIN : S_GAIN + 1, :] += colsum(upstream * normed)
            sums_out[S_BIAS : S_BIAS + 1, :] += colsum(upstream)
            grad_pre = norm_back(upstream, normed, inv_std, gain[0:1, :])
            grad_out[at, :] = grad_pre
            low_out[at, :] = grad_pre.astype(BF)

        by_rows(SEQ, last)


def attend_back(steps, first, last, meta, clips_ref, *refs):
    segments, qkv, t_qkv, lse, ctx, low, xq, full, sums = refs[:9]
    rest = list(refs[9:])
    grad_in = None if first else rest.pop(0)
    if last:
        grad_one, xa, xb = rest[:3]
        rest = rest[3:]
    keep_ref, send_ref, sums_out = rest[:3]
    rest = rest[3:]
    if last:
        own_out, partner_out = rest[:2]
        rest = rest[2:]
    else:
        grad_out = rest.pop(0)
    mask_bias, mask_scale, grad_qkv, acc, grad_acc = rest
    step = pl.program_id(0)

    @pl.when(step == 0)
    def _():
        same = same_segment(meta, segments)
        mask_bias[...] = jnp.where(same, 0.0, NEG)
        mask_scale[...] = jnp.where(same, 1.0 / SEQ, 0.0)
        sums_out[...] = sums[...]
        grad_acc[...] = jnp.zeros_like(grad_acc) if first else grad_in[...]

    width = ctx.shape[1]
    heads = width // HD
    level = clips_ref[1]
    ratio = ctx[0] / level
    tangent = jnp.tanh(ratio)
    slope = 1.0 - tangent * tangent
    grad_cq = nt(low[...], full[0, 3 * width :, :]).T
    clip_sum = jnp.sum(grad_cq * (tangent - ratio * slope), axis=0, keepdims=True)
    sums_out[S_CLIP + 1 : S_CLIP + 2, :SEQ] += clip_sum
    grad_ctx_t = (grad_cq * slope).astype(BF)
    grad_ctx = grad_ctx_t.T
    acc[3 * width :, :] = nn((level * tangent).astype(BF), low[...])
    for head in range(heads):
        lo = head * HD
        queries = qkv[0, lo : lo + HD, :] * BF(0.125)
        keys = qkv[0, width + lo : width + lo + HD, :]
        values = qkv[0, 2 * width + lo : 2 * width + lo + HD, :]
        t_queries = t_qkv[0, lo : lo + HD, :] * BF(0.125)
        t_keys = t_qkv[0, width + lo : width + lo + HD, :]
        scores = tn(keys, queries)
        probs = jnp.exp(scores + mask_bias[...] - lse[0, head : head + 1, :])
        grad_probs = tn(values, grad_ctx_t[lo : lo + HD, :])
        grad_values = nn(probs.astype(BF), grad_ctx[:, lo : lo + HD])
        row_sum = jnp.sum(probs * grad_probs, axis=0, keepdims=True)
        gap = scores - tn(t_keys, t_queries)
        grad_scores = (probs * (grad_probs - row_sum) + gap * mask_scale[...]).astype(BF)
        grad_keys = nn(grad_scores, queries.T)
        grad_qkv[lo : lo + HD, :] = (nn(keys, grad_scores) * 0.125).astype(BF)
        grad_qkv[width + lo : width + lo + HD, :] = grad_keys.T.astype(BF)
        grad_qkv[2 * width + lo : 2 * width + lo + HD, :] = grad_values.T.astype(BF)
    acc[: 3 * width, :] = nn(grad_qkv[...], xq[...])
    store_pieces(meta[0], acc, keep_ref, send_ref)
    grad_acc[...] += tn(grad_qkv[...], full[0, : 3 * width, :])

    @pl.when(step == steps - 1)
    def _():
        if not last:
            grad_out[...] = grad_acc[...]
            return
        half = xb.shape[0]
        level = clips_ref[0]
        for index in range(2):

            def finish_rows(at, index=index):
                to = pl.ds(pl.multiple_of(at.start + index * half, ROWS), ROWS)
                values = xa[meta[1], at, :] if index == 0 else xb[at, :]
                ratio = values.astype(F32) / level
                tangent = jnp.tanh(ratio)
                slope = 1.0 - tangent * tangent
                grad = grad_acc[to, :]
                sums_out[S_CLIP : S_CLIP + 1, :] += colsum(grad * (tangent - ratio * slope))
                total = grad * slope + grad_one[to, :]
                if index == 0:
                    own_out[at, :] = total
                else:
                    partner_out[at, :] = total.astype(BF)

            by_rows(half, finish_rows)


def finish(
    meta, attn_own, attn_other, own, other, sums, levels, attn_latent, in_latent, out_latent,
    qkv_out, attn_out, in_out, out_out, gain_out, bias_out, clip_out, scales, blocks, sems,
):
    place = meta[0]
    core = place & BIT_C
    bit_one = BIT_X + core * (BIT_Y - BIT_X)
    bit_two = BIT_X + BIT_Y - bit_one
    both = BIT_X | BIT_Y
    for j in range(6):
        total = jnp.sum(sums[j : j + 1, :], axis=1, keepdims=True)
        entries = D * D if j < 4 else D * FF
        scales[j : j + 1, :] = total / (levels[j : j + 1, :] * entries)
    gain_out[...] = sums[S_GAIN : S_GAIN + 2, :]
    bias_out[...] = sums[S_BIAS : S_BIAS + 2, :]
    clip_out[...] = jnp.broadcast_to(
        jnp.sum(sums[S_CLIP : S_CLIP + 4, :], axis=1, keepdims=True), clip_out.shape
    )
    flips = (0, bit_one, bit_two, both)
    flips += (BIT_C, BIT_C | bit_two, BIT_C | bit_one, BIT_C | both)

    def attn_copies(index):
        piece = place ^ flips[index]
        row = pl.multiple_of(piece * PIECE, PIECE)
        late = pl.multiple_of(jnp.maximum(piece * PIECE - ATTN_QKV, 0), PIECE)
        early = pl.multiple_of(jnp.minimum(row, ATTN_QKV - PIECE), PIECE)
        block = blocks.at[2, pl.ds(row, PIECE)]
        return (
            piece < ATTN_QKV // PIECE,
            pltpu.make_async_copy(block, qkv_out.at[pl.ds(early, PIECE)], sems.at[2, index]),
            pltpu.make_async_copy(block, attn_out.at[pl.ds(late, PIECE)], sems.at[2, index]),
        )

    copies = []
    for index, flip in enumerate(flips):
        piece = place ^ flip
        at = pl.ds(pl.multiple_of(piece * PIECE, PIECE), PIECE)
        unit = index % 4
        for kind, (latent, out) in enumerate(((in_latent, in_out), (out_latent, out_out))):
            source = own if index < 4 else other
            blocks[kind, at, :] = (
                source[unit, kind].astype(F32)
                + scales[4 + kind : 5 + kind, :] * latent[at, :].astype(F32)
            )
            copy = pltpu.make_async_copy(blocks.at[kind, at], out.at[at], sems.at[kind, index])
            copy.start()
            copies.append(copy)
        source = attn_own if index < 4 else attn_other
        blocks[2, at, :] = (
            source[unit, 0].astype(F32)
            + scales[pl.ds(piece // 2, 1), :] * attn_latent[at, :].astype(F32)
        )
        in_qkv, to_qkv, to_out = attn_copies(index)

        @pl.when(in_qkv)
        def _(copy=to_qkv):
            copy.start()

        @pl.when(jnp.logical_not(in_qkv))
        def _(copy=to_out):
            copy.start()

    for copy in copies:
        copy.wait()
    for index in range(8):
        in_qkv, to_qkv, to_out = attn_copies(index)

        @pl.when(in_qkv)
        def _(copy=to_qkv):
            copy.wait()

        @pl.when(jnp.logical_not(in_qkv))
        def _(copy=to_out):
            copy.wait()


VM = pl.BlockSpec(memory_space=pltpu.VMEM)
SM = pl.BlockSpec(memory_space=pltpu.SMEM)
HBM = pl.BlockSpec(memory_space=pltpu.HBM)
ANY = pl.BlockSpec(memory_space=pl.ANY)
DMA_SEMS = pltpu.SemaphoreType.DMA((N_COPIES + 1,))


def shape(dims, dtype):
    return jax.ShapeDtypeStruct(dims, dtype)


def cost(args, outs, flops):
    total = sum(a.size * a.dtype.itemsize for a in args) + sum(
        o.size * o.dtype.itemsize for o in outs
    )
    return pl.CostEstimate(flops=flops, bytes_accessed=total, transcendentals=0)


def call(name, body, args, specs, outs, scratch, flops, limit=VMEM_WIDE, out_specs=None):
    return pl.pallas_call(
        body,
        name=name,
        in_specs=specs,
        out_specs=out_specs or [VM] * len(outs),
        out_shape=outs,
        scratch_shapes=scratch,
        compiler_params=pltpu.CompilerParams(vmem_limit_bytes=limit),
        cost_estimate=cost(args, outs, flops),
    )(*args)


def every(array):
    dims = array.shape
    return pl.BlockSpec(dims, lambda i, meta: (0,) * len(dims))


def slot_of(array, first=0, rows=None):
    dims = array.shape
    block = (1, rows or dims[1]) + dims[2:]
    return pl.BlockSpec(block, lambda i, meta: ((first + i) % N_SLOTS,) + (0,) * (len(dims) - 1))


def call_by_slots(name, body, meta, args, specs, outs, out_specs, scratch, flops, steps=N_SLOTS, limit=VMEM_WIDE):
    return pl.pallas_call(
        body,
        name=name,
        grid_spec=pltpu.PrefetchScalarGridSpec(
            num_scalar_prefetch=1,
            grid=(steps,),
            in_specs=specs,
            out_specs=out_specs,
            scratch_shapes=scratch,
        ),
        out_shape=outs,
        compiler_params=pltpu.CompilerParams(vmem_limit_bytes=limit),
        cost_estimate=cost(args, outs, flops),
    )(meta, *args)


def swap(array, axis, size, bit):
    return lax.ppermute(array, axis, [(i, i ^ bit) for i in range(size)])


def swap_by_core(array, dp, bit_zero, bit_one):
    pairs = [(i, i ^ (bit_one if i & BIT_C else bit_zero)) for i in range(dp)]
    return lax.ppermute(array, "dp", pairs)


def near(array, dp):
    return swap_by_core(array, dp, BIT_X, BIT_Y)


def far(array, dp):
    return swap_by_core(array, dp, BIT_Y, BIT_X)


def cross(array, dp):
    return swap(array, "dp", dp, BIT_C)


def line(array, dp, n, bit_zero, bit_one):
    pairs = []
    for i in range(dp):
        for j in range(n):
            pairs.append((i * n + j, i * n + (j ^ (bit_one if i & BIT_C else bit_zero))))
    return lax.ppermute(array, ("dp", "head"), pairs)


def line_one(array, dp, n):
    return line(array, dp, n, 1, 3)


def line_two(array, dp, n):
    return line(array, dp, n, 2, 1)


class Line:
    def __init__(self, piece, dp, n):
        self.piece, self.dp, self.n = piece[None], dp, n
        self.flying = None
        self.stage = 0

    def land(self):
        stage, got = self.stage, self.flying
        self.stage += 1
        if stage == 0:
            self.flying = (line_one(self.piece, self.dp, self.n),)
        elif stage == 1:
            self.one = got[0]
            self.both = jnp.concatenate([self.piece, got[0]])
            self.flying = (line_two(self.both, self.dp, self.n),)
        else:
            self.flying = None
            remote = [self.one[0], got[0][0], got[0][1]]
            count = self.piece.shape[1]
            self.remote = [
                jnp.concatenate([r[index] for r in remote], axis=0) for index in range(count)
            ]


class Plane:
    def __init__(self, remote, dp):
        self.remote, self.dp = remote, dp
        self.flying = None
        self.stage = 0

    def land(self):
        dp, stage, got = self.dp, self.stage, self.flying
        self.stage += 1
        if stage == 0:
            self.flying = (near(self.remote, dp),)
        elif stage == 1:
            self.pair = jnp.concatenate([self.remote, got[0]])
            self.flying = (far(self.pair, dp),)
            self.crossed = cross(self.pair, dp)
        elif stage == 2:
            self.pair_far = got[0]
            self.flying = (cross(self.pair_far, dp),)
        else:
            self.parts = (self.pair, self.pair_far, self.crossed, got[0])
            self.flying = None


class Reduce:
    def __init__(self, keep, send, dp, n, mode, sent=None):
        self.keep, self.send, self.dp, self.n, self.mode = keep, send, dp, n, mode
        self.sent = sent
        self.flying = None
        self.stage = 0

    def land(self):
        dp, n, stage = self.dp, self.n, self.stage
        self.stage += 1
        got = self.flying
        if stage == 0:
            self.mark = self.send
            self.flying = (cross(self.send, dp),)
        elif stage == 1:
            self.total = self.keep.astype(F32) + got[0].astype(F32)
            self.mark = self.total[2:].astype(BF)
            self.flying = (near(self.mark, dp),)
        elif stage == 2:
            self.total = self.total[:2] + got[0].astype(F32)
            self.mark = self.total[1].astype(BF)
            self.flying = (far(self.mark, dp),)
        elif stage == 3:
            self.total = self.total[0] + got[0].astype(F32)
            if self.mode == "whole":
                self.mark = self.total[2:].astype(BF)
                self.flying = (line_two(self.mark, dp, n),)
            elif self.mode == "sent":
                self.mark = self.total.astype(BF)
                self.flying = (swap(self.mark, "head", n, 1),)
            else:
                self.mark = (self.total[0] + self.sent.result[1].astype(F32)).astype(BF)
                self.flying = (swap(self.mark, "head", n, 3),)
        elif stage == 4:
            if self.mode == "sent":
                self.flying, self.result = None, got[0]
            elif self.mode == "kept":
                self.finish(self.total[1] + self.sent.result[0].astype(F32) + got[0].astype(F32))
            else:
                self.total = self.total[:2] + got[0].astype(F32)
                self.mark = self.total[1].astype(BF)
                self.flying = (line_one(self.mark, dp, n),)
        elif stage == 5:
            self.finish(self.total[0] + got[0].astype(F32))

    def finish(self, mine):
        bit = GROUP
        while bit < self.dp:
            mine = mine + swap(mine.astype(BF), "dp", self.dp, bit).astype(F32)
            bit *= 2
        self.result, self.flying = mine, None


class Share:
    def __init__(self, piece, dp):
        self.piece, self.dp = piece[None], dp
        self.flying = None
        self.stage = 0

    def land(self):
        dp, stage = self.dp, self.stage
        self.stage += 1
        got = self.flying
        if stage == 0:
            self.flying = (near(self.piece, dp),)
        elif stage == 1:
            self.pair = jnp.concatenate([self.piece, got[0]])
            self.flying = (far(self.pair, dp),)
        elif stage == 2:
            self.quad = jnp.concatenate([self.pair, got[0]])
            self.flying = (cross(self.quad, dp),)
        elif stage == 3:
            self.result = (self.quad, got[0])
            self.flying = None


class Sum:
    def __init__(self, values, steps):
        self.values = values
        self.steps = steps
        self.flying = None
        self.stage = 0

    def land(self):
        got, values = self.flying, self.values
        if got is not None:
            self.values = values + got[0] if len(got) == 1 else (values + got[0]) + (got[1] + got[2])
        if self.stage < len(self.steps):
            axis, size, bits = self.steps[self.stage]
            flips = bits if len(bits) == 1 else (bits[0], bits[1], bits[0] | bits[1])
            self.flying = tuple(swap(self.values, axis, size, flip) for flip in flips)
        else:
            self.flying = None
            self.result = self.values
        self.stage += 1


def steps_over(axis, size, bit=1):
    steps = []
    while bit < size:
        bits = (bit, 2 * bit) if 2 * bit < size else (bit,)
        steps.append((axis, size, bits))
        bit <<= len(bits)
    return steps


def beside(flights, outs):
    flights = [f for f in flights if f.flying is not None]
    tied, outs = lax.optimization_barrier((tuple(f.flying for f in flights), tuple(outs)))
    for flight, flying in zip(flights, tied):
        flight.flying = flying
    return outs


class Once:
    def __init__(self, flying):
        self.flying = (flying,)

    def land(self):
        self.result = self.flying[0]
        self.flying = None


def then(first, *later):
    for flight in later:
        flight.flying, first.mark = lax.optimization_barrier((flight.flying, first.mark))


def land(*flights):
    for flight in flights:
        flight.land()


def on_device(
    dp,
    n,
    hidden_in,
    teacher_in,
    out_grad,
    segment_ids,
    qkv_latent,
    out_latent,
    ffn_in_latent,
    ffn_out_latent,
    norm_gain,
    norm_bias,
    clips,
    teacher_qkv,
    teacher_out,
    teacher_ffn_in,
    teacher_ffn_out,
    teacher_gain,
    teacher_bias,
):
    h = lax.axis_index("head")
    place = lax.axis_index("dp") % GROUP
    parity = h % MICRO
    half = hidden_in.shape[1]
    width = qkv_latent.shape[-1]
    meta = jnp.stack([place, parity, h // MICRO]).astype(jnp.int32)

    def exchange(array):
        return Once(swap(array, "head", n, 1))

    def tie(*values):
        return lax.optimization_barrier(values)

    def lines(array):
        return jnp.swapaxes(array, 1, 2).reshape(3 * width, D)

    big = pltpu.VMEM((n, D, D), BF)
    tall = pltpu.VMEM((SEQ, D), F32)
    mm = 2 * SEQ * D * D
    square, band, sheet = shape((D, D), BF), shape((PIECE, D), BF), shape((half, D), BF)
    weights = [ANY] * (1 + N_PARTS)

    t_qkv_rows, qkv_rows = lines(teacher_qkv), lines(qkv_latent)
    t_piece_attn, t_piece_in = call(
        "cut_first",
        cut_first,
        (meta, t_qkv_rows, teacher_out, teacher_ffn_in),
        [SM] + [HBM] * 3,
        [band] * 2,
        [pltpu.SemaphoreType.DMA((2,))],
        mm // 8,
    )
    z0, z1 = Line(t_piece_attn[None], dp, n), Line(t_piece_in[None], dp, n)
    land(z0, z1)
    t_send, t_piece_out, x_send, g_send = call(
        "cut_rest",
        cut_rest,
        (meta, teacher_in, teacher_ffn_out, hidden_in, out_grad),
        [SM] + [HBM] * 4,
        [sheet, band, sheet, sheet],
        [pltpu.SemaphoreType.DMA((4,))],
        mm // 8,
    )
    land(z0)
    t_send, z0.both = tie(t_send, z0.both)
    t_ex = exchange(t_send)
    attn_latent, squares = call(
        "sum_squares",
        sum_squares,
        (qkv_rows, out_latent, ffn_in_latent, ffn_out_latent),
        [VM] * 4,
        [square, shape((8, D), F32)],
        [],
        mm,
    )
    latents = [attn_latent, ffn_in_latent, ffn_out_latent]
    total = Sum(squares, steps_over("head", n))
    land(total)
    total.values, z1.flying = tie(total.values, z1.flying)
    land(z1)
    land(total)
    results = beside(
        (z0,),
        call(
            "binarize",
            binarize,
            (meta, total.result) + tuple(latents),
            [SM] + [VM] * 4,
            [square] * 3 + [band] * 3 + [shape((8, D), F32)],
            [],
            mm,
        ),
    )
    bins, s_pieces, levels = results[:3], results[3:6], results[6]
    land(z0)
    p0 = Plane(z0.remote[0], dp)
    land(p0)
    piece, p0.remote = tie(s_pieces[0], p0.remote)
    z2 = Line(piece[None], dp, n)
    land(z2)
    land(z1)
    p1 = Plane(z1.remote[0], dp)
    land(p0)
    p1.remote, p0.pair = tie(p1.remote, p0.pair)
    land(p1)
    land(z2)
    t_piece_out, z2.both = tie(t_piece_out, z2.both)
    z3 = Line(t_piece_out[None], dp, n)
    land(z3)
    land(t_ex)
    land(p0)
    p1.flying, p0.pair_far = tie(p1.flying, p0.pair_far)
    land(p1)
    z2.flying, p1.pair = tie(z2.flying, p1.pair)
    land(z2)
    p2 = Plane(z2.remote[0], dp)
    land(p2)
    land(z3)
    pieces_in, pieces_out, p2.remote = tie(s_pieces[1], s_pieces[2], p2.remote)
    z45 = Line(jnp.stack([pieces_in, pieces_out]), dp, n)
    land(z45)
    x_send, p1.pair = tie(x_send, p1.pair)
    x_ex = exchange(x_send)
    land(p0)

    def slots_shape(rows, columns, dtype=BF):
        return shape((n, rows, columns), dtype)

    def run(name, body, args, specs, outs, out_specs, scratch, flops, limit=VMEM_WIDE):
        specs = [spec if spec is not None else every(arg) for spec, arg in zip(specs, args)]
        out_specs = [spec if spec is not None else every(out) for spec, out in zip(out_specs, outs)]
        return call_by_slots(name, body, meta, args, specs, outs, out_specs, scratch, flops, limit=limit)

    attn_scratch = [big, pltpu.VMEM((D, SEQ), BF), pltpu.VMEM((SEQ, SEQ), F32), tall, DMA_SEMS]
    qkv_shape = slots_shape(3 * width, SEQ)
    tall_shape, low_shape = shape((SEQ, D), F32), shape((SEQ, D), BF)
    t_qkv, t_first, t_first_low = beside(
        (p1, p2, z3, z45, x_ex),
        run(
            "teacher_attend",
            functools.partial(attend_forward, False),
            (clips, teacher_in, t_ex.result, segment_ids, teacher_gain, teacher_bias, t_qkv_rows, teacher_out)
            + p0.parts,
            [SM] + [None] * 5 + [HBM] + weights,
            [qkv_shape, tall_shape, low_shape],
            [slot_of(qkv_shape)] + [None] * 2,
            [pltpu.VMEM((SEQ, D), BF)] + attn_scratch,
            8 * mm,
        ),
    )
    land(p1, p2, z3, z45, x_ex)
    p3 = Plane(z3.remote[0], dp)
    land(p3, p1)
    act_shape = slots_shape(SEQ, D)
    (t_act,) = beside(
        (p2, p3, z45),
        run(
            "teacher_hidden",
            functools.partial(hidden_forward, False),
            (clips, t_first_low, teacher_ffn_in) + p1.parts,
            [SM, None] + weights,
            [act_shape],
            [slot_of(act_shape)],
            [big, DMA_SEMS],
            6 * mm,
        ),
    )
    land(p2, p3, z45)
    p4, p5 = Plane(z45.remote[0], dp), Plane(z45.remote[1], dp)
    land(p4, p2)
    big_shape, quant_t_shape = shape((n, D, D), BF), shape((D, SEQ), BF)
    lse_shape, ctx_shape = slots_shape(8, SEQ, F32), slots_shape(width, SEQ, F32)
    full_attn, qkv, lse, ctx, pre_one, quant, quant_t, xq = beside(
        (p3, p4),
        run(
            "student_attend",
            functools.partial(attend_forward, True),
            (clips, hidden_in, x_ex.result, segment_ids, norm_gain, norm_bias, bins[0]) + p2.parts,
            [SM] + [None] * 5 + weights,
            [big_shape, qkv_shape, lse_shape, ctx_shape, tall_shape, low_shape, quant_t_shape, low_shape],
            [HBM] + [slot_of(a) for a in (qkv_shape, lse_shape, ctx_shape)] + [None] * 4,
            attn_scratch,
            8 * mm,
        ),
    )
    land(p3, p4)
    p5.remote, quant = tie(p5.remote, quant)
    land(p5, p3)
    (t_result,) = beside(
        (p4, p5),
        run(
            "teacher_output",
            functools.partial(output_forward, False),
            (t_act, teacher_gain, teacher_bias, teacher_ffn_out) + p3.parts + (t_first,),
            [slot_of(t_act), None, None] + weights + [ANY],
            [tall_shape],
            [None],
            [big, tall, DMA_SEMS, pltpu.SemaphoreType.DMA((1,)), tall],
            4 * mm,
        ),
    )
    land(p4, p5, p4)
    g_send, t_result = tie(g_send, t_result)
    g_ex = exchange(g_send)
    act_t_shape = slots_shape(D, SEQ)
    full_in, act, act_t, slope, clip_term = beside(
        (p5, g_ex),
        run(
            "student_hidden",
            functools.partial(hidden_forward, True),
            (clips, quant, bins[1]) + p4.parts,
            [SM, None] + weights,
            [big_shape, act_shape, act_t_shape, act_shape, act_shape],
            [HBM] + [slot_of(a) for a in (act_shape, act_t_shape, act_shape, act_shape)],
            [big, DMA_SEMS],
            8 * mm,
        ),
    )
    land(p5, p5, g_ex)
    sums_shape = shape((S_ROWS, D), F32)
    full_out, out_own, out_far, grad_two, low_two, sums = run(
        "student_output",
        functools.partial(output_forward, True),
        (act, norm_gain, norm_bias, bins[2]) + p5.parts + (pre_one, t_result, out_grad, g_ex.result),
        [slot_of(act), None, None] + weights + [ANY] * 4,
        [big_shape, sheet, sheet, tall_shape, low_shape, sums_shape],
        [HBM] + [None] * 5,
        [big, tall, DMA_SEMS, pltpu.SemaphoreType.DMA((4,)), tall, tall] + [pltpu.VMEM((half, D), BF)] * 2,
        4 * mm,
    )

    def grad_call(name, left_t, right):
        pieces_shape = shape((GROUP // 2, n, PIECE, D), BF)
        block = (GROUP // 2, 1, PIECE, D)

        def there(i, meta):
            return (0, jnp.where(i == 0, 0, crosswise(meta[0] & BIT_C, i)), 0, 0)

        return run(
            name,
            weight_grad,
            (left_t, right),
            [slot_of(a) if len(a.shape) == 3 else None for a in (left_t, right)],
            [pieces_shape] * 2,
            [pl.BlockSpec(block, lambda i, meta: (0, i, 0, 0)), pl.BlockSpec(block, there)],
            [pltpu.VMEM((D, D), F32)],
            4 * mm,
            limit=VMEM_SMALL,
        )

    out_ex = exchange(out_far)
    keep, send = grad_call("ffn_out_weight", act_t, low_two)
    r_out = Reduce(keep, send, dp, n, "whole")
    land(r_out)
    grad_hidden, sums = beside(
        (r_out,),
        run(
            "hidden_back",
            hidden_back,
            (low_two, full_out, slope, clip_term, sums),
            [None] + [slot_of(a) for a in (full_out, slope, clip_term)] + [None],
            [act_shape, sums_shape],
            [slot_of(act_shape), None],
            [],
            5 * mm,
            limit=VMEM_SMALL,
        ),
    )
    land(r_out)
    grad_hidden, r_out.mark = tie(grad_hidden, r_out.mark)
    keep, send = grad_call("ffn_in_weight", quant_t, grad_hidden)
    r_in = Reduce(keep, send, dp, n, "whole")
    land(r_in)
    grad_hidden, r_in.mark = tie(grad_hidden, r_in.mark)
    grad_one, low_one, sums = beside(
        (r_in, r_out, out_ex),
        run(
            "first_back",
            first_back,
            (clips, grad_hidden, full_in, pre_one, norm_gain, norm_bias, grad_two, sums),
            [SM, slot_of(grad_hidden), slot_of(full_in), ANY, None, None, ANY, None],
            [tall_shape, low_shape, sums_shape],
            [None] * 3,
            [tall] * 3 + [pltpu.SemaphoreType.DMA((2,))],
            4 * mm,
            limit=VMEM_SMALL,
        ),
    )

    def attend_back_slots(first_slot, steps, grad_xq, sums):
        first, last = first_slot == 1, first_slot == 3
        args = (clips, segment_ids, qkv, t_qkv, lse, ctx, low_one, xq, full_attn, sums)
        one = [slot_of(a, first_slot) for a in (qkv, t_qkv, lse, ctx)]
        one[1] = slot_of(t_qkv, first_slot, 2 * width)
        specs = [SM, every(segment_ids)] + one
        specs += [every(low_one), every(xq), slot_of(full_attn, first_slot), every(sums)]
        pieces_shape = shape((GROUP // 2, steps, PIECE, D), BF)
        block = pl.BlockSpec((GROUP // 2, 1, PIECE, D), lambda i, meta: (0, i, 0, 0))
        outs = [pieces_shape] * 2 + [sums_shape]
        more = () if first else (grad_xq,)
        if last:
            more += (grad_one, hidden_in, x_ex.result)
            outs += [shape((half, D), F32), sheet]
        else:
            outs += [tall_shape]
        return call_by_slots(
            "attend_back",
            functools.partial(attend_back, steps, first, last),
            meta,
            args + more,
            specs + [every(a) for a in more],
            outs,
            [block, block] + [every(o) for o in outs[2:]],
            [
                pltpu.VMEM((SEQ, SEQ), F32),
                pltpu.VMEM((SEQ, SEQ), F32),
                pltpu.VMEM((3 * width, SEQ), BF),
                pltpu.VMEM((D, D), F32),
                tall,
            ],
            5 * steps * mm,
            steps=steps,
            limit=VMEM_MIDDLE,
        )

    land(r_out, r_in, out_ex)
    low_one, r_out.mark, r_in.mark = tie(low_one, r_out.mark, r_in.mark)
    keep, send, sums, grad_xq = beside((r_out,), attend_back_slots(1, 2, None, sums))
    r_sent = Reduce(keep, send, dp, n, "sent")
    land(r_sent)
    land(r_out)
    then(r_out, r_in)
    land(r_in)
    then(r_in, r_sent)
    land(r_sent)
    grad_xq, r_sent.mark, r_out.mark = tie(grad_xq, r_sent.mark, r_out.mark)
    keep, send, sums, in_grad_own, in_grad_far = beside(
        (r_sent, r_in, r_out), attend_back_slots(3, 2, grad_xq, sums)
    )
    def both(own, far):
        first_row = jnp.where(parity == 0, own, far)
        second_row = jnp.where(parity == 0, far, own)
        return jnp.stack([first_row, second_row])

    r_kept = Reduce(keep, send, dp, n, "kept", r_sent)
    land(r_kept)
    land(r_sent)
    then(r_sent, r_kept)
    land(r_kept)
    then(r_kept, r_in, r_out)
    land(r_in)
    then(r_in, r_out)
    land(r_out)
    then(r_out, r_sent)
    land(r_sent)
    repeats = dp // GROUP

    then(r_sent, r_kept)
    land(r_kept)
    then(r_kept, r_sent, r_in)
    land(r_in)
    land(r_sent)
    land(r_kept)
    out_all = both(out_own, out_ex.result)
    (out_all,) = beside((r_kept, r_in, r_out), (out_all,))
    land(r_in, r_out, r_kept)
    in_grad_far, kept = tie(in_grad_far, r_kept.result)
    r_kept.result = kept
    in_ex = exchange(in_grad_far)
    direct_attn, direct_ffn, sums = call(
        "settle",
        functools.partial(settle, repeats),
        (meta, levels, sums, r_kept.result, r_in.result, r_out.result) + tuple(latents),
        [SM] + [VM] * 8,
        [shape((1, PIECE, D), BF), shape((2, PIECE, D), BF), sums_shape],
        [],
        mm // 4,
        limit=VMEM_SMALL,
    )
    s_attn, s_ffn = Share(direct_attn, dp), Share(direct_ffn, dp)
    total = Sum(sums, [("dp", dp, (BIT_C,))] + steps_over("dp", dp, BIT_X) + steps_over("head", n))
    land(total, s_attn, s_ffn)
    land(total)
    s_attn.flying, total.values = tie(s_attn.flying, total.values)
    land(s_attn)
    s_ffn.flying, s_attn.pair = tie(s_ffn.flying, s_attn.pair)
    land(s_ffn)
    total.flying, s_ffn.pair = tie(total.flying, s_ffn.pair)
    land(total)
    in_ex.flying, total.values = tie(in_ex.flying, total.values)
    land(in_ex)
    in_grad_all = both(in_grad_own, in_ex.result.astype(F32))
    (in_grad_all,) = beside((s_attn, total, s_ffn), (in_grad_all,))
    land(s_attn)
    while total.flying is not None:
        land(total)
    land(s_ffn, s_attn, s_ffn)
    sums = total.result
    flat = shape((D, D), F32)
    qkv_grad, attn_out_grad, in_grad, out_grad_w, gain_grad, bias_grad, clip_sums = call(
        "finish",
        finish,
        (meta,) + s_attn.result + s_ffn.result + (sums, levels) + tuple(latents),
        [SM] + [VM] * 9,
        [shape((ATTN_QKV, D), F32), shape((width, D), F32), flat, flat]
        + [shape((2, D), F32)] * 2
        + [shape((4, 128), F32)],
        [pltpu.VMEM((8, D), F32), pltpu.VMEM((3, D, D), F32), pltpu.SemaphoreType.DMA((3, 8))],
        mm // 2,
        limit=VMEM_SMALL,
        out_specs=[HBM] * 4 + [VM] * 3,
    )
    qkv_grad = jnp.swapaxes(qkv_grad.reshape(3, width, D), 1, 2)
    clip_grad = clip_sums[:, 0]

    return (
        out_all,
        in_grad_all,
        qkv_grad,
        attn_out_grad,
        in_grad,
        out_grad_w,
        gain_grad,
        bias_grad,
        clip_grad,
    )


def solution(mesh):
    placed = (
        P(None, ("dp", "head"), None),
        P(None, ("dp", "head"), None),
        P(None, ("dp", "head"), None),
        P(None, "dp", None),
        P(None, None, "head"),
        P("head", None),
        P(None, "head"),
        P("head", None),
        P(),
        P(),
        P(),
        P(None, None, "head"),
        P("head", None),
        P(None, "head"),
        P("head", None),
        P(),
        P(),
    )
    return jax.shard_map(
        functools.partial(on_device, mesh.shape["dp"], mesh.shape["head"]),
        mesh=mesh,
        in_specs=placed,
        out_specs=(
            P(None, ("dp", "head"), None),
            P(None, ("dp", "head"), None),
            P(None, None, "head"),
            P("head", None),
            P(None, "head"),
            P("head", None),
            P(),
            P(),
            P(),
        ),
        check_vma=False,
    )
```
